128 devices in a mesh: seq: 16 (over y, x_hi, core), tp: 8 (over x_lo, z).
Axes of the slice: x: 4 (x_hi: 2, x_lo: 2; x = x_hi * 2 + x_lo), y: 4, z: 4, core: 2. Of those that a mesh axis runs over, the one named last changes fastest.
Arguments:
- hidden_in: bfloat16 [6144, 8192], P('seq', 'tp'), may hold values from -6 to 6
- w_query: bfloat16 [8192, 8192], P(None, 'tp'), may hold values from -0.0625 to 0.0625
- w_key: bfloat16 [8192, 1024], P(None, 'tp'), may hold values from -0.0625 to 0.0625
- w_value: bfloat16 [8192, 1024], P(None, 'tp'), may hold values from -0.0625 to 0.0625
- q_bias: float32 [8192], P('tp'), may hold values from -10 to 10
- k_bias: float32 [1024], P('tp'), may hold values from -10 to 10
- v_bias: float32 [1024], P('tp'), may hold values from -3 to 3
Outputs:
- attended: bfloat16 [6144, 8192], P('seq', 'tp')
The draws below stay inside these ranges and needn't reach their ends.
All inputs are finite; a program needn't handle non-finite values.
Results may differ from the reference program's by a relative error of at most 0.0065.
The reference program's roundings to bfloat16 on the way (of `query`, `keys`, `values` and `weights`) count: a program that leaves them out, or rounds other values in their place, can miss the bound.
Values may be sent and summed in bfloat16 or wider, within the bound.
No kernel may reach another device: no remote copies, remote signals or barrier semaphores. Data moves between devices by JAX's collectives and lax.ppermute only.
A program may use at most 128 MiB of HBM per device.

```python
import jax
import jax.numpy as jnp
from jax import lax

D = 8192
HQ = 64
KVH = 8
HEAD = 128
TOKENS = 6144


def draw_k_bias(key, part):
    key = jax.random.fold_in(key, 2)
    result = jnp.clip(0.7 * jax.random.normal(key, (KVH, HEAD), jnp.float32), -3.0, 3.0)
    return result.reshape(KVH * HEAD)


def draw_q_bias(key, part):
    key = jax.random.fold_in(key, 1)
    result = jnp.clip(0.7 * jax.random.normal(key, (HQ, HEAD), jnp.float32), -3.0, 3.0)
    return result.reshape(HQ * HEAD)


def levels(own_key, shape, pieces, least, high):
    level, own = 1.0, jax.random.fold_in(own_key, 6)
    for axis_at, shards_of in pieces:
        heights = jnp.exp(jax.random.uniform(jax.random.fold_in(own, axis_at), (shards_of,), jnp.float32, least / len(pieces), high / len(pieces)))
        level = level * jnp.repeat(heights, shape[axis_at] // shards_of).reshape([-1 if axis == axis_at else 1 for axis in range(len(shape))])
    return level


def gaussian(own_key, extent, scale, limit, cuts=(), kind=jnp.bfloat16):
    drawn = scale * jax.random.normal(own_key, extent, jnp.float32)
    if cuts:
        drawn = drawn * levels(own_key, extent, cuts, -0.22, 0.18)
    return jnp.clip(drawn, -limit, limit).astype(kind)


def setup_inputs(seed: int = 0) -> dict:
    streams_of = jax.random.split(jax.random.key(seed), 8)
    return {
        "hidden_in": gaussian(streams_of[0], (TOKENS, D), 1.0, 6.0, ((0, 16), (1, 8))),
        "w_query": gaussian(streams_of[1], (D, HQ * HEAD), D ** -0.5, 0.0625, ((1, 8),)),
        "w_key": gaussian(streams_of[2], (D, KVH * HEAD), D ** -0.5, 0.0625, ((1, 8),)),
        "w_value": gaussian(streams_of[3], (D, KVH * HEAD), D ** -0.5, 0.0625, ((1, 8),)),
        "q_bias": draw_q_bias(jax.random.fold_in(streams_of[7], 71), 0),
        "k_bias": draw_k_bias(jax.random.fold_in(streams_of[7], 71), 0),
        "v_bias": gaussian(streams_of[6], (KVH * HEAD,), 0.5, 3.0, ((0, 8),), jnp.float32),
    }


rope_base = 1000000.0


def angles(positions, width):
    half = width // 2
    freq = rope_base ** (-2.0 * jnp.arange(half, dtype=jnp.float32) / width)
    phase = positions.astype(jnp.float32)[:, None] * freq[None, :]
    phase = jnp.concatenate([phase, phase], axis=-1)
    return jnp.cos(phase), jnp.sin(phase)


def rotate(vectors, cosine, sine):
    half = vectors.shape[-1] // 2
    turned = jnp.concatenate([-vectors[..., half:], vectors[..., :half]], axis=-1)
    return vectors * cosine + turned * sine


def reference(hidden_in, w_query, w_key, w_value, q_bias, k_bias, v_bias):
    positions = jnp.arange(TOKENS, dtype=jnp.int32)
    cosine, sine = angles(positions, HEAD)
    query = jnp.dot(hidden_in, w_query, preferred_element_type=jnp.float32) + q_bias
    query = query.reshape(TOKENS, HQ, HEAD).transpose(1, 0, 2)
    query = rotate(query, cosine, sine).astype(jnp.bfloat16)
    keys = jnp.dot(hidden_in, w_key, preferred_element_type=jnp.float32) + k_bias
    keys = keys.reshape(TOKENS, KVH, HEAD).transpose(1, 0, 2)
    keys = rotate(keys, cosine, sine).astype(jnp.bfloat16)
    values = jnp.dot(hidden_in, w_value, preferred_element_type=jnp.float32) + v_bias
    values = values.astype(jnp.bfloat16).reshape(TOKENS, KVH, HEAD).transpose(1, 0, 2)
    group = HQ // KVH
    scale = float(HEAD) ** -0.5
    causal = positions[:, None] >= positions[None, :]

    def one_head(head_index):
        q_head = lax.dynamic_index_in_dim(query, head_index, 0, keepdims=False)
        k_head = lax.dynamic_index_in_dim(keys, head_index // group, 0, keepdims=False)
        v_head = lax.dynamic_index_in_dim(values, head_index // group, 0, keepdims=False)
        scores = jnp.dot(q_head, k_head.T, preferred_element_type=jnp.float32) * scale
        scores = jnp.where(causal, scores, -jnp.inf)
        row_max = jnp.max(scores, axis=1, keepdims=True)
        weights = jnp.exp(scores - row_max)
        total_sum = jnp.sum(weights, axis=1)
        mixed = jnp.dot(weights.astype(jnp.bfloat16), v_head, preferred_element_type=jnp.float32)
        return (mixed / total_sum[:, None]).astype(jnp.bfloat16)

    result = lax.map(one_head, jnp.arange(HQ, dtype=jnp.int32))
    return result.transpose(1, 0, 2).reshape(TOKENS, HQ * HEAD)
```

```python
import functools
import math

import jax
import jax.numpy as jnp
from jax import lax
from jax.experimental import pallas as pl
from jax.experimental.pallas import tpu as pltpu
from jax.sharding import PartitionSpec as P

HEAD = 128
GROUP = 8
HALF = 192
PART = HALF // 2
DEPTH = 1024
QCOLS = GROUP * HEAD
ALLCOLS = QCOLS + 2 * HEAD
LANES = GROUP * HALF
TILES = 16
AXES = ("seq", "tp")
VMEM_LIMIT = 48 * 1024 * 1024
EXP2_SCALE = float(HEAD) ** (-0.5) * math.log2(math.e)
NT = (((1,), (1,)), ((), ()))
TN = (((0,), (0,)), ((), ()))
rope_base = 1000000.0


def _place(flat):
    seq, tp = divmod(flat, 8)
    x_lo, z = divmod(tp, 4)
    y, rest = divmod(seq, 4)
    x_hi, core = divmod(rest, 2)
    return x_hi * 2 + x_lo, y, z, core


def _index(x, y, z, core):
    x_hi, x_lo = divmod(x % 4, 2)
    return (((y % 4) * 2 + x_hi) * 2 + core) * 8 + x_lo * 4 + z % 4


def _send(value, move):
    pairs = [(i, _index(*move(*_place(i)))) for i in range(128)]
    return lax.ppermute(value, AXES, pairs)


def z_up(x, y, z, c):
    return x, y, z + 1, c


def z_down(x, y, z, c):
    return x, y, z - 1, c


def x_near(x, y, z, c):
    return x ^ 1, y, z, c


def x_far(x, y, z, c):
    return x ^ 2, y, z, c


def y_up(x, y, z, c):
    return x, y + 1, z, c


def y_down(x, y, z, c):
    return x, y - 1, z, c


def y_far(x, y, z, c):
    return x, y + 2, z, c


def other_core(x, y, z, c):
    return x, y, z, 1 - c


def mirror_cross(x, y, z, c):
    return 3 - x, 3 - y, z, 1 - c


def mirror(x, y, z, c):
    return x ^ 2, 3 - y, z, 1 - c


def _join(refs):
    if len(refs) == 1:
        return refs[0][...]
    return jnp.concatenate([r[...] for r in refs], axis=0)


def _proj_body(counts, first, meta, *refs):
    parts = sum(counts)
    pieces, at = [], 0
    for count in counts:
        pieces.append(refs[at : at + count])
        at += count
    w_q, w_k, w_v = refs[parts : parts + 3]
    acc = refs[-1]
    step, block = pl.program_id(0), pl.program_id(1)
    width = w_q.shape[1]

    if first:

        @pl.when((step == 0) & (block == 0))
        def _():
            acc[...] = jnp.zeros_like(acc)

    else:

        @pl.when((step == 0) & (block == 0))
        def _():
            acc[...] = refs[parts + 3][...]

    for i, piece in enumerate(pieces):

        @pl.when(step == i)
        def _():
            x = _join(piece)
            cols = pl.ds(pl.multiple_of(block * width, width), width)
            acc[:, cols] += jnp.dot(x, w_q[...], preferred_element_type=jnp.float32)

            @pl.when(block == 0)
            def _():
                acc[:, QCOLS : QCOLS + HEAD] += jnp.dot(
                    x, w_k[...], preferred_element_type=jnp.float32
                )
                acc[:, QCOLS + HEAD :] += jnp.dot(x, w_v[...], preferred_element_type=jnp.float32)


def _whole(shape):
    return pl.BlockSpec(shape, lambda *_: (0,) * len(shape))


def _project(slices, pieces, weights, acc=None, blocks=2):
    flat = [part for piece in pieces for part in piece]
    width = QCOLS // blocks
    in_specs = [_whole(part.shape) for part in flat] + [
        pl.BlockSpec((DEPTH, width), lambda p, b, m: (m[p], b)),
        pl.BlockSpec((DEPTH, HEAD), lambda p, b, m: (m[p], 0)),
        pl.BlockSpec((DEPTH, HEAD), lambda p, b, m: (m[p], 0)),
    ]
    operands = [slices, *flat, *weights]
    if acc is not None:
        in_specs.append(_whole((HALF, ALLCOLS)))
        operands.append(acc)
    n = len(pieces)
    return pl.pallas_call(
        functools.partial(_proj_body, [len(p) for p in pieces], acc is None),
        out_shape=jax.ShapeDtypeStruct((HALF, ALLCOLS), jnp.float32),
        grid_spec=pltpu.PrefetchScalarGridSpec(
            num_scalar_prefetch=1,
            grid=(n, blocks),
            in_specs=in_specs,
            out_specs=_whole((HALF, ALLCOLS)),
        ),
        compiler_params=pltpu.CompilerParams(vmem_limit_bytes=VMEM_LIMIT),
        cost_estimate=pl.CostEstimate(
            flops=2 * n * HALF * DEPTH * ALLCOLS,
            bytes_accessed=2 * n * DEPTH * ALLCOLS,
            transcendentals=0,
        ),
        name="project",
    )(*operands)


def _rotate(u, cosine, sine):
    return u * cosine + pltpu.roll(u, HEAD // 2, 1) * sine


def _last_kv_body(meta, a, b, w_k, w_v, acc, k_bias, v_bias, cosine, sine, out):
    x = _join([a, b])
    k = acc[:, :HEAD] + jnp.dot(x, w_k[...], preferred_element_type=jnp.float32)
    v = acc[:, HEAD:] + jnp.dot(x, w_v[...], preferred_element_type=jnp.float32)
    out[:, :HEAD] = _rotate(k + k_bias[...], cosine[...], sine[...]).astype(jnp.bfloat16)
    out[:, HEAD:] = (v + v_bias[...]).astype(jnp.bfloat16)


def _last_kv(slices, piece, w_k, w_v, acc, k_bias, v_bias, cosine, sine):
    a, b = piece
    return pl.pallas_call(
        _last_kv_body,
        out_shape=jax.ShapeDtypeStruct((HALF, 2 * HEAD), jnp.bfloat16),
        grid_spec=pltpu.PrefetchScalarGridSpec(
            num_scalar_prefetch=1,
            grid=(1,),
            in_specs=[
                _whole(a.shape),
                _whole(b.shape),
                pl.BlockSpec((DEPTH, HEAD), lambda i, m: (m[0], 0)),
                pl.BlockSpec((DEPTH, HEAD), lambda i, m: (m[0], 0)),
                pl.BlockSpec((HALF, 2 * HEAD), lambda i, m: (0, QCOLS // (2 * HEAD))),
                _whole((1, HEAD)),
                _whole((1, HEAD)),
                _whole((HALF, HEAD)),
                _whole((HALF, HEAD)),
            ],
            out_specs=_whole((HALF, 2 * HEAD)),
        ),
        compiler_params=pltpu.CompilerParams(vmem_limit_bytes=VMEM_LIMIT),
        cost_estimate=pl.CostEstimate(
            flops=4 * HALF * DEPTH * HEAD, bytes_accessed=4 * DEPTH * HEAD, transcendentals=0
        ),
        name="last_kv",
    )(slices, a, b, w_k, w_v, acc, k_bias, v_bias, cosine, sine)


def _last_q_body(meta, a, b, w_q, acc, q_bias, cosine, sine, out):
    x = _join([a, b])
    q = acc[...] + jnp.dot(x, w_q[...], preferred_element_type=jnp.float32) + q_bias[...]
    for h in range(q.shape[1] // HEAD):
        cols = slice(h * HEAD, (h + 1) * HEAD)
        out[:, cols] = _rotate(q[:, cols], cosine[...], sine[...]).astype(jnp.bfloat16)


def _last_q(slices, piece, w_q, acc, q_bias, cosine, sine, blocks=4):
    a, b = piece
    width = QCOLS // blocks
    return pl.pallas_call(
        _last_q_body,
        out_shape=jax.ShapeDtypeStruct((HALF, QCOLS), jnp.bfloat16),
        grid_spec=pltpu.PrefetchScalarGridSpec(
            num_scalar_prefetch=1,
            grid=(blocks,),
            in_specs=[
                _whole(a.shape),
                _whole(b.shape),
                pl.BlockSpec((DEPTH, width), lambda i, m: (m[0], i)),
                pl.BlockSpec((HALF, width), lambda i, m: (0, i)),
                pl.BlockSpec((1, width), lambda i, m: (0, i)),
                _whole((HALF, HEAD)),
                _whole((HALF, HEAD)),
            ],
            out_specs=pl.BlockSpec((HALF, width), lambda i, m: (0, i)),
        ),
        compiler_params=pltpu.CompilerParams(vmem_limit_bytes=VMEM_LIMIT),
        cost_estimate=pl.CostEstimate(
            flops=2 * HALF * DEPTH * QCOLS, bytes_accessed=2 * DEPTH * QCOLS, transcendentals=0
        ),
        name="last_q",
    )(slices, a, b, w_q, acc, q_bias, cosine, sine)


def _attend_body(jobs, has_state, final, heads, meta, *refs):
    kv = refs[:8]
    queries = refs[8 : 8 + len(jobs)]
    at = 8 + len(jobs)
    states_in = refs[at : at + 2 * len(jobs)] if has_state else ()
    at += len(states_in)
    n_out = len(jobs) * (1 if final else 2)
    outs = refs[at : at + n_out]
    rows, keys, values, stat, acc = refs[at + n_out :]
    lanes = heads * HALF
    for i in range(8):
        for j in range(2):
            start = pl.multiple_of(meta[2 * i + j] * HALF, HALF)
            keys[pl.ds(start, HALF), :] = kv[i][j, :, :HEAD]
            values[pl.ds(start, HALF), :] = kv[i][j, :, HEAD:]
    for job, diagonal in enumerate(jobs):
        for h in range(heads):
            rows[h * HALF : (h + 1) * HALF, :] = queries[job][:, h * HEAD : (h + 1) * HEAD]
        count = meta[TILES + job]
        if has_state:
            stat[...] = states_in[2 * job][...]
            acc[...] = states_in[2 * job + 1][...]
        else:
            stat[0:1, :] = jnp.full((1, lanes), -1e30, jnp.float32)
            stat[1:2, :] = jnp.zeros((1, lanes), jnp.float32)
            acc[...] = jnp.zeros_like(acc)

        def step(start, size, mask):
            k = keys[pl.ds(start, size), :]
            v = values[pl.ds(start, size), :]
            scores = lax.dot_general(k, rows[...], NT, preferred_element_type=jnp.float32)
            if mask:
                key = lax.broadcasted_iota(jnp.int32, (size, lanes), 0)
                row = lax.rem(lax.broadcasted_iota(jnp.int32, (1, lanes), 1), HALF)
                scores = jnp.where(key <= row, scores, -jnp.inf)
            old = stat[0:1, :]
            new = jnp.maximum(old, jnp.max(scores, axis=0, keepdims=True))
            weights = jnp.exp2((scores - new) * EXP2_SCALE)
            shrink = jnp.exp2((old - new) * EXP2_SCALE)
            stat[0:1, :] = new
            stat[1:2, :] = stat[1:2, :] * shrink + jnp.sum(weights, axis=0, keepdims=True)
            acc[...] = acc[...] * shrink + lax.dot_general(
                v, weights.astype(jnp.bfloat16), TN, preferred_element_type=jnp.float32
            )

        @pl.loop(0, count // 4)
        def _(j):
            step(pl.multiple_of(j * (4 * HALF), 4 * HALF), 4 * HALF, False)

        @pl.loop(count // 4 * 4, count)
        def _(j):
            step(pl.multiple_of(j * HALF, HALF), HALF, False)

        if diagonal:
            step(pl.multiple_of(count * HALF, HALF), HALF, True)
        if final:
            for h in range(0, heads, 2):
                cols = slice(h * HALF, (h + 2) * HALF)
                pair = (acc[:, cols] / stat[1:2, cols]).T.astype(jnp.bfloat16)
                outs[job][:, h * HEAD : (h + 1) * HEAD] = pair[:HALF]
                outs[job][:, (h + 1) * HEAD : (h + 2) * HEAD] = pair[HALF:]
        else:
            outs[2 * job][...] = stat[...]
            outs[2 * job + 1][...] = acc[...]


def _attend(meta, kv, queries, jobs, states=(), final=False, heads=GROUP, first_head=0):
    lanes = heads * HALF
    part = first_head // heads
    vmem = pl.BlockSpec(memory_space=pltpu.VMEM)
    width = heads * HEAD
    in_specs = [_whole((2, HALF, 2 * HEAD))] * 8
    in_specs += [pl.BlockSpec((HALF, width), lambda i, m: (0, part))] * len(jobs)
    in_specs += [_whole((8, lanes)), _whole((HEAD, lanes))] * (len(states) // 2)
    if final:
        out_shape = [jax.ShapeDtypeStruct((HALF, width), jnp.bfloat16)] * len(jobs)
    else:
        out_shape = [
            jax.ShapeDtypeStruct((8, lanes), jnp.float32),
            jax.ShapeDtypeStruct((HEAD, lanes), jnp.float32),
        ] * len(jobs)
    return pl.pallas_call(
        functools.partial(_attend_body, jobs, bool(states), final, heads),
        out_shape=out_shape,
        grid_spec=pltpu.PrefetchScalarGridSpec(
            num_scalar_prefetch=1,
            grid=(1,),
            in_specs=in_specs,
            out_specs=[_whole(o.shape) for o in out_shape],
            scratch_shapes=[
                pltpu.VMEM((lanes, HEAD), jnp.bfloat16),
                pltpu.VMEM((TILES * HALF, HEAD), jnp.bfloat16),
                pltpu.VMEM((TILES * HALF, HEAD), jnp.bfloat16),
                pltpu.VMEM((8, lanes), jnp.float32),
                pltpu.VMEM((HEAD, lanes), jnp.float32),
            ],
        ),
        compiler_params=pltpu.CompilerParams(vmem_limit_bytes=VMEM_LIMIT),
        cost_estimate=pl.CostEstimate(
            flops=4 * 8 * len(jobs) * HALF * HEAD * lanes,
            bytes_accessed=4 * 1024 * 1024,
            transcendentals=8 * len(jobs) * HALF * lanes,
        ),
        name="attend",
    )(meta, *kv, *queries, *states)


def _angles(positions):
    half = HEAD // 2
    freq = rope_base ** (-2.0 * jnp.arange(half, dtype=jnp.float32) / HEAD)
    phase = positions.astype(jnp.float32)[:, None] * freq[None, :]
    cosine, sine = jnp.cos(phase), jnp.sin(phase)
    return jnp.concatenate([cosine, cosine], axis=-1), jnp.concatenate([-sine, sine], axis=-1)


def _gather_kv(kv):
    far = _send(kv, x_far)
    pair = jnp.stack([kv, far])
    near = [pair, _send(pair, y_up), _send(pair, y_down), _send(pair, y_far)]
    return near + [_send(p, other_core) for p in near]


def local(hidden, w_query, w_key, w_value, q_bias, k_bias, v_bias):
    seq = lax.axis_index("seq")
    tp = lax.axis_index("tp")
    y, x_hi, core = seq // 4, seq // 2 % 2, seq % 2
    x_lo, z = tp // 4, tp % 4
    weights = (w_query, w_key, w_value)
    q_bias, k_bias, v_bias = q_bias[None], k_bias[None], v_bias[None]

    def feature(lo, dz):
        return lo * 4 + (z + dz) % 4

    def tile_seq(dy, dx, dc):
        return ((y + dy) % 4 * 2 + (x_hi ^ dx)) * 2 + (core ^ dc)

    order = [tile_seq(dy, dx, dc) for dc in (0, 1) for dy in (0, -1, 1, 2) for dx in (0, 1)]
    i32 = functools.partial(jnp.asarray, dtype=jnp.int32)
    early_order = [i32(s) for s in order]
    late_order = [i32(15 - s) for s in order]
    row = jnp.arange(HALF, dtype=jnp.int32)
    early_cos, early_sin = _angles(seq * (2 * HALF) + row)
    late_cos, late_sin = _angles((31 - 2 * seq) * HALF + row)

    def spread(whole, part_a, part_b, lo):
        up_a = _send(part_a, z_up)
        down_b = _send(part_b, z_down)
        side = _send(whole, x_near)
        up_b = _send(part_b, z_up)
        down_a = _send(part_a, z_down)
        slices = jnp.stack([i32(feature(lo, 0))])
        acc = _project(slices, [(whole,)], weights)
        far_a = _send(up_a, z_up)
        far_b = _send(down_b, z_down)
        side_up = _send(side, z_up)
        side_down = _send(side, z_down)
        slices = jnp.stack([i32(feature(lo, -1)), i32(feature(lo, 1)), i32(feature(1 - lo, 0))])
        acc = _project(slices, [(up_a, up_b), (down_a, down_b), (side,)], weights, acc)
        last_a = _send(far_a, x_near)
        last_b = _send(far_b, x_near)
        slices = jnp.stack([i32(feature(lo, 2)), i32(feature(1 - lo, -1)), i32(feature(1 - lo, 1))])
        acc = _project(slices, [(far_a, far_b), (side_up,), (side_down,)], weights, acc)
        return acc, (last_a, last_b), jnp.stack([i32(feature(1 - lo, 2))])

    early = hidden[:HALF]
    late = _send(hidden[HALF:], mirror_cross)

    acc, piece, slices = spread(early, hidden[:PART], hidden[PART:HALF], x_lo)
    early_kv = _last_kv(slices, piece, w_key, w_value, acc, k_bias, v_bias, early_cos, early_sin)
    early_keys = _gather_kv(early_kv)
    early_q = _last_q(slices, piece, w_query, acc, q_bias, early_cos, early_sin)

    acc, piece, slices = spread(late, late[:PART], late[PART:], 1 - x_lo)
    late_kv = _last_kv(slices, piece, w_key, w_value, acc, k_bias, v_bias, late_cos, late_sin)
    late_keys = _gather_kv(late_kv)
    late_q = _last_q(slices, piece, w_query, acc, q_bias, late_cos, late_sin)

    meta = jnp.stack(early_order + [i32(seq), i32(16 - seq)])
    queries = (early_q, late_q)
    low = _attend(meta, early_keys, queries, (True, False), heads=4, first_head=0)
    high = _attend(meta, early_keys, queries, (True, False), heads=4, first_head=4)
    late_meta = jnp.stack(late_order + [i32(15 - seq)])
    early_meta = jnp.stack(late_order + [i32(seq)])
    (late_low,) = _attend(
        late_meta, late_keys, (late_q,), (True,), low[2:], final=True, heads=4, first_head=0
    )
    back_low = _send(late_low, mirror)
    (late_high,) = _attend(
        late_meta, late_keys, (late_q,), (True,), high[2:], final=True, heads=4, first_head=4
    )
    back_high = _send(late_high, mirror)
    (early_low,) = _attend(
        early_meta, late_keys, (early_q,), (False,), low[:2], final=True, heads=4, first_head=0
    )
    (early_high,) = _attend(
        early_meta, late_keys, (early_q,), (False,), high[:2], final=True, heads=4, first_head=4
    )
    return jnp.concatenate(
        [
            jnp.concatenate([early_low, early_high], axis=1),
            jnp.concatenate([back_low, back_high], axis=1),
        ],
        axis=0,
    )


def solution(mesh):
    return jax.shard_map(
        local,
        mesh=mesh,
        in_specs=(
            P("seq", "tp"),
            P(None, "tp"),
            P(None, "tp"),
            P(None, "tp"),
            P("tp"),
            P("tp"),
            P("tp"),
        ),
        out_specs=P("seq", "tp"),
        check_vma=False,
    )
```

```python
import functools
import math

import jax
import jax.numpy as jnp
from jax import lax
from jax.experimental import pallas as pl
from jax.experimental.pallas import tpu as pltpu
from jax.sharding import PartitionSpec as P

HEAD = 128
GROUP = 8
HALF = 192
PART = HALF // 2
DEPTH = 1024
QCOLS = GROUP * HEAD
ALLCOLS = QCOLS + 2 * HEAD
LANES = GROUP * HALF
TILES = 16
AXES = ("seq", "tp")
VMEM_LIMIT = 48 * 1024 * 1024
EXP2_SCALE = float(HEAD) ** (-0.5) * math.log2(math.e)
NT = (((1,), (1,)), ((), ()))
TN = (((0,), (0,)), ((), ()))
rope_base = 1000000.0


def _place(flat):
    seq, tp = divmod(flat, 8)
    x_lo, z = divmod(tp, 4)
    y, rest = divmod(seq, 4)
    x_hi, core = divmod(rest, 2)
    return x_hi * 2 + x_lo, y, z, core


def _index(x, y, z, core):
    x_hi, x_lo = divmod(x % 4, 2)
    return (((y % 4) * 2 + x_hi) * 2 + core) * 8 + x_lo * 4 + z % 4


def _send(value, move):
    pairs = [(i, _index(*move(*_place(i)))) for i in range(128)]
    return lax.ppermute(value, AXES, pairs)


def z_up(x, y, z, c):
    return x, y, z + 1, c


def z_down(x, y, z, c):
    return x, y, z - 1, c


def x_near(x, y, z, c):
    return x ^ 1, y, z, c


def x_far(x, y, z, c):
    return x ^ 2, y, z, c


def y_up(x, y, z, c):
    return x, y + 1, z, c


def y_down(x, y, z, c):
    return x, y - 1, z, c


def y_far(x, y, z, c):
    return x, y + 2, z, c


def other_core(x, y, z, c):
    return x, y, z, 1 - c


def mirror_cross(x, y, z, c):
    return 3 - x, 3 - y, z, 1 - c


def mirror(x, y, z, c):
    return x ^ 2, 3 - y, z, 1 - c


VMEM = pl.BlockSpec(memory_space=pltpu.VMEM)
HBM = pl.BlockSpec(memory_space=pl.ANY)
SMEM = pl.BlockSpec(memory_space=pltpu.SMEM)


def _in_vmem(value):
    return pltpu.with_memory_space_constraint(value, pltpu.VMEM)


def _join(refs):
    if len(refs) == 1:
        return refs[0][...]
    return jnp.concatenate([r[...] for r in refs], axis=0)


def _block(index):
    return pl.ds(pl.multiple_of(index * DEPTH, DEPTH), DEPTH)


def _fetches(slices, n, far, near, sem):
    return [
        [
            pltpu.make_async_copy(
                src.at[_block(slices[i]), :], dst.at[_block(slices[i]), :], sem.at[i, j]
            )
            for j, (src, dst) in enumerate(zip(far, near))
        ]
        for i in range(n)
    ]


def _proj_body(counts, fetch, held, started, slices, *refs):
    n = len(counts)
    at = sum(counts)
    parts = refs[:at]
    far = refs[at : at + 3] if fetch else ()
    at += len(far)
    at += 3 if held else 0
    acc_in = refs[at] if started else None
    at += 1 if started else 0
    near, acc = refs[at : at + 3], refs[at + 3]
    copies = _fetches(slices, n, far, near, refs[at + 4]) if fetch else None
    if fetch:
        for group in copies:
            for copy in group:
                copy.start()
    at = 0
    for i, count in enumerate(counts):
        x = _join(parts[at : at + count])
        at += count
        if fetch:
            for copy in copies[i]:
                copy.wait()
        rows = _block(slices[i])
        for w, cols in zip(near, (slice(0, QCOLS), slice(QCOLS, QCOLS + HEAD), slice(QCOLS + HEAD, ALLCOLS))):
            term = jnp.dot(x, w[rows, :], preferred_element_type=jnp.float32)
            if i:
                acc[:, cols] += term
            elif started:
                acc[:, cols] = acc_in[:, cols] + term
            else:
                acc[:, cols] = term


def _project(slices, pieces, far=None, near=None, acc=None):
    flat = [part for piece in pieces for part in piece]
    n = len(pieces)
    operands = [slices, *map(_in_vmem, flat)]
    in_specs = [SMEM] + [VMEM] * len(flat)
    if far is not None:
        operands += far
        in_specs += [HBM] * 3
    aliases = {}
    if near is not None:
        aliases.update({len(operands) + i: i for i in range(3)})
        operands += map(_in_vmem, near)
        in_specs += [VMEM] * 3
    if acc is not None:
        aliases[len(operands)] = 3
        operands.append(_in_vmem(acc))
        in_specs.append(VMEM)
    shapes = [(8 * DEPTH, QCOLS), (8 * DEPTH, HEAD), (8 * DEPTH, HEAD)]
    out = pl.pallas_call(
        functools.partial(
            _proj_body, [len(p) for p in pieces], far is not None, near is not None, acc is not None
        ),
        out_shape=[pltpu.VMEM(shape, jnp.bfloat16) for shape in shapes]
        + [pltpu.VMEM((HALF, ALLCOLS), jnp.float32)],
        in_specs=in_specs,
        out_specs=[VMEM] * 4,
        input_output_aliases=aliases,
        scratch_shapes=[pltpu.SemaphoreType.DMA((n, 3))] if far is not None else [],
        compiler_params=pltpu.CompilerParams(vmem_limit_bytes=8 * 1024 * 1024),
        cost_estimate=pl.CostEstimate(
            flops=2 * n * HALF * DEPTH * ALLCOLS,
            bytes_accessed=2 * n * DEPTH * ALLCOLS,
            transcendentals=0,
        ),
        name="project",
    )(*operands)
    return out[:3], out[3]


def _rotate(u, cosine, sine):
    return u * cosine + pltpu.roll(u, HEAD // 2, 1) * sine


def _last_kv_body(fetch, slices, a, acc, k_bias, v_bias, cosine, sine, *refs):
    if fetch:
        far, (_, _), near, out, sem = refs[:2], refs[2:4], refs[4:6], refs[6], refs[7]
        copies = _fetches(slices, 1, far, near, sem)[0]
        for copy in copies:
            copy.start()
        for copy in copies:
            copy.wait()
    else:
        (_, _), near, out = refs[:2], refs[2:4], refs[4]
    x = a[...]
    rows = _block(slices[0])
    k = acc[:, QCOLS : QCOLS + HEAD] + jnp.dot(
        x, near[0][rows, :], preferred_element_type=jnp.float32
    )
    v = acc[:, QCOLS + HEAD :] + jnp.dot(x, near[1][rows, :], preferred_element_type=jnp.float32)
    out[:, :HEAD] = _rotate(k + k_bias[...], cosine[...], sine[...]).astype(jnp.bfloat16)
    out[:, HEAD:] = (v + v_bias[...]).astype(jnp.bfloat16)


def _last_kv(slices, piece, far, near, acc, k_bias, v_bias, cosine, sine):
    fetch = far is not None
    operands = [slices, piece, acc, k_bias, v_bias, cosine, sine]
    operands = [operands[0], *map(_in_vmem, operands[1:])]
    in_specs = [SMEM] + [VMEM] * 6
    if fetch:
        operands += far
        in_specs += [HBM] * 2
    aliases = {len(operands): 0, len(operands) + 1: 1}
    operands += map(_in_vmem, near)
    in_specs += [VMEM] * 2
    out = pl.pallas_call(
        functools.partial(_last_kv_body, fetch),
        out_shape=[pltpu.VMEM((8 * DEPTH, HEAD), jnp.bfloat16)] * 2
        + [pltpu.VMEM((HALF, 2 * HEAD), jnp.bfloat16)],
        in_specs=in_specs,
        out_specs=[VMEM] * 3,
        input_output_aliases=aliases,
        scratch_shapes=[pltpu.SemaphoreType.DMA((1, 2))] if fetch else [],
        compiler_params=pltpu.CompilerParams(vmem_limit_bytes=8 * 1024 * 1024),
        cost_estimate=pl.CostEstimate(
            flops=4 * HALF * DEPTH * HEAD, bytes_accessed=4 * DEPTH * HEAD, transcendentals=0
        ),
        name="last_kv",
    )(*operands)
    return out[:2], out[2]


def _last_q_body(fetch, slices, a, acc, q_bias, cosine, sine, *refs):
    if fetch:
        far, _, near, out, sem = refs
        ((copy,),) = _fetches(slices, 1, (far,), (near,), sem)
        copy.start()
        copy.wait()
    else:
        _, near, out = refs
    x = a[...]
    rows = _block(slices[0])
    for h in range(0, GROUP, 2):
        both = slice(h * HEAD, (h + 2) * HEAD)
        q = acc[:, both] + jnp.dot(x, near[rows, both], preferred_element_type=jnp.float32)
        q = q + q_bias[:, both]
        for i in range(2):
            cols = slice((h + i) * HEAD, (h + i + 1) * HEAD)
            u = q[:, i * HEAD : (i + 1) * HEAD]
            out[:, cols] = _rotate(u, cosine[...], sine[...]).astype(jnp.bfloat16)


def _last_q(slices, piece, far, near, acc, q_bias, cosine, sine):
    fetch = far is not None
    operands = [piece, acc, q_bias, cosine, sine]
    operands = [slices, *map(_in_vmem, operands)]
    in_specs = [SMEM] + [VMEM] * 5
    if fetch:
        operands.append(far)
        in_specs.append(HBM)
    aliases = {len(operands): 0}
    operands.append(_in_vmem(near))
    in_specs.append(VMEM)
    return pl.pallas_call(
        functools.partial(_last_q_body, fetch),
        out_shape=[
            pltpu.VMEM((8 * DEPTH, QCOLS), jnp.bfloat16),
            pltpu.VMEM((HALF, QCOLS), jnp.bfloat16),
        ],
        in_specs=in_specs,
        out_specs=[VMEM] * 2,
        input_output_aliases=aliases,
        scratch_shapes=[pltpu.SemaphoreType.DMA((1, 1))] if fetch else [],
        compiler_params=pltpu.CompilerParams(vmem_limit_bytes=8 * 1024 * 1024),
        cost_estimate=pl.CostEstimate(
            flops=2 * HALF * DEPTH * QCOLS, bytes_accessed=2 * DEPTH * QCOLS, transcendentals=0
        ),
        name="last_q",
    )(*operands)


def _attend_body(jobs, has_state, final, heads, meta, *refs):
    near, other = refs[:4], refs[4]
    queries = refs[5 : 5 + len(jobs)]
    at = 5 + len(jobs)
    states_in = refs[at : at + 2 * len(jobs)] if has_state else ()
    at += len(states_in)
    n_out = len(jobs) * (1 if final else 2)
    outs = refs[at : at + n_out]
    rows, keys, values, stat, acc = refs[at + n_out :]
    lanes = heads * HALF
    for i in range(TILES):
        start = pl.multiple_of(meta[i] * HALF, HALF)
        tile = near[i // 2].at[i % 2] if i < 8 else other.at[i - 8]
        keys[pl.ds(start, HALF), :] = tile[:, :HEAD]
        values[pl.ds(start, HALF), :] = tile[:, HEAD:]
    for job, (part, diagonal) in enumerate(jobs):
        for h in range(heads):
            col = (part * heads + h) * HEAD
            rows[h * HALF : (h + 1) * HALF, :] = queries[job][:, col : col + HEAD]
        count = meta[TILES + job]
        if has_state:
            stat[...] = states_in[2 * job][...]
            acc[...] = states_in[2 * job + 1][...]
        else:
            stat[0:1, :] = jnp.full((1, lanes), -1e30, jnp.float32)
            stat[1:8, :] = jnp.zeros((7, lanes), jnp.float32)
            acc[...] = jnp.zeros_like(acc)

        def step(start, size, mask):
            k = keys[pl.ds(start, size), :]
            v = values[pl.ds(start, size), :]
            scores = lax.dot_general(k, rows[...], NT, preferred_element_type=jnp.float32)
            if mask:
                key = lax.broadcasted_iota(jnp.int32, (size, lanes), 0)
                row = lax.rem(lax.broadcasted_iota(jnp.int32, (1, lanes), 1), HALF)
                scores = jnp.where(key <= row, scores, -jnp.inf)
            old = stat[0:1, :]
            new = jnp.maximum(old, jnp.max(scores, axis=0, keepdims=True))
            weights = jnp.exp2((scores - new) * EXP2_SCALE)
            shrink = jnp.exp2((old - new) * EXP2_SCALE)
            stat[0:1, :] = new
            stat[1:2, :] = stat[1:2, :] * shrink + jnp.sum(weights, axis=0, keepdims=True)
            acc[...] = acc[...] * shrink + lax.dot_general(
                v, weights.astype(jnp.bfloat16), TN, preferred_element_type=jnp.float32
            )

        @pl.loop(0, count // 4)
        def _(j):
            step(pl.multiple_of(j * (4 * HALF), 4 * HALF), 4 * HALF, False)

        @pl.loop(count // 4 * 4, count)
        def _(j):
            step(pl.multiple_of(j * HALF, HALF), HALF, False)

        if diagonal:
            step(pl.multiple_of(count * HALF, HALF), HALF, True)
        if final:
            for h in range(0, heads, 2):
                cols = slice(h * HALF, (h + 2) * HALF)
                pair = (acc[:, cols] / stat[1:2, cols]).T.astype(jnp.bfloat16)
                outs[job][:, h * HEAD : (h + 1) * HEAD] = pair[:HALF]
                outs[job][:, (h + 1) * HEAD : (h + 2) * HEAD] = pair[HALF:]
        else:
            outs[2 * job][...] = stat[...]
            outs[2 * job + 1][...] = acc[...]


def _attend(meta, kv, queries, jobs, states=(), final=False, heads=4):
    lanes = heads * HALF
    if final:
        out_shape = [pltpu.VMEM((HALF, heads * HEAD), jnp.bfloat16)] * len(jobs)
    else:
        out_shape = [
            pltpu.VMEM((8, lanes), jnp.float32),
            pltpu.VMEM((HEAD, lanes), jnp.float32),
        ] * len(jobs)
    operands = [*kv, *queries, *states]
    return pl.pallas_call(
        functools.partial(_attend_body, jobs, bool(states), final, heads),
        out_shape=out_shape,
        in_specs=[SMEM] + [VMEM] * len(operands),
        out_specs=[VMEM] * len(out_shape),
        scratch_shapes=[
            pltpu.VMEM((lanes, HEAD), jnp.bfloat16),
            pltpu.VMEM((TILES * HALF, HEAD), jnp.bfloat16),
            pltpu.VMEM((TILES * HALF, HEAD), jnp.bfloat16),
            pltpu.VMEM((8, lanes), jnp.float32),
            pltpu.VMEM((HEAD, lanes), jnp.float32),
        ],
        compiler_params=pltpu.CompilerParams(vmem_limit_bytes=24 * 1024 * 1024),
        cost_estimate=pl.CostEstimate(
            flops=4 * 8 * len(jobs) * HALF * HEAD * lanes,
            bytes_accessed=4 * 1024 * 1024,
            transcendentals=8 * len(jobs) * HALF * lanes,
        ),
        name="attend",
    )(meta, *map(_in_vmem, operands))


def _angles(positions):
    half = HEAD // 2
    freq = rope_base ** (-2.0 * jnp.arange(half, dtype=jnp.float32) / HEAD)
    phase = positions.astype(jnp.float32)[:, None] * freq[None, :]
    cosine, sine = jnp.cos(phase), jnp.sin(phase)
    return jnp.concatenate([cosine, cosine], axis=-1), jnp.concatenate([-sine, sine], axis=-1)


def _after(value, *earlier):
    return lax.optimization_barrier((value, *earlier))[0]


def local(hidden, w_query, w_key, w_value, q_bias, k_bias, v_bias):
    seq = lax.axis_index("seq")
    tp = lax.axis_index("tp")
    y, x_hi, core = seq // 4, seq // 2 % 2, seq % 2
    x_lo, z = tp // 4, tp % 4
    weights = [w_query, w_key, w_value]
    q_bias, k_bias, v_bias = q_bias[None], k_bias[None], v_bias[None]

    def feature(lo, dz):
        return lo * 4 + (z + dz) % 4

    def tile_seq(dy, dx, dc):
        return ((y + dy) % 4 * 2 + (x_hi ^ dx)) * 2 + (core ^ dc)

    order = jnp.stack(
        [tile_seq(dy, dx, dc) for dc in (0, 1) for dy in (0, -1, 1, 2) for dx in (0, 1)]
    ).astype(jnp.int32)
    far_lo = 1 - x_lo

    def ints(*values):
        return jnp.stack(values).astype(jnp.int32)

    early, late = hidden[:HALF], hidden[HALF:]
    late = _send(late, mirror_cross)

    def first_wave(own):
        return _send(own, z_up), _send(own, z_down), _send(own, x_near)

    def second_wave(up, down, side):
        far_a, far_b = _send(up[:PART], z_up), _send(down[PART:], z_down)
        return far_a, far_b, _send(side, z_up), _send(side, z_down)

    up, down, side = first_wave(early)
    near, acc = _project(ints(feature(x_lo, 0)), [(early,)], far=weights)
    far_a, far_b, side_up, side_down = second_wave(up, down, side)
    late_side = _send(late, x_near)
    near, acc = _project(
        ints(feature(x_lo, -1), feature(x_lo, 1), feature(far_lo, 0)),
        [(up,), (down,), (side,)],
        far=weights,
        near=near,
        acc=acc,
    )
    far = jnp.concatenate([far_a, far_b], axis=0)
    last = _send(far, x_near)
    near, acc = _project(
        ints(feature(x_lo, 2), feature(far_lo, -1), feature(far_lo, 1)),
        [(far,), (side_up,), (side_down,)],
        far=weights,
        near=near,
        acc=acc,
    )
    row = jnp.arange(HALF, dtype=jnp.int32)
    cosine, sine = _angles(seq * (2 * HALF) + row)
    late_cosine, late_sine = _angles((31 - 2 * seq) * HALF + row)
    which = ints(feature(far_lo, 2))
    (near_q, *near_kv) = near
    near_kv, early_kv = _last_kv(
        which, last, weights[1:], near_kv, acc, k_bias, v_bias, cosine, sine
    )
    near_q, early_q = _last_q(which, last, weights[0], near_q, acc, q_bias, cosine, sine)
    near = [near_q, *near_kv]

    late_z = _after(late, side_up, side_down)
    up, down = _send(late_z, z_up), _send(late_z, z_down)
    pair = jnp.stack([early_kv, _send(early_kv, x_far)])
    near, acc = _project(
        ints(feature(far_lo, 0), feature(x_lo, 0)), [(late,), (late_side,)], near=near
    )
    far_a, far_b, side_up, side_down = second_wave(up, down, late_side)
    early_pairs = [pair, _send(pair, y_up), _send(pair, y_down), _send(pair, y_far)]
    near, acc = _project(
        ints(feature(far_lo, -1), feature(far_lo, 1)), [(up,), (down,)], near=near, acc=acc
    )
    far = jnp.concatenate([far_a, far_b], axis=0)
    last = _send(far, x_near)
    early_keys = [*early_pairs, _send(jnp.concatenate(early_pairs, axis=0), other_core)]
    near, acc = _project(
        ints(feature(far_lo, 2), feature(x_lo, -1), feature(x_lo, 1)),
        [(far,), (side_up,), (side_down,)],
        near=near,
        acc=acc,
    )
    which = ints(feature(x_lo, 2))
    (near_q, *near_kv) = near
    near_kv, late_kv = _last_kv(
        which, last, None, near_kv, acc, k_bias, v_bias, late_cosine, late_sine
    )
    pair = jnp.stack([late_kv, _send(late_kv, x_far)])
    near_q, late_q = _last_q(
        which, _after(last, late_kv), None, near_q, acc, q_bias, late_cosine, late_sine
    )

    meta = jnp.concatenate([order, ints(seq, 16 - seq)])
    late_pairs = [pair, _send(pair, y_up), _send(pair, y_down), _send(pair, y_far)]
    low = _attend(meta, early_keys, (early_q, late_q), ((0, True), (0, False)))
    late_keys = [*late_pairs, _send(jnp.concatenate(late_pairs, axis=0), other_core)]
    high = _attend(meta, early_keys, (early_q, _after(late_q, low[0])), ((1, True), (1, False)))
    late_order = 15 - order
    meta = jnp.concatenate([late_order, ints(15 - seq)])
    (late_low,) = _attend(meta, late_keys, (late_q,), ((0, True),), low[2:], final=True)
    back_low = _send(late_low, mirror)
    (late_high,) = _attend(
        meta, late_keys, (_after(late_q, late_low),), ((1, True),), high[2:], final=True
    )
    back_high = _send(late_high, mirror)
    meta = jnp.concatenate([late_order, ints(seq, seq)])
    early_low, early_high = _attend(
        meta,
        late_keys,
        (_after(early_q, late_high), early_q),
        ((0, False), (1, False)),
        (*low[:2], *high[:2]),
        final=True,
    )
    return jnp.concatenate(
        [
            jnp.concatenate([early_low, early_high], axis=1),
            jnp.concatenate([back_low, back_high], axis=1),
        ],
        axis=0,
    )


def solution(mesh):
    return jax.shard_map(
        local,
        mesh=mesh,
        in_specs=(
            P("seq", "tp"),
            P(None, "tp"),
            P(None, "tp"),
            P(None, "tp"),
            P("tp"),
            P("tp"),
            P("tp"),
        ),
        out_specs=P("seq", "tp"),
        check_vma=False,
    )
```

```python
import functools
import math

import jax
import jax.numpy as jnp
from jax import lax
from jax.experimental import pallas as pl
from jax.experimental.pallas import tpu as pltpu
from jax.sharding import PartitionSpec as P

HEAD = 128
GROUP = 8
HALF = 192
PART = HALF // 2
DEPTH = 1024
QCOLS = GROUP * HEAD
ALLCOLS = QCOLS + 2 * HEAD
LANES = 4 * HALF
TILES = 16
SPAN = 4 * HALF
BLOCKS = 5
AXES = ("seq", "tp")
VMEM_LIMIT = 48 * 1024 * 1024
EXP2_SCALE = float(HEAD) ** (-0.5) * math.log2(math.e)
NT = (((1,), (1,)), ((), ()))
TN = (((0,), (0,)), ((), ()))
rope_base = 1000000.0


def _place(flat):
    seq, tp = divmod(flat, 8)
    x_lo, z = divmod(tp, 4)
    y, rest = divmod(seq, 4)
    x_hi, core = divmod(rest, 2)
    return x_hi * 2 + x_lo, y, z, core


def _index(x, y, z, core):
    x_hi, x_lo = divmod(x % 4, 2)
    return (((y % 4) * 2 + x_hi) * 2 + core) * 8 + x_lo * 4 + z % 4


def _send(value, move):
    pairs = [(i, _index(*move(*_place(i)))) for i in range(128)]
    return lax.ppermute(value, AXES, pairs)


def z_up(x, y, z, c):
    return x, y, z + 1, c


def z_down(x, y, z, c):
    return x, y, z - 1, c


def x_near(x, y, z, c):
    return x ^ 1, y, z, c


def x_far(x, y, z, c):
    return x ^ 2, y, z, c


def y_up(x, y, z, c):
    return x, y + 1, z, c


def y_down(x, y, z, c):
    return x, y - 1, z, c


def y_far(x, y, z, c):
    return x, y + 2, z, c


def other_core(x, y, z, c):
    return x, y, z, 1 - c


def mirror_cross(x, y, z, c):
    return 3 - x, 3 - y, z, 1 - c


def mirror(x, y, z, c):
    return x ^ 2, 3 - y, z, 1 - c


VMEM = pl.BlockSpec(memory_space=pltpu.VMEM)
HBM = pl.BlockSpec(memory_space=pl.ANY)
SMEM = pl.BlockSpec(memory_space=pltpu.SMEM)


def _block(index):
    return pl.ds(pl.multiple_of(index * DEPTH, DEPTH), DEPTH)


def _piece_loads(parts, pieces, x, sem):
    loads = []
    for i, piece in enumerate(pieces):
        at = 0
        loads.append([])
        for k, (operand, start, size) in enumerate(piece):
            loads[-1].append(
                pltpu.make_async_copy(
                    parts[operand].at[pl.ds(start, size)],
                    x.at[i, pl.ds(at, size)],
                    sem.at[i, k],
                )
            )
            at += size
    return loads


def _weight_loads(slices, n, far, near, sem):
    return [
        [
            pltpu.make_async_copy(src.at[_block(slices[i]), :], dst.at[i], sem.at[i, j])
            for j, (src, dst) in enumerate(zip(far, near))
        ]
        for i in range(n)
    ]


def _start(group):
    for copy in group:
        copy.start()


def _wait(group):
    for copy in group:
        copy.wait()


def _proj_body(arrays, pieces, started, slices, *refs):
    n = len(pieces)
    parts, far = refs[:arrays], refs[arrays : arrays + 3]
    at = arrays + 3
    acc_in = refs[at] if started else None
    at += 1 if started else 0
    acc, x, near = refs[at], refs[at + 1], refs[at + 2 : at + 5]
    x_sem, w_sem = refs[at + 5 : at + 7]
    x_loads = _piece_loads(parts, pieces, x, x_sem)
    w_loads = _weight_loads(slices, n, far, near, w_sem)
    for i in range(min(2, n)):
        _start(x_loads[i])
        _start(w_loads[i])
    spans = (slice(0, QCOLS), slice(QCOLS, QCOLS + HEAD), slice(QCOLS + HEAD, ALLCOLS))
    for i in range(n):
        _wait(x_loads[i])
        _wait(w_loads[i])
        if i + 2 < n:
            _start(x_loads[i + 2])
            _start(w_loads[i + 2])
        for w, cols in zip(near, spans):
            term = jnp.dot(x[i], w[i], preferred_element_type=jnp.float32)
            if i:
                acc[:, cols] += term
            elif started:
                acc[:, cols] = acc_in[:, cols] + term
            else:
                acc[:, cols] = term


def _project(slices, arrays, pieces, weights, acc=None):
    n = len(pieces)
    operands = [slices, *arrays, *weights]
    in_specs = [SMEM] + [HBM] * (len(arrays) + 3)
    aliases = {}
    if acc is not None:
        aliases[len(operands)] = 0
        operands.append(acc)
        in_specs.append(VMEM)
    return pl.pallas_call(
        functools.partial(_proj_body, len(arrays), pieces, acc is not None),
        out_shape=jax.ShapeDtypeStruct((HALF, ALLCOLS), jnp.float32),
        in_specs=in_specs,
        out_specs=VMEM,
        input_output_aliases=aliases,
        scratch_shapes=[
            pltpu.VMEM((n, HALF, DEPTH), jnp.bfloat16),
            pltpu.VMEM((n, DEPTH, QCOLS), jnp.bfloat16),
            pltpu.VMEM((n, DEPTH, HEAD), jnp.bfloat16),
            pltpu.VMEM((n, DEPTH, HEAD), jnp.bfloat16),
            pltpu.SemaphoreType.DMA((n, 2)),
            pltpu.SemaphoreType.DMA((n, 3)),
        ],
        compiler_params=pltpu.CompilerParams(vmem_limit_bytes=20 * 1024 * 1024),
        cost_estimate=pl.CostEstimate(
            flops=2 * n * HALF * DEPTH * ALLCOLS,
            bytes_accessed=2 * n * DEPTH * ALLCOLS,
            transcendentals=0,
        ),
        name="project",
    )(*operands)


def _rotate(u, cosine, sine):
    cosine = jnp.concatenate([cosine[...], cosine[...]], axis=1)
    sine = jnp.concatenate([-sine[...], sine[...]], axis=1)
    return u * cosine + pltpu.roll(u, HEAD // 2, 1) * sine


def _last_kv_body(arrays, pieces, slices, *refs):
    n = len(pieces)
    parts, (w_k, w_v) = refs[:arrays], refs[arrays : arrays + 2]
    acc, k_bias, v_bias, cosine, sine, out, x, near_k, near_v, x_sem, w_sem = refs[arrays + 2 :]
    x_loads = _piece_loads(parts, pieces, x, x_sem)
    w_loads = _weight_loads(slices, n, (w_k, w_v), (near_k, near_v), w_sem)
    for group in x_loads + w_loads:
        _start(group)
    k, v = acc[:, QCOLS : QCOLS + HEAD], acc[:, QCOLS + HEAD :]
    for i in range(n):
        _wait(x_loads[i])
        _wait(w_loads[i])
        k += jnp.dot(x[i], near_k[i], preferred_element_type=jnp.float32)
        v += jnp.dot(x[i], near_v[i], preferred_element_type=jnp.float32)
    out[:, :HEAD] = _rotate(k + k_bias[...], cosine, sine).astype(jnp.bfloat16)
    out[:, HEAD:] = (v + v_bias[...]).astype(jnp.bfloat16)


def _last_kv(slices, arrays, pieces, w_k, w_v, acc, k_bias, v_bias, cosine, sine):
    n = len(pieces)
    near = [acc, k_bias, v_bias, cosine, sine]
    return pl.pallas_call(
        functools.partial(_last_kv_body, len(arrays), pieces),
        out_shape=jax.ShapeDtypeStruct((HALF, 2 * HEAD), jnp.bfloat16),
        in_specs=[SMEM] + [HBM] * (len(arrays) + 2) + [VMEM] * len(near),
        out_specs=VMEM,
        scratch_shapes=[
            pltpu.VMEM((n, HALF, DEPTH), jnp.bfloat16),
            pltpu.VMEM((n, DEPTH, HEAD), jnp.bfloat16),
            pltpu.VMEM((n, DEPTH, HEAD), jnp.bfloat16),
            pltpu.SemaphoreType.DMA((n, 2)),
            pltpu.SemaphoreType.DMA((n, 2)),
        ],
        compiler_params=pltpu.CompilerParams(vmem_limit_bytes=8 * 1024 * 1024),
        cost_estimate=pl.CostEstimate(
            flops=4 * n * HALF * DEPTH * HEAD,
            bytes_accessed=4 * n * DEPTH * HEAD,
            transcendentals=0,
        ),
        name="last_kv",
    )(slices, *arrays, w_k, w_v, *near)


def _last_q_body(arrays, pieces, slices, *refs):
    n = len(pieces)
    parts, w_q = refs[:arrays], refs[arrays]
    acc, q_bias, cosine, sine, out, x, near, x_sem, w_sem = refs[arrays + 1 :]
    x_loads = _piece_loads(parts, pieces, x, x_sem)
    for group in x_loads:
        _start(group)
    w_loads = []
    for i in range(4):
        cols = slice(i * 2 * HEAD, (i + 1) * 2 * HEAD)
        w_loads.append(
            [
                pltpu.make_async_copy(
                    w_q.at[_block(slices[j]), cols], near.at[i, j], w_sem.at[i, j]
                )
                for j in range(n)
            ]
        )
    _start(w_loads[0])
    _start(w_loads[1])
    for group in x_loads:
        _wait(group)
    for i in range(4):
        both = slice(i * 2 * HEAD, (i + 1) * 2 * HEAD)
        q = acc[:, both] + q_bias[:, both]
        _wait(w_loads[i])
        if i + 2 < 4:
            _start(w_loads[i + 2])
        for j in range(n):
            q += jnp.dot(x[j], near[i, j], preferred_element_type=jnp.float32)
        for j in range(2):
            cols = slice((2 * i + j) * HEAD, (2 * i + j + 1) * HEAD)
            u = q[:, j * HEAD : (j + 1) * HEAD]
            out[:, cols] = _rotate(u, cosine, sine).astype(jnp.bfloat16)


def _last_q(slices, arrays, pieces, w_q, acc, q_bias, cosine, sine):
    n = len(pieces)
    near = [acc, q_bias, cosine, sine]
    return pl.pallas_call(
        functools.partial(_last_q_body, len(arrays), pieces),
        out_shape=jax.ShapeDtypeStruct((HALF, QCOLS), jnp.bfloat16),
        in_specs=[SMEM] + [HBM] * (len(arrays) + 1) + [VMEM] * len(near),
        out_specs=VMEM,
        scratch_shapes=[
            pltpu.VMEM((n, HALF, DEPTH), jnp.bfloat16),
            pltpu.VMEM((4, n, DEPTH, 2 * HEAD), jnp.bfloat16),
            pltpu.SemaphoreType.DMA((n, 2)),
            pltpu.SemaphoreType.DMA((4, n)),
        ],
        compiler_params=pltpu.CompilerParams(vmem_limit_bytes=12 * 1024 * 1024),
        cost_estimate=pl.CostEstimate(
            flops=2 * n * HALF * DEPTH * QCOLS,
            bytes_accessed=2 * n * DEPTH * QCOLS,
            transcendentals=0,
        ),
        name="last_q",
    )(slices, *arrays, w_q, *near)


def _stitch(shapes, moves, *operands):
    def body(*refs):
        sem = refs[-1]
        copies = []
        for i, (operand, start, size, o, at) in enumerate(moves):
            src, out = refs[operand], refs[len(operands) + o]
            if len(src.shape) < len(out.shape):
                copies.append(pltpu.make_async_copy(src, out.at[at], sem.at[i]))
            else:
                copies.append(
                    pltpu.make_async_copy(
                        src.at[pl.ds(start, size)], out.at[pl.ds(at, size)], sem.at[i]
                    )
                )
        _start(copies)
        _wait(copies)

    return pl.pallas_call(
        body,
        out_shape=[jax.ShapeDtypeStruct(shape, jnp.bfloat16) for shape in shapes],
        in_specs=[HBM] * len(operands),
        out_specs=[VMEM] * len(shapes),
        scratch_shapes=[pltpu.SemaphoreType.DMA((len(moves),))],
        compiler_params=pltpu.CompilerParams(vmem_limit_bytes=4 * 1024 * 1024),
        name="stitch",
    )(*operands)


def _stack_pair(first, second):
    return _stitch([(2, HALF, 2 * HEAD)], [(0, 0, 1, 0, 0), (1, 0, 1, 0, 1)], first, second)[0]


def _stack_pairs(pairs):
    moves = [(i, 0, 2, 0, 2 * i) for i in range(4)]
    return _stitch([(8, HALF, 2 * HEAD)], moves, *pairs)[0]


def _attend_body(given, first, final, part, meta, *refs):
    kv, refs = refs[:given], refs[given:]
    queries, refs = refs[:2], refs[2:]
    states_in, refs = ((), refs) if first else (refs[:2], refs[2:])
    outs, refs = refs[:2], refs[2:]
    keys, values = kv if given == 2 else refs[:2]
    rows, even, odd, place = refs[0 if given == 2 else 2 :][:4]
    stat, acc = refs[-2:] if final else outs
    groups = acc.shape[0] // 2
    for group in range(groups):
        for job in range(2):
            for h in range(4):
                col = (part * 4 + group * 4 + h) * HEAD
                rows[2 * group + job, h * HALF : (h + 1) * HALF, :] = queries[job][
                    :, col : col + HEAD
                ]
    for h in range(4):
        place[0:1, h * HALF : (h + 1) * HALF] = lax.broadcasted_iota(jnp.int32, (1, HALF), 1) + 1
    if first:
        stat[:, 0:1, :] = jnp.full((2 * groups, 1, LANES), -1e30, jnp.float32)
        stat[:, 1:8, :] = jnp.zeros((2 * groups, 7, LANES), jnp.float32)
        acc[...] = jnp.zeros_like(acc)
    else:
        stat[...] = states_in[0][2 * part : 2 * part + 2 * groups]
        acc[...] = states_in[1][2 * part : 2 * part + 2 * groups]
    for i in range(TILES if given == 5 else 0):
        start = pl.multiple_of(meta[i] * HALF, HALF)
        tile = kv[i // 2].at[i % 2] if i < 8 else kv[4].at[i - 8]
        keys[pl.ds(start, HALF), :] = tile[:, :HEAD]
        values[pl.ds(start, HALF), :] = tile[:, HEAD:]

    def entry(b, i):
        return meta[TILES + 4 * lax.rem(b, BLOCKS) + i]

    def job_of(b):
        return entry(b, 0) + 2 * lax.div(b, BLOCKS)

    def score(b, out):
        start = pl.multiple_of(entry(b, 1) * HALF, 4 * HALF)
        k = keys[pl.ds(start, SPAN), :]
        scores = lax.dot_general(k, rows[job_of(b)], NT, preferred_element_type=jnp.float32)
        seen = entry(b, 2) + entry(b, 3) * place[0:1, :]
        key = lax.broadcasted_iota(jnp.int32, (SPAN, LANES), 0)
        scores = jnp.where(key < seen, scores, -jnp.inf)
        out[0:SPAN, :] = scores
        out[SPAN : SPAN + 1, :] = jnp.max(scores, axis=0, keepdims=True)

    def finish(b, src):
        job = job_of(b)
        start = pl.multiple_of(entry(b, 1) * HALF, 4 * HALF)
        v = values[pl.ds(start, SPAN), :]
        old = stat[job, 0:1, :]
        new = jnp.maximum(old, src[SPAN : SPAN + 1, :])
        weights = jnp.exp2((src[0:SPAN, :] - new) * EXP2_SCALE)
        shrink = jnp.exp2((old - new) * EXP2_SCALE)
        stat[job, 0:1, :] = new
        stat[job, 1:2, :] = stat[job, 1:2, :] * shrink + jnp.sum(weights, axis=0, keepdims=True)
        acc[job] = acc[job] * shrink + lax.dot_general(
            v, weights.astype(jnp.bfloat16), TN, preferred_element_type=jnp.float32
        )

    total = BLOCKS * groups
    score(0, even)

    @pl.loop(0, (total - 1) // 2)
    def _(i):
        score(2 * i + 1, odd)
        finish(2 * i, even)
        score(2 * i + 2, even)
        finish(2 * i + 1, odd)

    if total % 2:
        finish(total - 1, even)
    else:
        score(total - 1, odd)
        finish(total - 2, even)
        finish(total - 1, odd)
    if final:
        for group in range(groups):
            for job in range(2):
                for h in range(0, 4, 2):
                    cols = slice(h * HALF, (h + 2) * HALF)
                    done = acc[2 * group + job, :, cols] / stat[2 * group + job, 1:2, cols]
                    pair = done.T.astype(jnp.bfloat16)
                    at = (group * 4 + h) * HEAD
                    outs[job][:HALF, at : at + HEAD] = pair[:HALF]
                    outs[job][:HALF, at + HEAD : at + 2 * HEAD] = pair[HALF:]
        if outs[1].shape[0] > HALF:
            spare = outs[1].shape[0] - HALF
            outs[1][HALF:, :] = jnp.zeros((spare, outs[1].shape[1]), jnp.bfloat16)


def _attend(meta, kv, queries, states=(), groups=1, part=0, spare=0):
    final = bool(states)
    ordered = [(TILES * HALF, HEAD)] * (2 if len(kv) == 5 else 0)
    state_shape = [(2 * groups, 8, LANES), (2 * groups, HEAD, LANES)]
    if final:
        out_shape = [
            jax.ShapeDtypeStruct((HALF, groups * 4 * HEAD), jnp.bfloat16),
            jax.ShapeDtypeStruct((HALF + spare, groups * 4 * HEAD), jnp.bfloat16),
        ]
    else:
        out_shape = [jax.ShapeDtypeStruct(shape, jnp.float32) for shape in state_shape]
    if final:
        out_shape += [jax.ShapeDtypeStruct(shape, jnp.bfloat16) for shape in ordered]
        ordered = []
    near = [*kv, *queries, *states]
    out = pl.pallas_call(
        functools.partial(_attend_body, len(kv), not states, final, part),
        out_shape=out_shape,
        in_specs=[SMEM] + [VMEM] * len(near),
        out_specs=[VMEM] * len(out_shape),
        scratch_shapes=[pltpu.VMEM(shape, jnp.bfloat16) for shape in ordered]
        + [
            pltpu.VMEM((2 * groups, LANES, HEAD), jnp.bfloat16),
            pltpu.VMEM((SPAN + 8, LANES), jnp.float32),
            pltpu.VMEM((SPAN + 8, LANES), jnp.float32),
            pltpu.VMEM((8, LANES), jnp.int32),
        ]
        + ([pltpu.VMEM(shape, jnp.float32) for shape in state_shape] if final else []),
        compiler_params=pltpu.CompilerParams(vmem_limit_bytes=28 * 1024 * 1024),
        cost_estimate=pl.CostEstimate(
            flops=4 * groups * BLOCKS * SPAN * HEAD * LANES,
            bytes_accessed=4 * 1024 * 1024,
            transcendentals=groups * BLOCKS * SPAN * LANES,
        ),
        name="attend",
    )(meta, *near)
    return out[:2], out[2:]


def _blocks(early_count, early_own, late_count, late_own):
    early_blocks = early_count // 4 + 1 if early_own else (early_count + 3) // 4
    entries = []
    for b in range(BLOCKS):
        is_late = (b >= early_blocks).astype(jnp.int32)
        tile = 4 * (b - is_late * early_blocks)
        count = jnp.where(is_late == 1, late_count, early_count)
        own = jnp.where(is_late == 1, int(late_own), int(early_own))
        entries += [is_late, jnp.minimum(tile, TILES - 4), (count - tile) * HALF, own]
    return jnp.stack(entries).astype(jnp.int32)


def _angles(positions):
    half = HEAD // 2
    freq = rope_base ** (-2.0 * jnp.arange(half, dtype=jnp.float32) / HEAD)
    phase = positions.astype(jnp.float32)[:, None] * freq[None, :]
    return jnp.cos(phase), jnp.sin(phase)


def _after(value, *earlier):
    return lax.optimization_barrier((value, *earlier))[0]


def local(hidden, w_query, w_key, w_value, q_bias, k_bias, v_bias):
    seq = lax.axis_index("seq")
    tp = lax.axis_index("tp")
    y, x_hi, core = seq // 4, seq // 2 % 2, seq % 2
    x_lo, z = tp // 4, tp % 4
    weights = [w_query, w_key, w_value]
    q_bias, k_bias, v_bias = q_bias[None], k_bias[None], v_bias[None]

    def feature(lo, dz):
        return lo * 4 + (z + dz) % 4

    def tile_seq(dy, dx, dc):
        return ((y + dy) % 4 * 2 + (x_hi ^ dx)) * 2 + (core ^ dc)

    order = jnp.stack(
        [tile_seq(dy, dx, dc) for dc in (0, 1) for dy in (0, -1, 1, 2) for dx in (0, 1)]
    ).astype(jnp.int32)
    far_lo = 1 - x_lo

    def ints(*values):
        return jnp.stack(values).astype(jnp.int32)

    w_query, w_key, w_value = weights = [
        pltpu.with_memory_space_constraint(w, pltpu.HBM) for w in weights
    ]
    early, late = _stitch(
        [(HALF, DEPTH)] * 2, [(0, 0, HALF, 0, 0), (0, HALF, HALF, 1, 0)], hidden
    )
    side = _send(early, x_near)
    up, down = _send(early, z_up), _send(early, z_down)
    late = _send(late, mirror_cross)
    row = jnp.arange(HALF, dtype=jnp.int32)
    rope = _angles(seq * (2 * HALF) + row)
    late_rope = _angles((31 - 2 * seq) * HALF + row)
    up, *ropes = lax.optimization_barrier((up, *rope, *late_rope))
    rope, late_rope = ropes[:2], ropes[2:]
    whole = [(0, 0, HALF)], [(1, 0, HALF)], [(2, 0, HALF)], [(3, 0, HALF)]

    to_up, to_down = _stitch(
        [(HALF + PART, DEPTH)] * 2,
        [(0, 0, PART, 0, 0), (2, 0, HALF, 0, PART), (1, PART, PART, 1, 0), (2, 0, HALF, 1, PART)],
        up,
        down,
        side,
    )
    from_down, from_up = _send(to_up, z_up), _send(to_down, z_down)
    late_side = _send(late, x_near)
    acc = _project(
        ints(feature(x_lo, 0), feature(x_lo, -1), feature(x_lo, 1), feature(far_lo, 0)),
        [early, up, down, side],
        whole,
        weights,
    )
    (far,) = _stitch(
        [(HALF, DEPTH)],
        [(0, 0, PART, 0, 0), (1, 0, PART, 0, PART)],
        _after(from_down, acc),
        from_up,
    )
    last = _send(far, x_near)
    both = _after(_stitch(
        [(2 * HALF, DEPTH)], [(0, 0, HALF, 0, 0), (1, 0, HALF, 0, HALF)], late, late_side
    )[0], far)
    up, down = _send(both, z_up), _send(both, z_down)
    acc = _project(
        ints(feature(x_lo, 2), feature(far_lo, -1), feature(far_lo, 1)),
        [far, from_down, from_up],
        ([(0, 0, HALF)], [(1, PART, HALF)], [(2, PART, HALF)]),
        weights,
        acc,
    )
    late_acc = _project(
        ints(feature(far_lo, 0), feature(x_lo, 0)),
        [_after(late, acc), late_side],
        whole[:2],
        weights,
    )
    which = ints(feature(far_lo, 2))
    last = _after(last, late_acc)
    early_kv = _last_kv(which, [last], whole[:1], w_key, w_value, acc, k_bias, v_bias, *rope)
    early_q = _last_q(
        which, [_after(last, early_kv)], whole[:1], w_query, acc, q_bias, *rope
    )
    pair = _stack_pair(_after(early_kv, early_q), _send(early_kv, x_far))

    early_pairs = [pair, _send(pair, y_up), _send(pair, y_down), _send(pair, y_far)]
    to_up, to_down = _stitch(
        [(HALF, DEPTH)] * 2,
        [
            (0, 0, PART, 0, 0),
            (0, HALF, PART, 0, PART),
            (1, PART, PART, 1, 0),
            (1, HALF + PART, PART, 1, PART),
        ],
        _after(up, pair),
        down,
    )
    from_down, from_up = _send(to_up, z_up), _send(to_down, z_down)
    acc = _project(
        ints(feature(far_lo, -1), feature(x_lo, -1), feature(far_lo, 1), feature(x_lo, 1)),
        [_after(up, to_up), down],
        ([(0, 0, HALF)], [(0, HALF, HALF)], [(1, 0, HALF)], [(1, HALF, HALF)]),
        weights,
        late_acc,
    )
    which = ints(feature(far_lo, 2), feature(x_lo, 2))
    pieces = ([(0, 0, PART), (1, 0, PART)], [(0, PART, PART), (1, PART, PART)])
    late_kv = _last_kv(
        which, [from_down, from_up], pieces, w_key, w_value, acc, k_bias, v_bias, *late_rope
    )
    late_q = _last_q(
        which,
        [_after(from_down, late_kv), from_up],
        pieces,
        w_query,
        acc,
        q_bias,
        *late_rope,
    )

    early_pairs = [*early_pairs[:3], _after(early_pairs[3], late_kv)]
    early_keys = [*early_pairs, _send(_stack_pairs(early_pairs), other_core)]
    pair = _stack_pair(_after(late_kv, late_q), _send(late_kv, x_far))
    early_meta = jnp.concatenate([order, _blocks(seq, True, 16 - seq, False)])
    late_meta = jnp.concatenate([15 - order, _blocks(seq, False, 15 - seq, True)])
    late_pairs = [pair, _send(pair, y_up), _send(pair, y_down), _send(pair, y_far)]
    queries = (early_q, late_q)
    states, _ = _attend(early_meta, early_keys, queries, groups=2)
    late_pairs = [*late_pairs[:3], _after(late_pairs[3], states[0])]
    late_keys = [*late_pairs, _send(_stack_pairs(late_pairs), other_core)]
    (early_low, late_low), ordered = _attend(
        late_meta, late_keys, queries, states, part=0, spare=16
    )
    back_low = _send(late_low, mirror)
    (early_high, late_high), _ = _attend(late_meta, ordered, queries, states, part=1)
    back_high = _send(late_high, mirror)
    return jnp.concatenate(
        [
            jnp.concatenate([early_low, early_high], axis=1),
            jnp.concatenate([back_low[:HALF], back_high], axis=1),
        ],
        axis=0,
    )


def solution(mesh):
    return jax.shard_map(
        local,
        mesh=mesh,
        in_specs=(
            P("seq", "tp"),
            P(None, "tp"),
            P(None, "tp"),
            P(None, "tp"),
            P("tp"),
            P("tp"),
            P("tp"),
        ),
        out_specs=P("seq", "tp"),
        check_vma=False,
    )
```

```python
import functools
import math

import jax
import jax.numpy as jnp
from jax import lax
from jax.experimental import pallas as pl
from jax.experimental.pallas import tpu as pltpu
from jax.sharding import PartitionSpec as P

HEAD = 128
GROUP = 8
HALF = 192
PART = HALF // 2
ROWS = 2 * HALF
DEPTH = 1024
QCOLS = GROUP * HEAD
ALLCOLS = QCOLS + 2 * HEAD
LANES = 4 * HALF
TILES = 16
SPAN = 4 * HALF
BLOCKS = 5
AXES = ("seq", "tp")
VMEM_LIMIT = 48 * 1024 * 1024
EXP2_SCALE = float(HEAD) ** (-0.5) * math.log2(math.e)
NT = (((1,), (1,)), ((), ()))
TN = (((0,), (0,)), ((), ()))
rope_base = 1000000.0


def _place(flat):
    seq, tp = divmod(flat, 8)
    x_lo, z = divmod(tp, 4)
    y, rest = divmod(seq, 4)
    x_hi, core = divmod(rest, 2)
    return x_hi * 2 + x_lo, y, z, core


def _index(x, y, z, core):
    x_hi, x_lo = divmod(x % 4, 2)
    return (((y % 4) * 2 + x_hi) * 2 + core) * 8 + x_lo * 4 + z % 4


def _send(value, move):
    pairs = [(i, _index(*move(*_place(i)))) for i in range(128)]
    return lax.ppermute(value, AXES, pairs)


def z_up(x, y, z, c):
    return x, y, z + 1, c


def z_down(x, y, z, c):
    return x, y, z - 1, c


def x_near(x, y, z, c):
    return x ^ 1, y, z, c


def x_far(x, y, z, c):
    return x ^ 2, y, z, c


def y_up(x, y, z, c):
    return x, y + 1, z, c


def y_down(x, y, z, c):
    return x, y - 1, z, c


def y_far(x, y, z, c):
    return x, y + 2, z, c


def other_core(x, y, z, c):
    return x, y, z, 1 - c


def mirror_cross(x, y, z, c):
    return 3 - x, 3 - y, z, 1 - c


def mirror(x, y, z, c):
    return x ^ 2, 3 - y, z, 1 - c


VMEM = pl.BlockSpec(memory_space=pltpu.VMEM)
HBM = pl.BlockSpec(memory_space=pl.ANY)
SMEM = pl.BlockSpec(memory_space=pltpu.SMEM)


def _in_hbm(value):
    return pltpu.with_memory_space_constraint(value, pltpu.HBM)


def _block(index):
    return pl.ds(pl.multiple_of(index * DEPTH, DEPTH), DEPTH)


def _piece_loads(parts, pieces, x, sem):
    loads = []
    for i, piece in enumerate(pieces):
        at = 0
        loads.append([])
        for k, (operand, start, size) in enumerate(piece):
            loads[-1].append(
                pltpu.make_async_copy(
                    parts[operand].at[pl.ds(start, size)],
                    x.at[i, pl.ds(at, size)],
                    sem.at[i, k],
                )
            )
            at += size
    return loads


def _weight_loads(slices, n, far, near, sem):
    return [
        [
            pltpu.make_async_copy(src.at[_block(slices[i]), :], dst.at[i], sem.at[i, j])
            for j, (src, dst) in enumerate(zip(far, near))
        ]
        for i in range(n)
    ]


def _start(group):
    for copy in group:
        copy.start()


def _wait(group):
    for copy in group:
        copy.wait()


def _proj_body(arrays, pieces, started, slices, *refs):
    n = len(pieces)
    parts, far = refs[:arrays], refs[arrays : arrays + 3]
    refs = refs[arrays + 3 :]
    acc_in, refs = (refs[0], refs[1:]) if started else (None, refs)
    acc, x, near, (x_sem, w_sem, acc_sem) = refs[0], refs[1], refs[2:5], refs[5:8]
    x_loads = _piece_loads(parts, pieces, x, x_sem)
    w_loads = _weight_loads(slices, n, far, near, w_sem)
    for i in range(min(2, n)):
        _start(x_loads[i])
        _start(w_loads[i])
    if started:
        acc_load = pltpu.make_async_copy(acc_in, acc, acc_sem)
        acc_load.start()
    spans = (slice(0, QCOLS), slice(QCOLS, QCOLS + HEAD), slice(QCOLS + HEAD, ALLCOLS))
    for i in range(n):
        _wait(x_loads[i])
        _wait(w_loads[i])
        if i + 2 < n:
            _start(x_loads[i + 2])
            _start(w_loads[i + 2])
        if started and i == 0:
            acc_load.wait()
        for w, cols in zip(near, spans):
            term = jnp.dot(x[i], w[i], preferred_element_type=jnp.float32)
            if i or started:
                acc[:, cols] += term
            else:
                acc[:, cols] = term


def _project(slices, arrays, pieces, weights, acc=None):
    n = len(pieces)
    started = [] if acc is None else [acc]
    return pl.pallas_call(
        functools.partial(_proj_body, len(arrays), pieces, acc is not None),
        out_shape=jax.ShapeDtypeStruct((ROWS, ALLCOLS), jnp.float32),
        in_specs=[SMEM] + [HBM] * (len(arrays) + 3 + len(started)),
        out_specs=VMEM,
        scratch_shapes=[
            pltpu.VMEM((n, ROWS, DEPTH), jnp.bfloat16),
            pltpu.VMEM((n, DEPTH, QCOLS), jnp.bfloat16),
            pltpu.VMEM((n, DEPTH, HEAD), jnp.bfloat16),
            pltpu.VMEM((n, DEPTH, HEAD), jnp.bfloat16),
            pltpu.SemaphoreType.DMA((n, 3)),
            pltpu.SemaphoreType.DMA((n, 3)),
            pltpu.SemaphoreType.DMA,
        ],
        compiler_params=pltpu.CompilerParams(vmem_limit_bytes=28 * 1024 * 1024),
        cost_estimate=pl.CostEstimate(
            flops=2 * n * ROWS * DEPTH * ALLCOLS,
            bytes_accessed=2 * n * DEPTH * ALLCOLS,
            transcendentals=0,
        ),
        name="project",
    )(slices, *map(_in_hbm, arrays), *weights, *started)


def _rotate(u, cosine, sine):
    return u * cosine[...] + pltpu.roll(u, HEAD // 2, 1) * sine[...]


def _last_kv_body(arrays, pieces, slices, *refs):
    n = len(pieces)
    parts, (w_k, w_v), refs = refs[:arrays], refs[arrays : arrays + 2], refs[arrays + 2 :]
    given, (k_bias, v_bias, cosine, sine, out), refs = refs[0], refs[1:6], refs[6:]
    x, near_k, near_v, acc, x_sem, w_sem, sem = refs
    x_loads = _piece_loads(parts, pieces, x, x_sem)
    w_loads = _weight_loads(slices, n, (w_k, w_v), (near_k, near_v), w_sem)
    others = [pltpu.make_async_copy(given.at[:, pl.ds(QCOLS, 2 * HEAD)], acc, sem)]
    for group in x_loads + w_loads + [others]:
        _start(group)
    k = v = 0
    for i in range(n):
        _wait(x_loads[i])
        _wait(w_loads[i])
        k += jnp.dot(x[i], near_k[i], preferred_element_type=jnp.float32)
        v += jnp.dot(x[i], near_v[i], preferred_element_type=jnp.float32)
    _wait(others)
    k += acc[:, :HEAD]
    v += acc[:, HEAD:]
    k = _rotate(k + k_bias[...], cosine, sine).astype(jnp.bfloat16)
    v = (v + v_bias[...]).astype(jnp.bfloat16)
    for half in range(2):
        rows = slice(half * HALF, (half + 1) * HALF)
        out[half, :, :HEAD] = k[rows]
        out[half, :, HEAD:] = v[rows]


def _last_kv(slices, arrays, pieces, w_k, w_v, acc, k_bias, v_bias, cosine, sine):
    n = len(pieces)
    return pl.pallas_call(
        functools.partial(_last_kv_body, len(arrays), pieces),
        out_shape=jax.ShapeDtypeStruct((2, HALF, 2 * HEAD), jnp.bfloat16),
        in_specs=[SMEM] + [HBM] * (len(arrays) + 3) + [VMEM] * 4,
        out_specs=VMEM,
        scratch_shapes=[
            pltpu.VMEM((n, ROWS, DEPTH), jnp.bfloat16),
            pltpu.VMEM((n, DEPTH, HEAD), jnp.bfloat16),
            pltpu.VMEM((n, DEPTH, HEAD), jnp.bfloat16),
            pltpu.VMEM((ROWS, 2 * HEAD), jnp.float32),
            pltpu.SemaphoreType.DMA((n, 4)),
            pltpu.SemaphoreType.DMA((n, 2)),
            pltpu.SemaphoreType.DMA,
        ],
        compiler_params=pltpu.CompilerParams(vmem_limit_bytes=12 * 1024 * 1024),
        cost_estimate=pl.CostEstimate(
            flops=4 * n * ROWS * DEPTH * HEAD,
            bytes_accessed=4 * n * DEPTH * HEAD,
            transcendentals=0,
        ),
        name="last_kv",
    )(slices, *map(_in_hbm, arrays), w_k, w_v, acc, k_bias, v_bias, cosine, sine)


def _last_q_body(arrays, pieces, slices, *refs):
    n = len(pieces)
    parts, w_q, refs = refs[:arrays], refs[arrays], refs[arrays + 1 :]
    given, (q_bias, cosine, sine, out), refs = refs[0], refs[1:5], refs[5:]
    x, near, acc, x_sem, w_sem, sem = refs
    x_loads = _piece_loads(parts, pieces, x, x_sem)
    w_loads = _weight_loads(slices, n, (w_q,), (near,), w_sem)
    others = [pltpu.make_async_copy(given.at[:, pl.ds(0, QCOLS)], acc, sem)]
    _start(x_loads[0])
    _start(w_loads[0])
    _start(others)
    for i in range(1, n):
        _start(x_loads[i])
        _start(w_loads[i])
    for i in range(n):
        _wait(x_loads[i])
        _wait(w_loads[i])
        if i == 0:
            _wait(others)
        if i < n - 1:
            acc[...] += jnp.dot(x[i], near[i], preferred_element_type=jnp.float32)
    for i in range(0, GROUP, 2):
        both = slice(i * HEAD, (i + 2) * HEAD)
        q = acc[:, both] + jnp.dot(x[n - 1], near[n - 1, :, both], preferred_element_type=jnp.float32)
        q += q_bias[:, both]
        for j in range(2):
            cols = slice((i + j) * HEAD, (i + j + 1) * HEAD)
            u = q[:, j * HEAD : (j + 1) * HEAD]
            out[:, cols] = _rotate(u, cosine, sine).astype(jnp.bfloat16)


def _last_q(slices, arrays, pieces, w_q, acc, q_bias, cosine, sine):
    n = len(pieces)
    return pl.pallas_call(
        functools.partial(_last_q_body, len(arrays), pieces),
        out_shape=jax.ShapeDtypeStruct((ROWS, QCOLS), jnp.bfloat16),
        in_specs=[SMEM] + [HBM] * (len(arrays) + 2) + [VMEM] * 3,
        out_specs=VMEM,
        scratch_shapes=[
            pltpu.VMEM((n, ROWS, DEPTH), jnp.bfloat16),
            pltpu.VMEM((n, DEPTH, QCOLS), jnp.bfloat16),
            pltpu.VMEM((ROWS, QCOLS), jnp.float32),
            pltpu.SemaphoreType.DMA((n, 4)),
            pltpu.SemaphoreType.DMA((n, 1)),
            pltpu.SemaphoreType.DMA,
        ],
        compiler_params=pltpu.CompilerParams(vmem_limit_bytes=20 * 1024 * 1024),
        cost_estimate=pl.CostEstimate(
            flops=2 * n * ROWS * DEPTH * QCOLS,
            bytes_accessed=2 * n * DEPTH * QCOLS,
            transcendentals=0,
        ),
        name="last_q",
    )(slices, *map(_in_hbm, arrays), w_q, acc, q_bias, cosine, sine)


def _stitch(shapes, moves, *operands):
    def body(*refs):
        sem = refs[-1]
        copies = []
        for i, (operand, start, size, o, at) in enumerate(moves):
            src, out = refs[operand], refs[len(operands) + o]
            if len(src.shape) < len(out.shape):
                copies.append(pltpu.make_async_copy(src, out.at[at], sem.at[i]))
            else:
                copies.append(
                    pltpu.make_async_copy(
                        src.at[pl.ds(start, size)], out.at[pl.ds(at, size)], sem.at[i]
                    )
                )
        _start(copies)
        _wait(copies)

    return pl.pallas_call(
        body,
        out_shape=[jax.ShapeDtypeStruct(shape, jnp.bfloat16) for shape in shapes],
        in_specs=[HBM] * len(operands),
        out_specs=[VMEM] * len(shapes),
        scratch_shapes=[pltpu.SemaphoreType.DMA((len(moves),))],
        compiler_params=pltpu.CompilerParams(vmem_limit_bytes=4 * 1024 * 1024),
        name="stitch",
    )(*map(_in_hbm, operands))


def _stack_tiles(arrays):
    moves = [(i, 0, 2, 0, 2 * i) for i in range(4)]
    return _stitch([(8, HALF, 2 * HEAD)], moves, *arrays)[0]


def _attend_body(given, sort, first, final, part, meta, *refs):
    kv, refs = refs[:given], refs[given:]
    queries, refs = refs[0], refs[1:]
    states_in, refs = ((), refs) if first else (refs[:2], refs[2:])
    outs, refs = refs[:2], refs[2:]
    keys, values = refs[:2] if sort else kv
    rows, even, odd, place = refs[2 if sort else 0 :][:4]
    stat, acc = refs[-2:] if final else outs
    groups = acc.shape[0] // 2
    for group in range(groups):
        for job in range(2):
            for h in range(4):
                col = (part * 4 + group * 4 + h) * HEAD
                rows[2 * group + job, h * HALF : (h + 1) * HALF, :] = queries[
                    job * HALF : (job + 1) * HALF, col : col + HEAD
                ]
    for h in range(4):
        place[0:1, h * HALF : (h + 1) * HALF] = lax.broadcasted_iota(jnp.int32, (1, HALF), 1) + 1
    if first:
        stat[:, 0:1, :] = jnp.full((2 * groups, 1, LANES), -1e30, jnp.float32)
        stat[:, 1:8, :] = jnp.zeros((2 * groups, 7, LANES), jnp.float32)
        acc[...] = jnp.zeros_like(acc)
    else:
        stat[...] = states_in[0][2 * part : 2 * part + 2 * groups]
        acc[...] = states_in[1][2 * part : 2 * part + 2 * groups]
    tiles = [array.at[i] for array in kv for i in range(array.shape[0])] if sort else []
    for i, tile in enumerate(tiles):
        start = pl.multiple_of(meta[i] * HALF, HALF)
        keys[pl.ds(start, HALF), :] = tile[:, :HEAD]
        values[pl.ds(start, HALF), :] = tile[:, HEAD:]

    def entry(b, i):
        return meta[TILES + 4 * lax.rem(b, BLOCKS) + i]

    def job_of(b):
        return entry(b, 0) + 2 * lax.div(b, BLOCKS)

    def score(b, out):
        start = pl.multiple_of(entry(b, 1) * HALF, 4 * HALF)
        k = keys[pl.ds(start, SPAN), :]
        scores = lax.dot_general(k, rows[job_of(b)], NT, preferred_element_type=jnp.float32)
        seen = entry(b, 2) + entry(b, 3) * place[0:1, :]
        key = lax.broadcasted_iota(jnp.int32, (SPAN, LANES), 0)
        scores = jnp.where(key < seen, scores, -jnp.inf)
        out[0:SPAN, :] = scores
        out[SPAN : SPAN + 1, :] = jnp.max(scores, axis=0, keepdims=True)

    def finish(b, src):
        job = job_of(b)
        start = pl.multiple_of(entry(b, 1) * HALF, 4 * HALF)
        v = values[pl.ds(start, SPAN), :]
        old = stat[job, 0:1, :]
        new = jnp.maximum(old, src[SPAN : SPAN + 1, :])
        weights = jnp.exp2((src[0:SPAN, :] - new) * EXP2_SCALE)
        shrink = jnp.exp2((old - new) * EXP2_SCALE)
        stat[job, 0:1, :] = new
        stat[job, 1:2, :] = stat[job, 1:2, :] * shrink + jnp.sum(weights, axis=0, keepdims=True)
        acc[job] = acc[job] * shrink + lax.dot_general(
            v, weights.astype(jnp.bfloat16), TN, preferred_element_type=jnp.float32
        )

    total = BLOCKS * groups
    score(0, even)

    @pl.loop(0, (total - 1) // 2)
    def _(i):
        score(2 * i + 1, odd)
        finish(2 * i, even)
        score(2 * i + 2, even)
        finish(2 * i + 1, odd)

    if total % 2:
        finish(total - 1, even)
    else:
        score(total - 1, odd)
        finish(total - 2, even)
        finish(total - 1, odd)
    if final:
        for group in range(groups):
            for job in range(2):
                for h in range(0, 4, 2):
                    cols = slice(h * HALF, (h + 2) * HALF)
                    done = acc[2 * group + job, :, cols] / stat[2 * group + job, 1:2, cols]
                    pair = done.T.astype(jnp.bfloat16)
                    at = (group * 4 + h) * HEAD
                    outs[job][:HALF, at : at + HEAD] = pair[:HALF]
                    outs[job][:HALF, at + HEAD : at + 2 * HEAD] = pair[HALF:]
        if outs[1].shape[0] > HALF:
            spare = outs[1].shape[0] - HALF
            outs[1][HALF:, :] = jnp.zeros((spare, outs[1].shape[1]), jnp.bfloat16)


def _attend(meta, kv, queries, states=(), groups=1, part=0, spare=0):
    final = bool(states)
    sort = len(kv[0].shape) == 3
    ordered = [(TILES * HALF, HEAD)] * (2 if sort else 0)
    state_shape = [(2 * groups, 8, LANES), (2 * groups, HEAD, LANES)]
    if final:
        out_shape = [
            jax.ShapeDtypeStruct((HALF, groups * 4 * HEAD), jnp.bfloat16),
            jax.ShapeDtypeStruct((HALF + spare, groups * 4 * HEAD), jnp.bfloat16),
        ]
    else:
        out_shape = [jax.ShapeDtypeStruct(shape, jnp.float32) for shape in state_shape]
    if final:
        out_shape += [jax.ShapeDtypeStruct(shape, jnp.bfloat16) for shape in ordered]
        ordered = []
    near = [*kv, queries, *states]
    out = pl.pallas_call(
        functools.partial(_attend_body, len(kv), sort, not states, final, part),
        out_shape=out_shape,
        in_specs=[SMEM] + [VMEM] * len(near),
        out_specs=[VMEM] * len(out_shape),
        scratch_shapes=[pltpu.VMEM(shape, jnp.bfloat16) for shape in ordered]
        + [
            pltpu.VMEM((2 * groups, LANES, HEAD), jnp.bfloat16),
            pltpu.VMEM((SPAN + 8, LANES), jnp.float32),
            pltpu.VMEM((SPAN + 8, LANES), jnp.float32),
            pltpu.VMEM((8, LANES), jnp.int32),
        ]
        + ([pltpu.VMEM(shape, jnp.float32) for shape in state_shape] if final else []),
        compiler_params=pltpu.CompilerParams(vmem_limit_bytes=28 * 1024 * 1024),
        cost_estimate=pl.CostEstimate(
            flops=4 * groups * BLOCKS * SPAN * HEAD * LANES,
            bytes_accessed=4 * 1024 * 1024,
            transcendentals=groups * BLOCKS * SPAN * LANES,
        ),
        name="attend",
    )(meta, *near)
    return out[:2], out[2:]


def _blocks(early_count, early_own, late_count, late_own):
    early_blocks = early_count // 4 + 1 if early_own else (early_count + 3) // 4
    entries = []
    for b in range(BLOCKS):
        is_late = (b >= early_blocks).astype(jnp.int32)
        tile = 4 * (b - is_late * early_blocks)
        count = jnp.where(is_late == 1, late_count, early_count)
        own = jnp.where(is_late == 1, int(late_own), int(early_own))
        entries += [is_late, jnp.minimum(tile, TILES - 4), (count - tile) * HALF, own]
    return jnp.stack(entries).astype(jnp.int32)


def _angles(positions):
    half = HEAD // 2
    freq = rope_base ** (-2.0 * jnp.arange(half, dtype=jnp.float32) / HEAD)
    phase = positions.astype(jnp.float32)[:, None] * freq[None, :]
    cosine, sine = jnp.cos(phase), jnp.sin(phase)
    return jnp.concatenate([cosine, cosine], axis=1), jnp.concatenate([-sine, sine], axis=1)


def _after(value, *earlier):
    return lax.optimization_barrier((value, *earlier))[0]


def local(hidden, w_query, w_key, w_value, q_bias, k_bias, v_bias):
    seq = lax.axis_index("seq")
    tp = lax.axis_index("tp")
    y, x_hi, core = seq // 4, seq // 2 % 2, seq % 2
    x_lo, z = tp // 4, tp % 4
    weights = [w_query, w_key, w_value]
    q_bias, k_bias, v_bias = q_bias[None], k_bias[None], v_bias[None]

    def feature(lo, dz):
        return lo * 4 + (z + dz) % 4

    def tile_seq(dy, dx, dc):
        return ((y + dy) % 4 * 2 + (x_hi ^ dx)) * 2 + (core ^ dc)

    def places(dc):
        seqs = [tile_seq(dy, dx, dc) for dx in (0, 1) for dy in (0, -1, 1, 2)]
        return jnp.stack([p for s in seqs for p in (s, 15 - s)]).astype(jnp.int32)

    far_lo = 1 - x_lo

    def ints(*values):
        return jnp.stack(values).astype(jnp.int32)

    w_query, w_key, w_value = weights = [
        pltpu.with_memory_space_constraint(w, pltpu.HBM) for w in weights
    ]
    early, late = _stitch(
        [(HALF, DEPTH)] * 2, [(0, 0, HALF, 0, 0), (0, HALF, HALF, 1, 0)], hidden
    )
    side = _send(early, x_near)
    up, down = _send(early, z_up), _send(early, z_down)
    late = _send(late, mirror_cross)
    row = jnp.arange(HALF, dtype=jnp.int32)
    rope = _angles(jnp.concatenate([seq * ROWS + row, (31 - 2 * seq) * HALF + row]))
    up, *rope = lax.optimization_barrier((up, *rope))

    to_up, to_down = _stitch(
        [(HALF, DEPTH)] * 2,
        [
            (0, 0, PART, 0, 0),
            (2, 0, PART, 0, PART),
            (1, PART, PART, 1, 0),
            (2, 0, PART, 1, PART),
        ],
        up,
        down,
        side,
    )
    from_down, from_up = _send(to_up, z_up), _send(to_down, z_down)
    late_side = _send(late, x_near)

    across, both = _stitch(
        [(ROWS, DEPTH)] * 2,
        [
            (2, 0, PART, 0, 0),
            (3, 0, PART, 0, PART),
            (0, PART, PART, 0, HALF),
            (1, PART, PART, 0, HALF + PART),
            (4, 0, HALF, 1, 0),
            (5, 0, HALF, 1, HALF),
        ],
        up,
        down,
        from_down,
        from_up,
        late,
        late_side,
    )
    late_up, late_down = _send(both, z_up), _send(both, z_down)
    got = _send(across, x_near)
    acc = _project(
        ints(feature(x_lo, 0), feature(far_lo, 0)),
        [_after(early, across), late_side, side, late],
        ([(0, 0, HALF), (1, 0, HALF)], [(2, 0, HALF), (3, 0, HALF)]),
        weights,
    )

    to_up, to_down = _stitch(
        [(HALF, DEPTH)] * 2,
        [
            (0, 0, PART, 0, 0),
            (0, HALF, PART, 0, PART),
            (1, PART, PART, 1, 0),
            (1, HALF + PART, PART, 1, PART),
        ],
        _after(late_up, acc),
        late_down,
    )
    late_from_down, late_from_up = _send(to_up, z_up), _send(to_down, z_down)
    acc = _project(
        ints(feature(x_lo, -1), feature(x_lo, 1), feature(far_lo, -1), feature(far_lo, 1)),
        [_after(up, to_up), down, from_down, from_up, got, late_up, late_down],
        (
            [(0, 0, HALF), (5, HALF, HALF)],
            [(1, 0, HALF), (6, HALF, HALF)],
            [(2, PART, PART), (4, HALF, PART), (5, 0, HALF)],
            [(3, PART, PART), (4, HALF + PART, PART), (6, 0, HALF)],
        ),
        weights,
        acc,
    )
    which = ints(feature(far_lo, 2), feature(x_lo, 2))
    arrays = [got, from_down, from_up, late_from_down, late_from_up]
    pieces = (
        [(0, 0, HALF), (3, 0, PART), (4, 0, PART)],
        [(1, 0, PART), (2, 0, PART), (3, PART, PART), (4, PART, PART)],
    )
    kv = _last_kv(which, arrays, pieces, w_key, w_value, acc, k_bias, v_bias, *rope)
    far_kv = _send(kv, x_far)
    near_kv = [kv, _send(kv, y_up), _send(kv, y_down), _send(kv, y_far)]
    queries = _last_q(which, [_after(got, kv), *arrays[1:]], pieces, w_query, acc, q_bias, *rope)
    far_kv = _after(far_kv, queries)
    far_kv = [far_kv, _send(far_kv, y_up), _send(far_kv, y_down), _send(far_kv, y_far)]
    near_tiles = _stack_tiles(near_kv)
    far_tiles = _stack_tiles(far_kv)
    other_kv = [_send(near_tiles, other_core), _send(far_tiles, other_core)]

    meta = jnp.concatenate([places(0), _blocks(seq, True, 15 - seq, True)])
    other_meta = jnp.concatenate([places(1), _blocks(seq, False, 16 - seq, False)])
    states, _ = _attend(_after(meta, far_tiles), [near_tiles, far_tiles], queries, groups=2)
    (early_low, late_low), ordered = _attend(
        other_meta, other_kv, queries, states, part=0, spare=16
    )
    back_low = _send(late_low, mirror)
    (early_high, late_high), _ = _attend(other_meta, ordered, queries, states, part=1)
    back_high = _send(late_high, mirror)
    return jnp.concatenate(
        [
            jnp.concatenate([early_low, early_high], axis=1),
            jnp.concatenate([back_low[:HALF], back_high], axis=1),
        ],
        axis=0,
    )


def solution(mesh):
    return jax.shard_map(
        local,
        mesh=mesh,
        in_specs=(
            P("seq", "tp"),
            P(None, "tp"),
            P(None, "tp"),
            P(None, "tp"),
            P("tp"),
            P("tp"),
            P("tp"),
        ),
        out_specs=P("seq", "tp"),
        check_vma=False,
    )
```

```python
import functools
import math

import jax
import jax.numpy as jnp
from jax import lax
from jax.experimental import pallas as pl
from jax.experimental.pallas import tpu as pltpu
from jax.sharding import PartitionSpec as P

HEAD = 128
GROUP = 8
HALF = 192
PART = HALF // 2
ROWS = 2 * HALF
DEPTH = 1024
QCOLS = GROUP * HEAD
ALLCOLS = QCOLS + 2 * HEAD
LANES = 4 * HALF
TILES = 16
SPAN = 4 * HALF
BLOCKS = 5
WHOLE = 3
AXES = ("seq", "tp")
VMEM_LIMIT = 48 * 1024 * 1024
EXP2_SCALE = float(HEAD) ** (-0.5) * math.log2(math.e)
NT = (((1,), (1,)), ((), ()))
TN = (((0,), (0,)), ((), ()))
rope_base = 1000000.0


def _place(flat):
    seq, tp = divmod(flat, 8)
    x_lo, z = divmod(tp, 4)
    y, rest = divmod(seq, 4)
    x_hi, core = divmod(rest, 2)
    return x_hi * 2 + x_lo, y, z, core


def _index(x, y, z, core):
    x_hi, x_lo = divmod(x % 4, 2)
    return (((y % 4) * 2 + x_hi) * 2 + core) * 8 + x_lo * 4 + z % 4


def _send(value, move):
    pairs = [(i, _index(*move(*_place(i)))) for i in range(128)]
    return lax.ppermute(value, AXES, pairs)


def z_up(x, y, z, c):
    return x, y, z + 1, c


def z_down(x, y, z, c):
    return x, y, z - 1, c


def x_near(x, y, z, c):
    return x ^ 1, y, z, c


def x_far(x, y, z, c):
    return x ^ 2, y, z, c


def y_up(x, y, z, c):
    return x, y + 1, z, c


def y_down(x, y, z, c):
    return x, y - 1, z, c


def y_far(x, y, z, c):
    return x, y + 2, z, c


def other_core(x, y, z, c):
    return x, y, z, 1 - c


def mirror_cross(x, y, z, c):
    return 3 - x, 3 - y, z, 1 - c


def mirror(x, y, z, c):
    return x ^ 2, 3 - y, z, 1 - c


VMEM = pl.BlockSpec(memory_space=pltpu.VMEM)
HBM = pl.BlockSpec(memory_space=pl.ANY)
SMEM = pl.BlockSpec(memory_space=pltpu.SMEM)


def _in_hbm(value):
    return pltpu.with_memory_space_constraint(value, pltpu.HBM)


def _block(index):
    return pl.ds(pl.multiple_of(index * DEPTH, DEPTH), DEPTH)


def _piece_loads(parts, pieces, x, sem):
    loads = []
    for i, piece in enumerate(pieces):
        at = 0
        loads.append([])
        for k, (operand, start, size) in enumerate(piece):
            loads[-1].append(
                pltpu.make_async_copy(
                    parts[operand].at[pl.ds(start, size)],
                    x.at[i, pl.ds(at, size)],
                    sem.at[i, k],
                )
            )
            at += size
    return loads


def _weight_loads(slices, n, far, near, sem):
    return [
        [
            pltpu.make_async_copy(src.at[_block(slices[i]), :], dst.at[i], sem.at[i, j])
            for j, (src, dst) in enumerate(zip(far, near))
        ]
        for i in range(n)
    ]


def _start(group):
    for copy in group:
        copy.start()


def _wait(group):
    for copy in group:
        copy.wait()


def _proj_body(arrays, pieces, started, slices, *refs):
    n = len(pieces)
    parts, far = refs[:arrays], refs[arrays : arrays + 3]
    refs = refs[arrays + 3 :]
    acc_in, refs = (refs[0], refs[1:]) if started else (None, refs)
    acc, x, near, (x_sem, w_sem, acc_sem) = refs[0], refs[1], refs[2:5], refs[5:8]
    x_loads = _piece_loads(parts, pieces, x, x_sem)
    w_loads = _weight_loads(slices, n, far, near, w_sem)
    for i in range(min(2, n)):
        _start(x_loads[i])
        _start(w_loads[i])
    if started:
        acc_load = pltpu.make_async_copy(acc_in, acc, acc_sem)
        acc_load.start()
    spans = (slice(0, QCOLS), slice(QCOLS, QCOLS + HEAD), slice(QCOLS + HEAD, ALLCOLS))
    for i in range(n):
        _wait(x_loads[i])
        _wait(w_loads[i])
        if i + 2 < n:
            _start(x_loads[i + 2])
            _start(w_loads[i + 2])
        if started and i == 0:
            acc_load.wait()
        for w, cols in zip(near, spans):
            term = jnp.dot(x[i], w[i], preferred_element_type=jnp.float32)
            if i or started:
                acc[:, cols] += term
            else:
                acc[:, cols] = term


def _project(slices, arrays, pieces, weights, acc=None):
    n = len(pieces)
    started = [] if acc is None else [acc]
    return pl.pallas_call(
        functools.partial(_proj_body, len(arrays), pieces, acc is not None),
        out_shape=jax.ShapeDtypeStruct((ROWS, ALLCOLS), jnp.float32),
        in_specs=[SMEM] + [HBM] * (len(arrays) + 3 + len(started)),
        out_specs=VMEM,
        scratch_shapes=[
            pltpu.VMEM((n, ROWS, DEPTH), jnp.bfloat16),
            pltpu.VMEM((n, DEPTH, QCOLS), jnp.bfloat16),
            pltpu.VMEM((n, DEPTH, HEAD), jnp.bfloat16),
            pltpu.VMEM((n, DEPTH, HEAD), jnp.bfloat16),
            pltpu.SemaphoreType.DMA((n, 3)),
            pltpu.SemaphoreType.DMA((n, 3)),
            pltpu.SemaphoreType.DMA,
        ],
        compiler_params=pltpu.CompilerParams(vmem_limit_bytes=28 * 1024 * 1024),
        cost_estimate=pl.CostEstimate(
            flops=2 * n * ROWS * DEPTH * ALLCOLS,
            bytes_accessed=2 * n * DEPTH * ALLCOLS,
            transcendentals=0,
        ),
        name="project",
    )(slices, *map(_in_hbm, arrays), *weights, *started)


def _rotate(u, cosine, sine):
    return u * cosine[...] + pltpu.roll(u, HEAD // 2, 1) * sine[...]


def _last_kv_body(arrays, pieces, slices, *refs):
    n = len(pieces)
    parts, (w_k, w_v), refs = refs[:arrays], refs[arrays : arrays + 2], refs[arrays + 2 :]
    given, (k_bias, v_bias, cosine, sine, out), refs = refs[0], refs[1:6], refs[6:]
    x, near_k, near_v, acc, x_sem, w_sem, sem = refs
    x_loads = _piece_loads(parts, pieces, x, x_sem)
    w_loads = _weight_loads(slices, n, (w_k, w_v), (near_k, near_v), w_sem)
    others = [pltpu.make_async_copy(given.at[:, pl.ds(QCOLS, 2 * HEAD)], acc, sem)]
    for group in x_loads + w_loads + [others]:
        _start(group)
    k = v = 0
    for i in range(n):
        _wait(x_loads[i])
        _wait(w_loads[i])
        k += jnp.dot(x[i], near_k[i], preferred_element_type=jnp.float32)
        v += jnp.dot(x[i], near_v[i], preferred_element_type=jnp.float32)
    _wait(others)
    k += acc[:, :HEAD]
    v += acc[:, HEAD:]
    k = _rotate(k + k_bias[...], cosine, sine).astype(jnp.bfloat16)
    v = (v + v_bias[...]).astype(jnp.bfloat16)
    for half in range(2):
        rows = slice(half * HALF, (half + 1) * HALF)
        out[half, :, :HEAD] = k[rows]
        out[half, :, HEAD:] = v[rows]


def _last_kv(slices, arrays, pieces, w_k, w_v, acc, k_bias, v_bias, cosine, sine):
    n = len(pieces)
    return pl.pallas_call(
        functools.partial(_last_kv_body, len(arrays), pieces),
        out_shape=jax.ShapeDtypeStruct((2, HALF, 2 * HEAD), jnp.bfloat16),
        in_specs=[SMEM] + [HBM] * (len(arrays) + 3) + [VMEM] * 4,
        out_specs=VMEM,
        scratch_shapes=[
            pltpu.VMEM((n, ROWS, DEPTH), jnp.bfloat16),
            pltpu.VMEM((n, DEPTH, HEAD), jnp.bfloat16),
            pltpu.VMEM((n, DEPTH, HEAD), jnp.bfloat16),
            pltpu.VMEM((ROWS, 2 * HEAD), jnp.float32),
            pltpu.SemaphoreType.DMA((n, 4)),
            pltpu.SemaphoreType.DMA((n, 2)),
            pltpu.SemaphoreType.DMA,
        ],
        compiler_params=pltpu.CompilerParams(vmem_limit_bytes=12 * 1024 * 1024),
        cost_estimate=pl.CostEstimate(
            flops=4 * n * ROWS * DEPTH * HEAD,
            bytes_accessed=4 * n * DEPTH * HEAD,
            transcendentals=0,
        ),
        name="last_kv",
    )(slices, *map(_in_hbm, arrays), w_k, w_v, acc, k_bias, v_bias, cosine, sine)


def _last_q_body(arrays, pieces, slices, *refs):
    n = len(pieces)
    parts, w_q, refs = refs[:arrays], refs[arrays], refs[arrays + 1 :]
    given, (q_bias, cosine, sine, out), refs = refs[0], refs[1:5], refs[5:]
    x, near, acc, x_sem, w_sem, sem = refs
    x_loads = _piece_loads(parts, pieces, x, x_sem)
    w_loads = _weight_loads(slices, n, (w_q,), (near,), w_sem)
    others = [pltpu.make_async_copy(given.at[:, pl.ds(0, QCOLS)], acc, sem)]
    _start(x_loads[0])
    _start(w_loads[0])
    _start(others)
    for i in range(1, n):
        _start(x_loads[i])
        _start(w_loads[i])
    for i in range(n):
        _wait(x_loads[i])
        _wait(w_loads[i])
        if i == 0:
            _wait(others)
        if i < n - 1:
            acc[...] += jnp.dot(x[i], near[i], preferred_element_type=jnp.float32)
    for i in range(0, GROUP, 2):
        both = slice(i * HEAD, (i + 2) * HEAD)
        q = acc[:, both] + jnp.dot(x[n - 1], near[n - 1, :, both], preferred_element_type=jnp.float32)
        q += q_bias[:, both]
        for j in range(2):
            cols = slice((i + j) * HEAD, (i + j + 1) * HEAD)
            u = q[:, j * HEAD : (j + 1) * HEAD]
            out[:, cols] = _rotate(u, cosine, sine).astype(jnp.bfloat16)


def _last_q(slices, arrays, pieces, w_q, acc, q_bias, cosine, sine):
    n = len(pieces)
    return pl.pallas_call(
        functools.partial(_last_q_body, len(arrays), pieces),
        out_shape=jax.ShapeDtypeStruct((ROWS, QCOLS), jnp.bfloat16),
        in_specs=[SMEM] + [HBM] * (len(arrays) + 2) + [VMEM] * 3,
        out_specs=VMEM,
        scratch_shapes=[
            pltpu.VMEM((n, ROWS, DEPTH), jnp.bfloat16),
            pltpu.VMEM((n, DEPTH, QCOLS), jnp.bfloat16),
            pltpu.VMEM((ROWS, QCOLS), jnp.float32),
            pltpu.SemaphoreType.DMA((n, 4)),
            pltpu.SemaphoreType.DMA((n, 1)),
            pltpu.SemaphoreType.DMA,
        ],
        compiler_params=pltpu.CompilerParams(vmem_limit_bytes=20 * 1024 * 1024),
        cost_estimate=pl.CostEstimate(
            flops=2 * n * ROWS * DEPTH * QCOLS,
            bytes_accessed=2 * n * DEPTH * QCOLS,
            transcendentals=0,
        ),
        name="last_q",
    )(slices, *map(_in_hbm, arrays), w_q, acc, q_bias, cosine, sine)


def _stitch(shapes, moves, *operands):
    def body(*refs):
        sem = refs[-1]
        copies = []
        for i, (operand, start, size, o, at) in enumerate(moves):
            src, out = refs[operand], refs[len(operands) + o]
            if len(src.shape) < len(out.shape):
                copies.append(pltpu.make_async_copy(src, out.at[at], sem.at[i]))
            else:
                copies.append(
                    pltpu.make_async_copy(
                        src.at[pl.ds(start, size)], out.at[pl.ds(at, size)], sem.at[i]
                    )
                )
        _start(copies)
        _wait(copies)

    return pl.pallas_call(
        body,
        out_shape=[jax.ShapeDtypeStruct(shape, jnp.bfloat16) for shape in shapes],
        in_specs=[HBM] * len(operands),
        out_specs=[VMEM] * len(shapes),
        scratch_shapes=[pltpu.SemaphoreType.DMA((len(moves),))],
        compiler_params=pltpu.CompilerParams(vmem_limit_bytes=4 * 1024 * 1024),
        name="stitch",
    )(*map(_in_hbm, operands))


def _stack_tiles(arrays):
    moves = [(i, 0, 2, 0, 2 * i) for i in range(4)]
    return _stitch([(8, HALF, 2 * HEAD)], moves, *arrays)[0]


def _attend_body(given, sort, first, final, part, meta, *refs):
    kv, refs = refs[:given], refs[given:]
    queries, refs = refs[0], refs[1:]
    states_in, refs = ((), refs) if first else (refs[:2], refs[2:])
    outs, refs = refs[:2], refs[2:]
    keys, values = refs[:2] if sort else kv
    rows, even, odd, place = refs[2 if sort else 0 :][:4]
    stat, acc = refs[-2:] if final else outs
    groups = acc.shape[0] // 2
    for group in range(groups):
        for job in range(2):
            for h in range(4):
                col = (part * 4 + group * 4 + h) * HEAD
                rows[2 * group + job, h * HALF : (h + 1) * HALF, :] = queries[
                    job * HALF : (job + 1) * HALF, col : col + HEAD
                ]
    for h in range(4):
        place[0:1, h * HALF : (h + 1) * HALF] = lax.broadcasted_iota(jnp.int32, (1, HALF), 1) + 1
    if first:
        stat[:, 0:1, :] = jnp.full((2 * groups, 1, LANES), -1e30, jnp.float32)
        stat[:, 1:8, :] = jnp.zeros((2 * groups, 7, LANES), jnp.float32)
        acc[...] = jnp.zeros_like(acc)
    else:
        stat[...] = states_in[0][2 * part : 2 * part + 2 * groups]
        acc[...] = states_in[1][2 * part : 2 * part + 2 * groups]
    tiles = [array.at[i] for array in kv for i in range(array.shape[0])] if sort else []
    for i, tile in enumerate(tiles):
        start = pl.multiple_of(meta[i] * HALF, HALF)
        keys[pl.ds(start, HALF), :] = tile[:, :HEAD]
        values[pl.ds(start, HALF), :] = tile[:, HEAD:]

    def entry(block, i):
        return meta[TILES + 4 * block[1] + i]

    def job_of(block):
        return entry(block, 0) + 2 * block[0]

    def score(block, out, mask):
        start = pl.multiple_of(entry(block, 1) * HALF, 4 * HALF)
        k = keys[pl.ds(start, SPAN), :]
        scores = lax.dot_general(k, rows[job_of(block)], NT, preferred_element_type=jnp.float32)
        if mask:
            seen = entry(block, 2) + entry(block, 3) * place[0:1, :]
            key = lax.broadcasted_iota(jnp.int32, (SPAN, LANES), 0)
            scores = jnp.where(key < seen, scores, -jnp.inf)
        out[0:SPAN, :] = scores
        out[SPAN : SPAN + 1, :] = jnp.max(scores, axis=0, keepdims=True)

    def finish(block, src):
        job = job_of(block)
        start = pl.multiple_of(entry(block, 1) * HALF, 4 * HALF)
        v = values[pl.ds(start, SPAN), :]
        old = stat[job, 0:1, :]
        new = jnp.maximum(old, src[SPAN : SPAN + 1, :])
        weights = jnp.exp2((src[0:SPAN, :] - new) * EXP2_SCALE)
        shrink = jnp.exp2((old - new) * EXP2_SCALE)
        stat[job, 0:1, :] = new
        stat[job, 1:2, :] = stat[job, 1:2, :] * shrink + jnp.sum(weights, axis=0, keepdims=True)
        acc[job] = acc[job] * shrink + lax.dot_general(
            v, weights.astype(jnp.bfloat16), TN, preferred_element_type=jnp.float32
        )

    def whole(b):
        return lax.div(b, WHOLE), lax.rem(b, WHOLE)

    last = [(g, p) for g in range(groups) for p in range(WHOLE, BLOCKS)]
    loops = (WHOLE * groups - 1) // 2
    score((0, 0), even, False)

    @pl.loop(0, loops)
    def _(i):
        score(whole(2 * i + 1), odd, False)
        finish(whole(2 * i), even)
        score(whole(2 * i + 2), even, False)
        finish(whole(2 * i + 1), odd)

    rest = [(b // WHOLE, b % WHOLE) for b in range(2 * loops, WHOLE * groups)]
    steps = [(block, False) for block in rest] + [(block, True) for block in last]
    buffers = (even, odd)
    for i, (block, _) in enumerate(steps):
        if i + 1 < len(steps):
            score(steps[i + 1][0], buffers[(i + 1) % 2], steps[i + 1][1])
        finish(block, buffers[i % 2])
    if final:
        for group in range(groups):
            for job in range(2):
                for h in range(0, 4, 2):
                    cols = slice(h * HALF, (h + 2) * HALF)
                    done = acc[2 * group + job, :, cols] / stat[2 * group + job, 1:2, cols]
                    pair = done.T.astype(jnp.bfloat16)
                    at = (group * 4 + h) * HEAD
                    outs[job][:HALF, at : at + HEAD] = pair[:HALF]
                    outs[job][:HALF, at + HEAD : at + 2 * HEAD] = pair[HALF:]
        if outs[1].shape[0] > HALF:
            spare = outs[1].shape[0] - HALF
            outs[1][HALF:, :] = jnp.zeros((spare, outs[1].shape[1]), jnp.bfloat16)


def _attend(meta, kv, queries, states=(), groups=1, part=0, spare=0):
    final = bool(states)
    sort = len(kv[0].shape) == 3
    ordered = [(TILES * HALF, HEAD)] * (2 if sort else 0)
    state_shape = [(2 * groups, 8, LANES), (2 * groups, HEAD, LANES)]
    if final:
        out_shape = [
            jax.ShapeDtypeStruct((HALF, groups * 4 * HEAD), jnp.bfloat16),
            jax.ShapeDtypeStruct((HALF + spare, groups * 4 * HEAD), jnp.bfloat16),
        ]
    else:
        out_shape = [jax.ShapeDtypeStruct(shape, jnp.float32) for shape in state_shape]
    if final:
        out_shape += [jax.ShapeDtypeStruct(shape, jnp.bfloat16) for shape in ordered]
        ordered = []
    near = [*kv, queries, *states]
    out = pl.pallas_call(
        functools.partial(_attend_body, len(kv), sort, not states, final, part),
        out_shape=out_shape,
        in_specs=[SMEM] + [VMEM] * len(near),
        out_specs=[VMEM] * len(out_shape),
        scratch_shapes=[pltpu.VMEM(shape, jnp.bfloat16) for shape in ordered]
        + [
            pltpu.VMEM((2 * groups, LANES, HEAD), jnp.bfloat16),
            pltpu.VMEM((SPAN + 8, LANES), jnp.float32),
            pltpu.VMEM((SPAN + 8, LANES), jnp.float32),
            pltpu.VMEM((8, LANES), jnp.int32),
        ]
        + ([pltpu.VMEM(shape, jnp.float32) for shape in state_shape] if final else []),
        compiler_params=pltpu.CompilerParams(vmem_limit_bytes=28 * 1024 * 1024),
        cost_estimate=pl.CostEstimate(
            flops=4 * groups * BLOCKS * SPAN * HEAD * LANES,
            bytes_accessed=4 * 1024 * 1024,
            transcendentals=groups * BLOCKS * SPAN * LANES,
        ),
        name="attend",
    )(meta, *near)
    return out[:2], out[2:]


def _blocks(early_count, late_count, own):
    early_whole, late_whole = early_count // 4, late_count // 4
    four = early_whole + late_whole == 4
    blocks = []
    for b in range(WHOLE):
        late = (b >= early_whole).astype(jnp.int32)
        blocks.append((late, b - late * early_whole))
    blocks.append((four.astype(jnp.int32), jnp.where(four, late_whole - 1, early_whole)))
    blocks.append((1, late_whole))
    entries = []
    for late, block in blocks:
        count = jnp.where(late == 1, late_count, early_count)
        entries += [late, jnp.minimum(4 * block, TILES - 4), (count - 4 * block) * HALF, int(own)]
    return jnp.stack([jnp.asarray(e, jnp.int32) for e in entries])


def _angles(positions):
    half = HEAD // 2
    freq = rope_base ** (-2.0 * jnp.arange(half, dtype=jnp.float32) / HEAD)
    phase = positions.astype(jnp.float32)[:, None] * freq[None, :]
    cosine, sine = jnp.cos(phase), jnp.sin(phase)
    return jnp.concatenate([cosine, cosine], axis=1), jnp.concatenate([-sine, sine], axis=1)


def _after(value, *earlier):
    return lax.optimization_barrier((value, *earlier))[0]


def local(hidden, w_query, w_key, w_value, q_bias, k_bias, v_bias):
    seq = lax.axis_index("seq")
    tp = lax.axis_index("tp")
    y, x_hi, core = seq // 4, seq // 2 % 2, seq % 2
    x_lo, z = tp // 4, tp % 4
    weights = [w_query, w_key, w_value]
    q_bias, k_bias, v_bias = q_bias[None], k_bias[None], v_bias[None]

    def feature(lo, dz):
        return lo * 4 + (z + dz) % 4

    def tile_seq(dy, dx, dc):
        return ((y + dy) % 4 * 2 + (x_hi ^ dx)) * 2 + (core ^ dc)

    def places(dc):
        seqs = [tile_seq(dy, dx, dc) for dx in (0, 1) for dy in (0, -1, 1, 2)]
        return jnp.stack([p for s in seqs for p in (s, 15 - s)]).astype(jnp.int32)

    far_lo = 1 - x_lo

    def ints(*values):
        return jnp.stack(values).astype(jnp.int32)

    w_query, w_key, w_value = weights = [
        pltpu.with_memory_space_constraint(w, pltpu.HBM) for w in weights
    ]
    early, late = _stitch(
        [(HALF, DEPTH)] * 2, [(0, 0, HALF, 0, 0), (0, HALF, HALF, 1, 0)], hidden
    )
    side = _send(early, x_near)
    up, down = _send(early, z_up), _send(early, z_down)
    late = _send(late, mirror_cross)
    row = jnp.arange(HALF, dtype=jnp.int32)
    rope = _angles(jnp.concatenate([seq * ROWS + row, (31 - 2 * seq) * HALF + row]))
    up, *rope = lax.optimization_barrier((up, *rope))

    to_up, to_down = _stitch(
        [(HALF, DEPTH)] * 2,
        [
            (0, 0, PART, 0, 0),
            (2, 0, PART, 0, PART),
            (1, PART, PART, 1, 0),
            (2, 0, PART, 1, PART),
        ],
        up,
        down,
        side,
    )
    from_down, from_up = _send(to_up, z_up), _send(to_down, z_down)
    late_side = _send(late, x_near)

    across, both = _stitch(
        [(ROWS, DEPTH)] * 2,
        [
            (2, 0, PART, 0, 0),
            (3, 0, PART, 0, PART),
            (0, PART, PART, 0, HALF),
            (1, PART, PART, 0, HALF + PART),
            (4, 0, HALF, 1, 0),
            (5, 0, HALF, 1, HALF),
        ],
        up,
        down,
        from_down,
        from_up,
        late,
        late_side,
    )
    late_up, late_down = _send(both, z_up), _send(both, z_down)
    got = _send(across, x_near)
    acc = _project(
        ints(feature(x_lo, 0), feature(far_lo, 0)),
        [_after(early, across), late_side, side, late],
        ([(0, 0, HALF), (1, 0, HALF)], [(2, 0, HALF), (3, 0, HALF)]),
        weights,
    )

    to_up, to_down = _stitch(
        [(HALF, DEPTH)] * 2,
        [
            (0, 0, PART, 0, 0),
            (0, HALF, PART, 0, PART),
            (1, PART, PART, 1, 0),
            (1, HALF + PART, PART, 1, PART),
        ],
        _after(late_up, acc),
        late_down,
    )
    late_from_down, late_from_up = _send(to_up, z_up), _send(to_down, z_down)
    acc = _project(
        ints(feature(x_lo, -1), feature(x_lo, 1), feature(far_lo, -1), feature(far_lo, 1)),
        [_after(up, to_up), down, from_down, from_up, got, late_up, late_down],
        (
            [(0, 0, HALF), (5, HALF, HALF)],
            [(1, 0, HALF), (6, HALF, HALF)],
            [(2, PART, PART), (4, HALF, PART), (5, 0, HALF)],
            [(3, PART, PART), (4, HALF + PART, PART), (6, 0, HALF)],
        ),
        weights,
        acc,
    )
    which = ints(feature(far_lo, 2), feature(x_lo, 2))
    arrays = [got, from_down, from_up, late_from_down, late_from_up]
    pieces = (
        [(0, 0, HALF), (3, 0, PART), (4, 0, PART)],
        [(1, 0, PART), (2, 0, PART), (3, PART, PART), (4, PART, PART)],
    )
    kv = _last_kv(which, arrays, pieces, w_key, w_value, acc, k_bias, v_bias, *rope)
    far_kv = _send(kv, x_far)
    near_kv = [kv, _send(kv, y_up), _send(kv, y_down), _send(kv, y_far)]
    queries = _last_q(which, [_after(got, kv), *arrays[1:]], pieces, w_query, acc, q_bias, *rope)
    far_kv = _after(far_kv, queries)
    far_kv = [far_kv, _send(far_kv, y_up), _send(far_kv, y_down), _send(far_kv, y_far)]
    near_tiles = _stack_tiles(near_kv)
    far_tiles = _stack_tiles(far_kv)
    other_kv = [_send(near_tiles, other_core), _send(far_tiles, other_core)]

    meta = jnp.concatenate([places(0), _blocks(seq, 15 - seq, True)])
    other_meta = jnp.concatenate([places(1), _blocks(seq, 16 - seq, False)])
    states, _ = _attend(_after(meta, far_tiles), [near_tiles, far_tiles], queries, groups=2)
    (early_low, late_low), ordered = _attend(
        other_meta, other_kv, queries, states, part=0, spare=16
    )
    back_low = _send(late_low, mirror)
    (early_high, late_high), _ = _attend(other_meta, ordered, queries, states, part=1)
    back_high = _send(late_high, mirror)
    return jnp.concatenate(
        [
            jnp.concatenate([early_low, early_high], axis=1),
            jnp.concatenate([back_low[:HALF], back_high], axis=1),
        ],
        axis=0,
    )


def solution(mesh):
    return jax.shard_map(
        local,
        mesh=mesh,
        in_specs=(
            P("seq", "tp"),
            P(None, "tp"),
            P(None, "tp"),
            P(None, "tp"),
            P("tp"),
            P("tp"),
            P("tp"),
        ),
        out_specs=P("seq", "tp"),
        check_vma=False,
    )
```

```python
import functools
import math

import jax
import jax.numpy as jnp
from jax import lax
from jax.experimental import pallas as pl
from jax.experimental.pallas import tpu as pltpu
from jax.sharding import PartitionSpec as P

HEAD = 128
GROUP = 8
HALF = 192
PART = HALF // 2
ROWS = 2 * HALF
DEPTH = 1024
QCOLS = GROUP * HEAD
ALLCOLS = QCOLS + 2 * HEAD
LANES = 4 * HALF
SPAN = 4 * HALF
BLOCKS = 5
WHOLE = 3
AXES = ("seq", "tp")
VMEM_LIMIT = 48 * 1024 * 1024
EXP2_SCALE = float(HEAD) ** (-0.5) * math.log2(math.e)
NT = (((1,), (1,)), ((), ()))
TN = (((0,), (0,)), ((), ()))
rope_base = 1000000.0


def _place(flat):
    seq, tp = divmod(flat, 8)
    x_lo, z = divmod(tp, 4)
    y, rest = divmod(seq, 4)
    x_hi, core = divmod(rest, 2)
    return x_hi * 2 + x_lo, y, z, core


def _index(x, y, z, core):
    x_hi, x_lo = divmod(x % 4, 2)
    return (((y % 4) * 2 + x_hi) * 2 + core) * 8 + x_lo * 4 + z % 4


def _send(value, move):
    pairs = [(i, _index(*move(*_place(i)))) for i in range(128)]
    return lax.ppermute(value, AXES, pairs)


def z_up(x, y, z, c):
    return x, y, z + 1, c


def z_down(x, y, z, c):
    return x, y, z - 1, c


def x_near(x, y, z, c):
    return x ^ 1, y, z, c


def x_far(x, y, z, c):
    return x ^ 2, y, z, c


def y_up(x, y, z, c):
    return x, y + 1, z, c


def y_down(x, y, z, c):
    return x, y - 1, z, c


def y_far(x, y, z, c):
    return x, y + 2, z, c


def other_core(x, y, z, c):
    return x, y, z, 1 - c


def mirror_cross(x, y, z, c):
    return 3 - x, 3 - y, z, 1 - c


def mirror(x, y, z, c):
    return x ^ 2, 3 - y, z, 1 - c


VMEM = pl.BlockSpec(memory_space=pltpu.VMEM)
HBM = pl.BlockSpec(memory_space=pl.ANY)
SMEM = pl.BlockSpec(memory_space=pltpu.SMEM)


def _in_hbm(value):
    return pltpu.with_memory_space_constraint(value, pltpu.HBM)


def _block(index):
    return pl.ds(pl.multiple_of(index * DEPTH, DEPTH), DEPTH)


def _piece_loads(parts, pieces, x, sem):
    loads = []
    for i, piece in enumerate(pieces):
        at = 0
        loads.append([])
        for k, (operand, start, size) in enumerate(piece):
            loads[-1].append(
                pltpu.make_async_copy(
                    parts[operand].at[pl.ds(start, size)],
                    x.at[i, pl.ds(at, size)],
                    sem.at[i, k],
                )
            )
            at += size
    return loads


def _weight_loads(slices, n, far, near, sem):
    return [
        [
            pltpu.make_async_copy(src.at[_block(slices[i]), :], dst.at[i], sem.at[i, j])
            for j, (src, dst) in enumerate(zip(far, near))
        ]
        for i in range(n)
    ]


def _side_by_side(slices, n, far, near, sem):
    loads = []
    for i in range(n):
        at, group = 0, []
        for j, src in enumerate(far):
            width = src.shape[1]
            dst = near.at[i, :, pl.ds(at, width)]
            group.append(pltpu.make_async_copy(src.at[_block(slices[i]), :], dst, sem.at[i, j]))
            at += width
        loads.append(group)
    return loads


def _start(group):
    for copy in group:
        copy.start()


def _wait(group):
    for copy in group:
        copy.wait()


def _proj_body(arrays, pieces, started, slices, *refs):
    n = len(pieces)
    parts, far = refs[:arrays], refs[arrays : arrays + 3]
    refs = refs[arrays + 3 :]
    acc_in, refs = (refs[0], refs[1:]) if started else (None, refs)
    acc, x, near, (x_sem, w_sem, acc_sem) = refs[0], refs[1], refs[2:5], refs[5:8]
    x_loads = _piece_loads(parts, pieces, x, x_sem)
    w_loads = _weight_loads(slices, n, far, near, w_sem)
    for group in [x_loads[0], w_loads[0], *x_loads[1:], w_loads[1]]:
        _start(group)
    if started:
        acc_load = pltpu.make_async_copy(acc_in, acc, acc_sem)
        acc_load.start()
    spans = (slice(0, QCOLS), slice(QCOLS, QCOLS + HEAD), slice(QCOLS + HEAD, ALLCOLS))
    for i in range(n):
        _wait(x_loads[i])
        _wait(w_loads[i])
        if i + 2 < n:
            _start(w_loads[i + 2])
        if started and i == 0:
            acc_load.wait()
        for w, cols in zip(near, spans):
            term = jnp.dot(x[i], w[i], preferred_element_type=jnp.float32)
            if i or started:
                acc[:, cols] += term
            else:
                acc[:, cols] = term


def _project(slices, arrays, pieces, weights, acc=None):
    n = len(pieces)
    started = [] if acc is None else [acc]
    return pl.pallas_call(
        functools.partial(_proj_body, len(arrays), pieces, acc is not None),
        out_shape=jax.ShapeDtypeStruct((ROWS, ALLCOLS), jnp.float32),
        in_specs=[SMEM] + [HBM] * (len(arrays) + 3 + len(started)),
        out_specs=VMEM,
        scratch_shapes=[
            pltpu.VMEM((n, ROWS, DEPTH), jnp.bfloat16),
            pltpu.VMEM((n, DEPTH, QCOLS), jnp.bfloat16),
            pltpu.VMEM((n, DEPTH, HEAD), jnp.bfloat16),
            pltpu.VMEM((n, DEPTH, HEAD), jnp.bfloat16),
            pltpu.SemaphoreType.DMA((n, 3)),
            pltpu.SemaphoreType.DMA((n, 3)),
            pltpu.SemaphoreType.DMA,
        ],
        compiler_params=pltpu.CompilerParams(vmem_limit_bytes=28 * 1024 * 1024),
        cost_estimate=pl.CostEstimate(
            flops=2 * n * ROWS * DEPTH * ALLCOLS,
            bytes_accessed=2 * n * DEPTH * ALLCOLS,
            transcendentals=0,
        ),
        name="project",
    )(slices, *map(_in_hbm, arrays), *weights, *started)


def _rotate(u, cosine, sine):
    return u * cosine[...] + pltpu.roll(u, HEAD // 2, 1) * sine[...]


def _last_kv_body(arrays, pieces, slices, *refs):
    n = len(pieces)
    parts, (w_k, w_v), refs = refs[:arrays], refs[arrays : arrays + 2], refs[arrays + 2 :]
    given, (k_bias, v_bias, cosine, sine, out), refs = refs[0], refs[1:6], refs[6:]
    x, near, acc, x_sem, w_sem, sem = refs
    x_loads = _piece_loads(parts, pieces, x, x_sem)
    w_loads = _side_by_side(slices, n, (w_k, w_v), near, w_sem)
    others = [pltpu.make_async_copy(given.at[:, pl.ds(QCOLS, 2 * HEAD)], acc, sem)]
    for group in x_loads + w_loads + [others]:
        _start(group)
    both = 0
    for i in range(n):
        _wait(x_loads[i])
        _wait(w_loads[i])
        both += jnp.dot(x[i], near[i], preferred_element_type=jnp.float32)
    _wait(others)
    both += acc[...]
    k, v = both[:, :HEAD], both[:, HEAD:]
    k = _rotate(k + k_bias[...], cosine, sine).astype(jnp.bfloat16)
    v = (v + v_bias[...]).astype(jnp.bfloat16)
    for half in range(2):
        rows = slice(half * HALF, (half + 1) * HALF)
        out[half, :, :HEAD] = k[rows]
        out[half, :, HEAD:] = v[rows]


def _last_kv(slices, arrays, pieces, w_k, w_v, acc, k_bias, v_bias, cosine, sine):
    n = len(pieces)
    return pl.pallas_call(
        functools.partial(_last_kv_body, len(arrays), pieces),
        out_shape=jax.ShapeDtypeStruct((2, HALF, 2 * HEAD), jnp.bfloat16),
        in_specs=[SMEM] + [HBM] * (len(arrays) + 3) + [VMEM] * 4,
        out_specs=VMEM,
        scratch_shapes=[
            pltpu.VMEM((n, ROWS, DEPTH), jnp.bfloat16),
            pltpu.VMEM((n, DEPTH, 2 * HEAD), jnp.bfloat16),
            pltpu.VMEM((ROWS, 2 * HEAD), jnp.float32),
            pltpu.SemaphoreType.DMA((n, 4)),
            pltpu.SemaphoreType.DMA((n, 2)),
            pltpu.SemaphoreType.DMA,
        ],
        compiler_params=pltpu.CompilerParams(vmem_limit_bytes=12 * 1024 * 1024),
        cost_estimate=pl.CostEstimate(
            flops=4 * n * ROWS * DEPTH * HEAD,
            bytes_accessed=4 * n * DEPTH * HEAD,
            transcendentals=0,
        ),
        name="last_kv",
    )(slices, *map(_in_hbm, arrays), w_k, w_v, acc, k_bias, v_bias, cosine, sine)


def _last_q_body(arrays, pieces, slices, *refs):
    n = len(pieces)
    parts, w_q, refs = refs[:arrays], refs[arrays], refs[arrays + 1 :]
    given, (q_bias, cosine, sine, out), refs = refs[0], refs[1:5], refs[5:]
    x, near, acc, x_sem, w_sem, sem = refs
    x_loads = _piece_loads(parts, pieces, x, x_sem)
    w_loads = _weight_loads(slices, n, (w_q,), (near,), w_sem)
    others = [pltpu.make_async_copy(given.at[:, pl.ds(0, QCOLS)], acc, sem)]
    _start(x_loads[0])
    _start(w_loads[0])
    _start(others)
    for i in range(1, n):
        _start(x_loads[i])
        _start(w_loads[i])
    for i in range(n):
        _wait(x_loads[i])
        _wait(w_loads[i])
        if i == 0:
            _wait(others)
        if i < n - 1:
            acc[...] += jnp.dot(x[i], near[i], preferred_element_type=jnp.float32)
    for i in range(0, GROUP, 2):
        both = slice(i * HEAD, (i + 2) * HEAD)
        q = acc[:, both] + jnp.dot(x[n - 1], near[n - 1, :, both], preferred_element_type=jnp.float32)
        q += q_bias[:, both]
        for j in range(2):
            cols = slice((i + j) * HEAD, (i + j + 1) * HEAD)
            u = q[:, j * HEAD : (j + 1) * HEAD]
            out[:, cols] = _rotate(u, cosine, sine).astype(jnp.bfloat16)


def _last_q(slices, arrays, pieces, w_q, acc, q_bias, cosine, sine):
    n = len(pieces)
    return pl.pallas_call(
        functools.partial(_last_q_body, len(arrays), pieces),
        out_shape=jax.ShapeDtypeStruct((ROWS, QCOLS), jnp.bfloat16),
        in_specs=[SMEM] + [HBM] * (len(arrays) + 2) + [VMEM] * 3,
        out_specs=VMEM,
        scratch_shapes=[
            pltpu.VMEM((n, ROWS, DEPTH), jnp.bfloat16),
            pltpu.VMEM((n, DEPTH, QCOLS), jnp.bfloat16),
            pltpu.VMEM((ROWS, QCOLS), jnp.float32),
            pltpu.SemaphoreType.DMA((n, 4)),
            pltpu.SemaphoreType.DMA((n, 1)),
            pltpu.SemaphoreType.DMA,
        ],
        compiler_params=pltpu.CompilerParams(vmem_limit_bytes=20 * 1024 * 1024),
        cost_estimate=pl.CostEstimate(
            flops=2 * n * ROWS * DEPTH * QCOLS,
            bytes_accessed=2 * n * DEPTH * QCOLS,
            transcendentals=0,
        ),
        name="last_q",
    )(slices, *map(_in_hbm, arrays), w_q, acc, q_bias, cosine, sine)


def _stitch(shapes, moves, *operands):
    def body(*refs):
        sem = refs[-1]
        copies = []
        for i, (operand, start, size, o, at) in enumerate(moves):
            src, out = refs[operand], refs[len(operands) + o]
            if len(src.shape) < len(out.shape):
                copies.append(pltpu.make_async_copy(src, out.at[at], sem.at[i]))
            else:
                copies.append(
                    pltpu.make_async_copy(
                        src.at[pl.ds(start, size)], out.at[pl.ds(at, size)], sem.at[i]
                    )
                )
        _start(copies)
        _wait(copies)

    return pl.pallas_call(
        body,
        out_shape=[jax.ShapeDtypeStruct(shape, jnp.bfloat16) for shape in shapes],
        in_specs=[HBM] * len(operands),
        out_specs=[VMEM] * len(shapes),
        scratch_shapes=[pltpu.SemaphoreType.DMA((len(moves),))],
        compiler_params=pltpu.CompilerParams(vmem_limit_bytes=4 * 1024 * 1024),
        name="stitch",
    )(*map(_in_hbm, operands))


def _stack_tiles(arrays):
    moves = [(i, 0, 2, 0, 2 * i) for i in range(4)]
    return _stitch([(8, HALF, 2 * HEAD)], moves, *arrays)[0]


def _attend_body(first, final, part, meta, near, far, queries, *refs):
    states_in, refs = ((), refs) if first else (refs[:2], refs[2:])
    outs, refs = refs[:2], refs[2:]
    rows, even, odd, place = refs[:4]
    stat, acc = refs[-2:] if final else outs
    groups = acc.shape[0] // 2
    for group in range(groups):
        for job in range(2):
            for h in range(4):
                col = (part * 4 + group * 4 + h) * HEAD
                rows[2 * group + job, h * HALF : (h + 1) * HALF, :] = queries[
                    job * HALF : (job + 1) * HALF, col : col + HEAD
                ]
    for h in range(4):
        place[0:1, h * HALF : (h + 1) * HALF] = lax.broadcasted_iota(jnp.int32, (1, HALF), 1) + 1
    if first:
        stat[:, 0:1, :] = jnp.full((2 * groups, 1, LANES), -1e30, jnp.float32)
        stat[:, 1:8, :] = jnp.zeros((2 * groups, 7, LANES), jnp.float32)
        acc[...] = jnp.zeros_like(acc)
    else:
        stat[...] = states_in[0][2 * part : 2 * part + 2 * groups]
        acc[...] = states_in[1][2 * part : 2 * part + 2 * groups]
    def entry(block, i):
        return meta[22 + 2 * block[1] + i]

    def tiles(block, cols):
        j = jnp.minimum(entry(block, 1), 3)
        return jnp.concatenate(
            [array[meta[8 * i + 2 * j + t], :, cols] for i, array in enumerate((near, far)) for t in range(2)],
            axis=0,
        )

    def job_of(block):
        return entry(block, 0) + 2 * block[0]

    def score(block, out, mask):
        k = tiles(block, slice(0, HEAD))
        scores = lax.dot_general(k, rows[job_of(block)], NT, preferred_element_type=jnp.float32)
        if mask:
            mine = meta[20 + entry(block, 0)]
            key = lax.broadcasted_iota(jnp.int32, (HALF, LANES), 0)
            parts = []
            for t in range(4):
                tile = 8 * entry(block, 1) + meta[16 + t]
                seen = jnp.where(tile < mine, HALF, 0) + jnp.where(tile == mine, 1, 0) * place[0:1, :]
                parts.append(jnp.where(key < seen, scores[t * HALF : (t + 1) * HALF], -jnp.inf))
            scores = jnp.concatenate(parts, axis=0)
        out[0:SPAN, :] = scores
        out[SPAN : SPAN + 1, :] = jnp.max(scores, axis=0, keepdims=True)

    def finish(block, src):
        job = job_of(block)
        v = tiles(block, slice(HEAD, 2 * HEAD))
        old = stat[job, 0:1, :]
        new = jnp.maximum(old, src[SPAN : SPAN + 1, :])
        weights = jnp.exp2((src[0:SPAN, :] - new) * EXP2_SCALE)
        shrink = jnp.exp2((old - new) * EXP2_SCALE)
        stat[job, 0:1, :] = new
        stat[job, 1:2, :] = stat[job, 1:2, :] * shrink + jnp.sum(weights, axis=0, keepdims=True)
        acc[job] = acc[job] * shrink + lax.dot_general(
            v, weights.astype(jnp.bfloat16), TN, preferred_element_type=jnp.float32
        )

    def whole(b):
        return lax.div(b, WHOLE), lax.rem(b, WHOLE)

    last = [(g, p) for g in range(groups) for p in range(WHOLE, BLOCKS)]
    loops = (WHOLE * groups - 1) // 2
    score((0, 0), even, False)

    @pl.loop(0, loops)
    def _(i):
        score(whole(2 * i + 1), odd, False)
        finish(whole(2 * i), even)
        score(whole(2 * i + 2), even, False)
        finish(whole(2 * i + 1), odd)

    rest = [(b // WHOLE, b % WHOLE) for b in range(2 * loops, WHOLE * groups)]
    steps = [(block, False) for block in rest] + [(block, True) for block in last]
    buffers = (even, odd)
    for i, (block, _) in enumerate(steps):
        if i + 1 < len(steps):
            score(steps[i + 1][0], buffers[(i + 1) % 2], steps[i + 1][1])
        finish(block, buffers[i % 2])
    if final:
        for group in range(groups):
            for job in range(2):
                for h in range(0, 4, 2):
                    cols = slice(h * HALF, (h + 2) * HALF)
                    done = acc[2 * group + job, :, cols] / stat[2 * group + job, 1:2, cols]
                    pair = done.T.astype(jnp.bfloat16)
                    at = (group * 4 + h) * HEAD
                    outs[job][:HALF, at : at + HEAD] = pair[:HALF]
                    outs[job][:HALF, at + HEAD : at + 2 * HEAD] = pair[HALF:]
        if outs[1].shape[0] > HALF:
            spare = outs[1].shape[0] - HALF
            outs[1][HALF:, :] = jnp.zeros((spare, outs[1].shape[1]), jnp.bfloat16)


def _attend(meta, near, far, queries, states=(), groups=2, part=0, spare=0):
    final = bool(states)
    state_shape = [(2 * groups, 8, LANES), (2 * groups, HEAD, LANES)]
    if final:
        out_shape = [
            jax.ShapeDtypeStruct((HALF, groups * 4 * HEAD), jnp.bfloat16),
            jax.ShapeDtypeStruct((HALF + spare, groups * 4 * HEAD), jnp.bfloat16),
        ]
    else:
        out_shape = [jax.ShapeDtypeStruct(shape, jnp.float32) for shape in state_shape]
    operands = [near, far, queries, *states]
    return pl.pallas_call(
        functools.partial(_attend_body, not states, final, part),
        out_shape=out_shape,
        in_specs=[SMEM] + [VMEM] * len(operands),
        out_specs=[VMEM] * len(out_shape),
        scratch_shapes=[
            pltpu.VMEM((2 * groups, LANES, HEAD), jnp.bfloat16),
            pltpu.VMEM((SPAN + 8, LANES), jnp.float32),
            pltpu.VMEM((SPAN + 8, LANES), jnp.float32),
            pltpu.VMEM((8, LANES), jnp.int32),
        ]
        + ([pltpu.VMEM(shape, jnp.float32) for shape in state_shape] if final else []),
        compiler_params=pltpu.CompilerParams(vmem_limit_bytes=28 * 1024 * 1024),
        cost_estimate=pl.CostEstimate(
            flops=4 * groups * BLOCKS * SPAN * HEAD * LANES,
            bytes_accessed=4 * 1024 * 1024,
            transcendentals=groups * BLOCKS * SPAN * LANES,
        ),
        name="attend",
    )(meta, *operands)


def _meta(order, lowest, early_query, late_query, early_count, late_count):
    early_whole, late_whole = early_count // 4, late_count // 4
    four = early_whole + late_whole == 4
    blocks = []
    for b in range(WHOLE):
        late = (b >= early_whole).astype(jnp.int32)
        blocks.append((late, b - late * early_whole))
    blocks.append((four.astype(jnp.int32), jnp.where(four, late_whole - 1, early_whole)))
    blocks.append((1, late_whole))
    entries = [*lowest, early_query, late_query]
    for late, block in blocks:
        entries += [late, block]
    return jnp.concatenate([order, jnp.stack([jnp.asarray(e, jnp.int32) for e in entries])])


def _angles(positions):
    half = HEAD // 2
    freq = rope_base ** (-2.0 * jnp.arange(half, dtype=jnp.float32) / HEAD)
    phase = positions.astype(jnp.float32)[:, None] * freq[None, :]
    cosine, sine = jnp.cos(phase), jnp.sin(phase)
    return jnp.concatenate([cosine, cosine], axis=1), jnp.concatenate([-sine, sine], axis=1)


def _after(value, *earlier):
    return lax.optimization_barrier((value, *earlier))[0]


def local(hidden, w_query, w_key, w_value, q_bias, k_bias, v_bias):
    seq = lax.axis_index("seq")
    tp = lax.axis_index("tp")
    y, x_hi, core = seq // 4, seq // 2 % 2, seq % 2
    x_lo, z = tp // 4, tp % 4
    weights = [w_query, w_key, w_value]
    q_bias, k_bias, v_bias = q_bias[None], k_bias[None], v_bias[None]

    def feature(lo, dz):
        return lo * 4 + (z + dz) % 4

    def tile_seq(dy, dx, dc):
        return ((y + dy) % 4 * 2 + (x_hi ^ dx)) * 2 + (core ^ dc)

    def order(dc):
        where, lowest = [], []
        for dx in (0, 1):
            seqs = [tile_seq(dy, dx, dc) for dy in (0, -1, 1, 2)]
            ranks = jnp.stack([t // 4 for s in seqs for t in (2 * s, 31 - 2 * s)])
            at = jnp.arange(8, dtype=jnp.int32)
            where.append(jnp.sum(jnp.where(ranks[None, :] == at[:, None], at[None, :], 0), axis=1))
            a = 4 * (x_hi ^ dx) + 2 * (core ^ dc)
            lowest += [jnp.minimum(a, 7 - a), jnp.maximum(a, 7 - a)]
        return jnp.concatenate(where).astype(jnp.int32), lowest

    far_lo = 1 - x_lo

    def ints(*values):
        return jnp.stack(values).astype(jnp.int32)

    w_query, w_key, w_value = weights = [
        pltpu.with_memory_space_constraint(w, pltpu.HBM) for w in weights
    ]
    early, late = _stitch(
        [(HALF, DEPTH)] * 2, [(0, 0, HALF, 0, 0), (0, HALF, HALF, 1, 0)], hidden
    )
    side = _send(early, x_near)
    up, down = _send(early, z_up), _send(early, z_down)
    late = _send(late, mirror_cross)
    row = jnp.arange(HALF, dtype=jnp.int32)
    rope = _angles(jnp.concatenate([seq * ROWS + row, (31 - 2 * seq) * HALF + row]))
    mine = seq * 2, 31 - seq * 2
    meta = _meta(*order(0), *mine, seq, 15 - seq)
    other_meta = _meta(*order(1), *mine, seq, 16 - seq)
    up, meta, other_meta, *rope = lax.optimization_barrier((up, meta, other_meta, *rope))

    to_up, to_down = _stitch(
        [(HALF, DEPTH)] * 2,
        [
            (0, 0, PART, 0, 0),
            (2, 0, PART, 0, PART),
            (1, PART, PART, 1, 0),
            (2, 0, PART, 1, PART),
        ],
        up,
        down,
        side,
    )
    from_down, from_up = _send(to_up, z_up), _send(to_down, z_down)
    late_side = _send(late, x_near)

    across, both = _stitch(
        [(ROWS, DEPTH)] * 2,
        [
            (2, 0, PART, 0, 0),
            (3, 0, PART, 0, PART),
            (0, PART, PART, 0, HALF),
            (1, PART, PART, 0, HALF + PART),
            (4, 0, HALF, 1, 0),
            (5, 0, HALF, 1, HALF),
        ],
        up,
        down,
        from_down,
        from_up,
        late,
        late_side,
    )
    late_up, late_down = _send(both, z_up), _send(both, z_down)
    got = _send(across, x_near)
    acc = _project(
        ints(feature(x_lo, 0), feature(far_lo, 0)),
        [_after(early, across), late_side, side, late],
        ([(0, 0, HALF), (1, 0, HALF)], [(2, 0, HALF), (3, 0, HALF)]),
        weights,
    )

    to_up, to_down = _stitch(
        [(HALF, DEPTH)] * 2,
        [
            (0, 0, PART, 0, 0),
            (0, HALF, PART, 0, PART),
            (1, PART, PART, 1, 0),
            (1, HALF + PART, PART, 1, PART),
        ],
        _after(late_up, acc),
        late_down,
    )
    late_from_down, late_from_up = _send(to_up, z_up), _send(to_down, z_down)
    acc = _project(
        ints(feature(x_lo, -1), feature(x_lo, 1), feature(far_lo, -1), feature(far_lo, 1)),
        [_after(up, to_up), down, from_down, from_up, got, late_up, late_down],
        (
            [(0, 0, HALF), (5, HALF, HALF)],
            [(1, 0, HALF), (6, HALF, HALF)],
            [(2, PART, PART), (4, HALF, PART), (5, 0, HALF)],
            [(3, PART, PART), (4, HALF + PART, PART), (6, 0, HALF)],
        ),
        weights,
        acc,
    )
    which = ints(feature(far_lo, 2), feature(x_lo, 2))
    arrays = [got, from_down, from_up, late_from_down, late_from_up]
    pieces = (
        [(0, 0, HALF), (3, 0, PART), (4, 0, PART)],
        [(1, 0, PART), (2, 0, PART), (3, PART, PART), (4, PART, PART)],
    )
    kv = _last_kv(which, arrays, pieces, w_key, w_value, acc, k_bias, v_bias, *rope)
    far_kv = _send(kv, x_far)
    near_kv = [kv, _send(kv, y_up), _send(kv, y_down), _send(kv, y_far)]
    queries = _last_q(which, [_after(got, kv), *arrays[1:]], pieces, w_query, acc, q_bias, *rope)
    far_kv = _after(far_kv, queries)
    far_kv = [far_kv, _send(far_kv, y_up), _send(far_kv, y_down), _send(far_kv, y_far)]
    near_tiles = _stack_tiles(near_kv)
    far_tiles = _stack_tiles(far_kv)
    other_kv = [_send(near_tiles, other_core), _send(far_tiles, other_core)]

    states = _attend(_after(meta, far_tiles), near_tiles, far_tiles, queries)
    early_low, late_low = _attend(other_meta, *other_kv, queries, states, groups=1, spare=16)
    back_low = _send(late_low, mirror)
    early_high, late_high = _attend(
        _after(other_meta, late_low), *other_kv, queries, states, groups=1, part=1
    )
    back_high = _send(late_high, mirror)
    return jnp.concatenate(
        [
            jnp.concatenate([early_low, early_high], axis=1),
            jnp.concatenate([back_low[:HALF], back_high], axis=1),
        ],
        axis=0,
    )


def solution(mesh):
    return jax.shard_map(
        local,
        mesh=mesh,
        in_specs=(
            P("seq", "tp"),
            P(None, "tp"),
            P(None, "tp"),
            P(None, "tp"),
            P("tp"),
            P("tp"),
            P("tp"),
        ),
        out_specs=P("seq", "tp"),
        check_vma=False,
    )
```

```python
import functools
import math

import jax
import jax.numpy as jnp
from jax import lax
from jax.experimental import pallas as pl
from jax.experimental.pallas import tpu as pltpu
from jax.sharding import PartitionSpec as P

HEAD = 128
GROUP = 8
HALF = 192
PART = HALF // 2
ROWS = 2 * HALF
DEPTH = 1024
QCOLS = GROUP * HEAD
ALLCOLS = QCOLS + 2 * HEAD
LANES = 4 * HALF
SPAN = 4 * HALF
BLOCKS = 5
WHOLE = 3
AXES = ("seq", "tp")
VMEM_LIMIT = 48 * 1024 * 1024
EXP2_SCALE = float(HEAD) ** (-0.5) * math.log2(math.e)
NT = (((1,), (1,)), ((), ()))
TN = (((0,), (0,)), ((), ()))
rope_base = 1000000.0


def _place(flat):
    seq, tp = divmod(flat, 8)
    x_lo, z = divmod(tp, 4)
    y, rest = divmod(seq, 4)
    x_hi, core = divmod(rest, 2)
    return x_hi * 2 + x_lo, y, z, core


def _index(x, y, z, core):
    x_hi, x_lo = divmod(x % 4, 2)
    return (((y % 4) * 2 + x_hi) * 2 + core) * 8 + x_lo * 4 + z % 4


def _send(value, move):
    pairs = [(i, _index(*move(*_place(i)))) for i in range(128)]
    return lax.ppermute(value, AXES, pairs)


def z_up(x, y, z, c):
    return x, y, z + 1, c


def z_down(x, y, z, c):
    return x, y, z - 1, c


def x_near(x, y, z, c):
    return x ^ 1, y, z, c


def x_far(x, y, z, c):
    return x ^ 2, y, z, c


def y_up(x, y, z, c):
    return x, y + 1, z, c


def y_down(x, y, z, c):
    return x, y - 1, z, c


def y_far(x, y, z, c):
    return x, y + 2, z, c


def other_core(x, y, z, c):
    return x, y, z, 1 - c


def mirror_cross(x, y, z, c):
    return 3 - x, 3 - y, z, 1 - c


def mirror(x, y, z, c):
    return x ^ 2, 3 - y, z, 1 - c


VMEM = pl.BlockSpec(memory_space=pltpu.VMEM)
HBM = pl.BlockSpec(memory_space=pl.ANY)
SMEM = pl.BlockSpec(memory_space=pltpu.SMEM)


def _in_hbm(value):
    return pltpu.with_memory_space_constraint(value, pltpu.HBM)


def _block(index):
    return pl.ds(pl.multiple_of(index * DEPTH, DEPTH), DEPTH)


def _piece_loads(parts, pieces, x, sem):
    loads = []
    for i, piece in enumerate(pieces):
        at = 0
        loads.append([])
        for k, (operand, start, size) in enumerate(piece):
            loads[-1].append(
                pltpu.make_async_copy(
                    parts[operand].at[pl.ds(start, size)],
                    x.at[i, pl.ds(at, size)],
                    sem.at[i, k],
                )
            )
            at += size
    return loads


def _weight_loads(slices, n, far, near, sem):
    return [
        [
            pltpu.make_async_copy(src.at[_block(slices[i]), :], dst.at[i], sem.at[i, j])
            for j, (src, dst) in enumerate(zip(far, near))
        ]
        for i in range(n)
    ]


def _side_by_side(slices, n, far, near, sem):
    loads = []
    for i in range(n):
        at, group = 0, []
        for j, src in enumerate(far):
            width = src.shape[1]
            dst = near.at[i, :, pl.ds(at, width)]
            group.append(pltpu.make_async_copy(src.at[_block(slices[i]), :], dst, sem.at[i, j]))
            at += width
        loads.append(group)
    return loads


def _start(group):
    for copy in group:
        copy.start()


def _wait(group):
    for copy in group:
        copy.wait()


def _proj_body(arrays, pieces, started, slices, *refs):
    n = len(pieces)
    parts, far = refs[:arrays], refs[arrays : arrays + 3]
    refs = refs[arrays + 3 :]
    acc_in, refs = (refs[0], refs[1:]) if started else (None, refs)
    acc, x, near, (x_sem, w_sem, acc_sem) = refs[0], refs[1], refs[2:5], refs[5:8]
    x_loads = _piece_loads(parts, pieces, x, x_sem)
    w_loads = _weight_loads(slices, n, far, near, w_sem)
    for group in [x_loads[0], w_loads[0], *x_loads[1:], w_loads[1]]:
        _start(group)
    if started:
        acc_load = pltpu.make_async_copy(acc_in, acc, acc_sem)
        acc_load.start()
    spans = (slice(0, QCOLS), slice(QCOLS, QCOLS + HEAD), slice(QCOLS + HEAD, ALLCOLS))
    for i in range(n):
        _wait(x_loads[i])
        _wait(w_loads[i])
        if i + 2 < n:
            _start(w_loads[i + 2])
        if started and i == 0:
            acc_load.wait()
        for w, cols in zip(near, spans):
            term = jnp.dot(x[i], w[i], preferred_element_type=jnp.float32)
            if i or started:
                acc[:, cols] += term
            else:
                acc[:, cols] = term


def _project(slices, arrays, pieces, weights, acc=None):
    n = len(pieces)
    started = [] if acc is None else [acc]
    return pl.pallas_call(
        functools.partial(_proj_body, len(arrays), pieces, acc is not None),
        out_shape=jax.ShapeDtypeStruct((ROWS, ALLCOLS), jnp.float32),
        in_specs=[SMEM] + [HBM] * (len(arrays) + 3 + len(started)),
        out_specs=VMEM,
        scratch_shapes=[
            pltpu.VMEM((n, ROWS, DEPTH), jnp.bfloat16),
            pltpu.VMEM((n, DEPTH, QCOLS), jnp.bfloat16),
            pltpu.VMEM((n, DEPTH, HEAD), jnp.bfloat16),
            pltpu.VMEM((n, DEPTH, HEAD), jnp.bfloat16),
            pltpu.SemaphoreType.DMA((n, 3)),
            pltpu.SemaphoreType.DMA((n, 3)),
            pltpu.SemaphoreType.DMA,
        ],
        compiler_params=pltpu.CompilerParams(vmem_limit_bytes=28 * 1024 * 1024),
        cost_estimate=pl.CostEstimate(
            flops=2 * n * ROWS * DEPTH * ALLCOLS,
            bytes_accessed=2 * n * DEPTH * ALLCOLS,
            transcendentals=0,
        ),
        name="project",
    )(slices, *map(_in_hbm, arrays), *weights, *started)


def _rotate(u, cosine, sine):
    return u * cosine[...] + pltpu.roll(u, HEAD // 2, 1) * sine[...]


def _last_kv_body(arrays, pieces, slices, *refs):
    n = len(pieces)
    parts, (w_k, w_v), refs = refs[:arrays], refs[arrays : arrays + 2], refs[arrays + 2 :]
    given, (k_bias, v_bias, cosine, sine, out), refs = refs[0], refs[1:6], refs[6:]
    x, near, acc, x_sem, w_sem, sem = refs
    x_loads = _piece_loads(parts, pieces, x, x_sem)
    w_loads = _side_by_side(slices, n, (w_k, w_v), near, w_sem)
    others = [pltpu.make_async_copy(given.at[:, pl.ds(QCOLS, 2 * HEAD)], acc, sem)]
    for group in x_loads + w_loads + [others]:
        _start(group)
    both = 0
    for i in range(n):
        _wait(x_loads[i])
        _wait(w_loads[i])
        both += jnp.dot(x[i], near[i], preferred_element_type=jnp.float32)
    _wait(others)
    both += acc[...]
    k, v = both[:, :HEAD], both[:, HEAD:]
    k = _rotate(k + k_bias[...], cosine, sine).astype(jnp.bfloat16)
    v = (v + v_bias[...]).astype(jnp.bfloat16)
    for half in range(2):
        rows = slice(half * HALF, (half + 1) * HALF)
        out[half, :, :HEAD] = k[rows]
        out[half, :, HEAD:] = v[rows]


def _last_kv(slices, arrays, pieces, w_k, w_v, acc, k_bias, v_bias, cosine, sine):
    n = len(pieces)
    return pl.pallas_call(
        functools.partial(_last_kv_body, len(arrays), pieces),
        out_shape=jax.ShapeDtypeStruct((2, HALF, 2 * HEAD), jnp.bfloat16),
        in_specs=[SMEM] + [HBM] * (len(arrays) + 3) + [VMEM] * 4,
        out_specs=VMEM,
        scratch_shapes=[
            pltpu.VMEM((n, ROWS, DEPTH), jnp.bfloat16),
            pltpu.VMEM((n, DEPTH, 2 * HEAD), jnp.bfloat16),
            pltpu.VMEM((ROWS, 2 * HEAD), jnp.float32),
            pltpu.SemaphoreType.DMA((n, 4)),
            pltpu.SemaphoreType.DMA((n, 2)),
            pltpu.SemaphoreType.DMA,
        ],
        compiler_params=pltpu.CompilerParams(vmem_limit_bytes=12 * 1024 * 1024),
        cost_estimate=pl.CostEstimate(
            flops=4 * n * ROWS * DEPTH * HEAD,
            bytes_accessed=4 * n * DEPTH * HEAD,
            transcendentals=0,
        ),
        name="last_kv",
    )(slices, *map(_in_hbm, arrays), w_k, w_v, acc, k_bias, v_bias, cosine, sine)


def _last_q_body(arrays, pieces, slices, *refs):
    n = len(pieces)
    parts, w_q, refs = refs[:arrays], refs[arrays], refs[arrays + 1 :]
    given, (q_bias, cosine, sine, out), refs = refs[0], refs[1:5], refs[5:]
    x, near, acc, x_sem, w_sem, sem = refs
    x_loads = _piece_loads(parts, pieces, x, x_sem)
    w_loads = _weight_loads(slices, n, (w_q,), (near,), w_sem)
    others = [pltpu.make_async_copy(given.at[:, pl.ds(0, QCOLS)], acc, sem)]
    _start(x_loads[0])
    _start(w_loads[0])
    _start(others)
    for i in range(1, n):
        _start(x_loads[i])
        _start(w_loads[i])
    for i in range(n):
        _wait(x_loads[i])
        _wait(w_loads[i])
        if i == 0:
            _wait(others)
        if i < n - 1:
            acc[...] += jnp.dot(x[i], near[i], preferred_element_type=jnp.float32)
    for i in range(0, GROUP, 2):
        both = slice(i * HEAD, (i + 2) * HEAD)
        q = acc[:, both] + jnp.dot(x[n - 1], near[n - 1, :, both], preferred_element_type=jnp.float32)
        q += q_bias[:, both]
        for j in range(2):
            cols = slice((i + j) * HEAD, (i + j + 1) * HEAD)
            u = q[:, j * HEAD : (j + 1) * HEAD]
            out[:, cols] = _rotate(u, cosine, sine).astype(jnp.bfloat16)


def _last_q(slices, arrays, pieces, w_q, acc, q_bias, cosine, sine):
    n = len(pieces)
    return pl.pallas_call(
        functools.partial(_last_q_body, len(arrays), pieces),
        out_shape=jax.ShapeDtypeStruct((ROWS, QCOLS), jnp.bfloat16),
        in_specs=[SMEM] + [HBM] * (len(arrays) + 2) + [VMEM] * 3,
        out_specs=VMEM,
        scratch_shapes=[
            pltpu.VMEM((n, ROWS, DEPTH), jnp.bfloat16),
            pltpu.VMEM((n, DEPTH, QCOLS), jnp.bfloat16),
            pltpu.VMEM((ROWS, QCOLS), jnp.float32),
            pltpu.SemaphoreType.DMA((n, 4)),
            pltpu.SemaphoreType.DMA((n, 1)),
            pltpu.SemaphoreType.DMA,
        ],
        compiler_params=pltpu.CompilerParams(vmem_limit_bytes=20 * 1024 * 1024),
        cost_estimate=pl.CostEstimate(
            flops=2 * n * ROWS * DEPTH * QCOLS,
            bytes_accessed=2 * n * DEPTH * QCOLS,
            transcendentals=0,
        ),
        name="last_q",
    )(slices, *map(_in_hbm, arrays), w_q, acc, q_bias, cosine, sine)


def _stitch(shapes, moves, *operands, pinned=True):
    def body(*refs):
        sem = refs[-1]
        copies = []
        for i, (operand, start, size, o, at) in enumerate(moves):
            src, out = refs[operand], refs[len(operands) + o]
            if len(src.shape) < len(out.shape):
                copies.append(pltpu.make_async_copy(src, out.at[at], sem.at[i]))
            else:
                copies.append(
                    pltpu.make_async_copy(
                        src.at[pl.ds(start, size)], out.at[pl.ds(at, size)], sem.at[i]
                    )
                )
        _start(copies)
        _wait(copies)

    return pl.pallas_call(
        body,
        out_shape=[jax.ShapeDtypeStruct(shape, jnp.bfloat16) for shape in shapes],
        in_specs=[HBM] * len(operands),
        out_specs=[VMEM] * len(shapes),
        scratch_shapes=[pltpu.SemaphoreType.DMA((len(moves),))],
        compiler_params=pltpu.CompilerParams(vmem_limit_bytes=4 * 1024 * 1024),
        name="stitch",
    )(*(map(_in_hbm, operands) if pinned else operands))


def _stack_tiles(arrays):
    moves = [(i, 0, 2, 0, 2 * i) for i in range(4)]
    return _stitch([(8, HALF, 2 * HEAD)], moves, *arrays, pinned=False)[0]


def _attend_body(first, final, part, meta, near, far, queries, *refs):
    states_in, refs = ((), refs) if first else (refs[:2], refs[2:])
    outs, refs = refs[:2], refs[2:]
    rows, even, odd, place = refs[:4]
    stat, acc = refs[-2:] if final else outs
    groups = acc.shape[0] // 2
    for group in range(groups):
        for job in range(2):
            for h in range(4):
                col = (part * 4 + group * 4 + h) * HEAD
                rows[2 * group + job, h * HALF : (h + 1) * HALF, :] = queries[
                    job * HALF : (job + 1) * HALF, col : col + HEAD
                ]
    for h in range(4):
        place[0:1, h * HALF : (h + 1) * HALF] = lax.broadcasted_iota(jnp.int32, (1, HALF), 1) + 1
    if first:
        stat[:, 0:1, :] = jnp.full((2 * groups, 1, LANES), -1e30, jnp.float32)
        stat[:, 1:8, :] = jnp.zeros((2 * groups, 7, LANES), jnp.float32)
        acc[...] = jnp.zeros_like(acc)
    else:
        stat[...] = states_in[0][2 * part : 2 * part + 2 * groups]
        acc[...] = states_in[1][2 * part : 2 * part + 2 * groups]
    def entry(block, i):
        return meta[22 + 2 * block[1] + i]

    def tiles(block, cols):
        j = jnp.minimum(entry(block, 1), 3)
        return jnp.concatenate(
            [array[meta[8 * i + 2 * j + t], :, cols] for i, array in enumerate((near, far)) for t in range(2)],
            axis=0,
        )

    def job_of(block):
        return entry(block, 0) + 2 * block[0]

    def score(block, out, mask):
        k = tiles(block, slice(0, HEAD))
        scores = lax.dot_general(k, rows[job_of(block)], NT, preferred_element_type=jnp.float32)
        if mask:
            mine = meta[20 + entry(block, 0)]
            key = lax.broadcasted_iota(jnp.int32, (HALF, LANES), 0)
            parts = []
            for t in range(4):
                tile = 8 * entry(block, 1) + meta[16 + t]
                seen = jnp.where(tile < mine, HALF, 0) + jnp.where(tile == mine, 1, 0) * place[0:1, :]
                parts.append(jnp.where(key < seen, scores[t * HALF : (t + 1) * HALF], -jnp.inf))
            scores = jnp.concatenate(parts, axis=0)
        out[0:SPAN, :] = scores
        out[SPAN : SPAN + 1, :] = jnp.max(scores, axis=0, keepdims=True)

    def finish(block, src):
        job = job_of(block)
        v = tiles(block, slice(HEAD, 2 * HEAD))
        old = stat[job, 0:1, :]
        new = jnp.maximum(old, src[SPAN : SPAN + 1, :])
        weights = jnp.exp2((src[0:SPAN, :] - new) * EXP2_SCALE)
        shrink = jnp.exp2((old - new) * EXP2_SCALE)
        stat[job, 0:1, :] = new
        stat[job, 1:2, :] = stat[job, 1:2, :] * shrink + jnp.sum(weights, axis=0, keepdims=True)
        acc[job] = acc[job] * shrink + lax.dot_general(
            v, weights.astype(jnp.bfloat16), TN, preferred_element_type=jnp.float32
        )

    def whole(b):
        return lax.div(b, WHOLE), lax.rem(b, WHOLE)

    last = [(g, p) for g in range(groups) for p in range(WHOLE, BLOCKS)]
    loops = (WHOLE * groups - 1) // 2
    score((0, 0), even, False)

    @pl.loop(0, loops)
    def _(i):
        score(whole(2 * i + 1), odd, False)
        finish(whole(2 * i), even)
        score(whole(2 * i + 2), even, False)
        finish(whole(2 * i + 1), odd)

    rest = [(b // WHOLE, b % WHOLE) for b in range(2 * loops, WHOLE * groups)]
    steps = [(block, False) for block in rest] + [(block, True) for block in last]
    buffers = (even, odd)
    for i, (block, _) in enumerate(steps):
        if i + 1 < len(steps):
            score(steps[i + 1][0], buffers[(i + 1) % 2], steps[i + 1][1])
        finish(block, buffers[i % 2])
    if final:
        for group in range(groups):
            for job in range(2):
                for h in range(0, 4, 2):
                    cols = slice(h * HALF, (h + 2) * HALF)
                    done = acc[2 * group + job, :, cols] / stat[2 * group + job, 1:2, cols]
                    pair = done.T.astype(jnp.bfloat16)
                    at = (group * 4 + h) * HEAD
                    outs[job][:HALF, at : at + HEAD] = pair[:HALF]
                    outs[job][:HALF, at + HEAD : at + 2 * HEAD] = pair[HALF:]
        if outs[1].shape[0] > HALF:
            spare = outs[1].shape[0] - HALF
            outs[1][HALF:, :] = jnp.zeros((spare, outs[1].shape[1]), jnp.bfloat16)


def _attend(meta, near, far, queries, states=(), groups=2, part=0, spare=0):
    final = bool(states)
    state_shape = [(2 * groups, 8, LANES), (2 * groups, HEAD, LANES)]
    if final:
        out_shape = [
            jax.ShapeDtypeStruct((HALF, groups * 4 * HEAD), jnp.bfloat16),
            jax.ShapeDtypeStruct((HALF + spare, groups * 4 * HEAD), jnp.bfloat16),
        ]
    else:
        out_shape = [jax.ShapeDtypeStruct(shape, jnp.float32) for shape in state_shape]
    operands = [near, far, queries, *states]
    return pl.pallas_call(
        functools.partial(_attend_body, not states, final, part),
        out_shape=out_shape,
        in_specs=[SMEM] + [VMEM] * len(operands),
        out_specs=[VMEM] * len(out_shape),
        scratch_shapes=[
            pltpu.VMEM((2 * groups, LANES, HEAD), jnp.bfloat16),
            pltpu.VMEM((SPAN + 8, LANES), jnp.float32),
            pltpu.VMEM((SPAN + 8, LANES), jnp.float32),
            pltpu.VMEM((8, LANES), jnp.int32),
        ]
        + ([pltpu.VMEM(shape, jnp.float32) for shape in state_shape] if final else []),
        compiler_params=pltpu.CompilerParams(vmem_limit_bytes=28 * 1024 * 1024),
        cost_estimate=pl.CostEstimate(
            flops=4 * groups * BLOCKS * SPAN * HEAD * LANES,
            bytes_accessed=4 * 1024 * 1024,
            transcendentals=groups * BLOCKS * SPAN * LANES,
        ),
        name="attend",
    )(meta, *operands)


def _meta(order, lowest, early_query, late_query, early_count, late_count):
    early_whole, late_whole = early_count // 4, late_count // 4
    four = early_whole + late_whole == 4
    blocks = []
    for b in range(WHOLE):
        late = (b >= early_whole).astype(jnp.int32)
        blocks.append((late, b - late * early_whole))
    blocks.append((four.astype(jnp.int32), jnp.where(four, late_whole - 1, early_whole)))
    blocks.append((1, late_whole))
    entries = [*lowest, early_query, late_query]
    for late, block in blocks:
        entries += [late, block]
    return jnp.concatenate([order, jnp.stack([jnp.asarray(e, jnp.int32) for e in entries])])


def _angles(positions):
    half = HEAD // 2
    freq = rope_base ** (-2.0 * jnp.arange(half, dtype=jnp.float32) / HEAD)
    phase = positions.astype(jnp.float32)[:, None] * freq[None, :]
    cosine, sine = jnp.cos(phase), jnp.sin(phase)
    return jnp.concatenate([cosine, cosine], axis=1), jnp.concatenate([-sine, sine], axis=1)


def _after(value, *earlier):
    return lax.optimization_barrier((value, *earlier))[0]


def local(hidden, w_query, w_key, w_value, q_bias, k_bias, v_bias):
    seq = lax.axis_index("seq")
    tp = lax.axis_index("tp")
    y, x_hi, core = seq // 4, seq // 2 % 2, seq % 2
    x_lo, z = tp // 4, tp % 4
    weights = [w_query, w_key, w_value]
    q_bias, k_bias, v_bias = q_bias[None], k_bias[None], v_bias[None]

    def feature(lo, dz):
        return lo * 4 + (z + dz) % 4

    def tile_seq(dy, dx, dc):
        return ((y + dy) % 4 * 2 + (x_hi ^ dx)) * 2 + (core ^ dc)

    def order(dc):
        where, lowest = [], []
        for dx in (0, 1):
            seqs = [tile_seq(dy, dx, dc) for dy in (0, -1, 1, 2)]
            ranks = jnp.stack([t // 4 for s in seqs for t in (2 * s, 31 - 2 * s)])
            at = jnp.arange(8, dtype=jnp.int32)
            where.append(jnp.sum(jnp.where(ranks[None, :] == at[:, None], at[None, :], 0), axis=1))
            a = 4 * (x_hi ^ dx) + 2 * (core ^ dc)
            lowest += [jnp.minimum(a, 7 - a), jnp.maximum(a, 7 - a)]
        return jnp.concatenate(where).astype(jnp.int32), lowest

    far_lo = 1 - x_lo

    def ints(*values):
        return jnp.stack(values).astype(jnp.int32)

    w_query, w_key, w_value = weights = [
        pltpu.with_memory_space_constraint(w, pltpu.HBM) for w in weights
    ]
    early, late = _stitch(
        [(HALF, DEPTH)] * 2, [(0, 0, HALF, 0, 0), (0, HALF, HALF, 1, 0)], hidden
    )
    side = _send(early, x_near)
    up, down = _send(early, z_up), _send(early, z_down)
    late = _send(late, mirror_cross)
    row = jnp.arange(HALF, dtype=jnp.int32)
    rope = _angles(jnp.concatenate([seq * ROWS + row, (31 - 2 * seq) * HALF + row]))
    mine = seq * 2, 31 - seq * 2
    meta = _meta(*order(0), *mine, seq, 15 - seq)
    other_meta = _meta(*order(1), *mine, seq, 16 - seq)
    up, meta, other_meta, *rope = lax.optimization_barrier((up, meta, other_meta, *rope))

    to_up, to_down = _stitch(
        [(HALF, DEPTH)] * 2,
        [
            (0, 0, PART, 0, 0),
            (2, 0, PART, 0, PART),
            (1, PART, PART, 1, 0),
            (2, 0, PART, 1, PART),
        ],
        up,
        down,
        side,
    )
    from_down, from_up = _send(to_up, z_up), _send(to_down, z_down)
    late_side = _send(late, x_near)

    across, both = _stitch(
        [(ROWS, DEPTH)] * 2,
        [
            (2, 0, PART, 0, 0),
            (3, 0, PART, 0, PART),
            (0, PART, PART, 0, HALF),
            (1, PART, PART, 0, HALF + PART),
            (4, 0, HALF, 1, 0),
            (5, 0, HALF, 1, HALF),
        ],
        up,
        down,
        from_down,
        from_up,
        late,
        late_side,
    )
    late_up, late_down = _send(both, z_up), _send(both, z_down)
    got = _send(across, x_near)
    acc = _project(
        ints(feature(x_lo, 0), feature(far_lo, 0)),
        [_after(early, across), late_side, side, late],
        ([(0, 0, HALF), (1, 0, HALF)], [(2, 0, HALF), (3, 0, HALF)]),
        weights,
    )

    to_up, to_down = _stitch(
        [(HALF, DEPTH)] * 2,
        [
            (0, 0, PART, 0, 0),
            (0, HALF, PART, 0, PART),
            (1, PART, PART, 1, 0),
            (1, HALF + PART, PART, 1, PART),
        ],
        _after(late_up, acc),
        late_down,
    )
    late_from_down, late_from_up = _send(to_up, z_up), _send(to_down, z_down)
    acc = _project(
        ints(feature(x_lo, -1), feature(x_lo, 1), feature(far_lo, -1), feature(far_lo, 1)),
        [_after(up, to_up), down, from_down, from_up, got, late_up, late_down],
        (
            [(0, 0, HALF), (5, HALF, HALF)],
            [(1, 0, HALF), (6, HALF, HALF)],
            [(2, PART, PART), (4, HALF, PART), (5, 0, HALF)],
            [(3, PART, PART), (4, HALF + PART, PART), (6, 0, HALF)],
        ),
        weights,
        acc,
    )
    which = ints(feature(far_lo, 2), feature(x_lo, 2))
    arrays = [got, from_down, from_up, late_from_down, late_from_up]
    pieces = (
        [(0, 0, HALF), (3, 0, PART), (4, 0, PART)],
        [(1, 0, PART), (2, 0, PART), (3, PART, PART), (4, PART, PART)],
    )
    kv = _last_kv(which, arrays, pieces, w_key, w_value, acc, k_bias, v_bias, *rope)
    far_kv = _send(kv, x_far)
    near_kv = [kv, _send(kv, y_up), _send(kv, y_down), _send(kv, y_far)]
    queries = _last_q(which, [_after(got, kv), *arrays[1:]], pieces, w_query, acc, q_bias, *rope)
    far_kv = _after(far_kv, queries)
    far_kv = [far_kv, _send(far_kv, y_up), _send(far_kv, y_down), _send(far_kv, y_far)]
    near_tiles = _stack_tiles(near_kv)
    far_tiles = _stack_tiles(far_kv)
    other_kv = [_send(near_tiles, other_core), _send(far_tiles, other_core)]

    states = _attend(_after(meta, far_tiles), near_tiles, far_tiles, queries)
    early_low, late_low = _attend(other_meta, *other_kv, queries, states, groups=1, spare=16)
    back_low = _send(late_low, mirror)
    early_high, late_high = _attend(
        _after(other_meta, late_low), *other_kv, queries, states, groups=1, part=1
    )
    back_high = _send(late_high, mirror)
    return jnp.concatenate(
        [
            jnp.concatenate([early_low, early_high], axis=1),
            jnp.concatenate([back_low[:HALF], back_high], axis=1),
        ],
        axis=0,
    )


def solution(mesh):
    return jax.shard_map(
        local,
        mesh=mesh,
        in_specs=(
            P("seq", "tp"),
            P(None, "tp"),
            P(None, "tp"),
            P(None, "tp"),
            P("tp"),
            P("tp"),
            P("tp"),
        ),
        out_specs=P("seq", "tp"),
        check_vma=False,
    )
```

```python
import functools
import math

import jax
import jax.numpy as jnp
from jax import lax
from jax.experimental import pallas as pl
from jax.experimental.pallas import tpu as pltpu
from jax.sharding import PartitionSpec as P

HEAD = 128
GROUP = 8
HALF = 192
PART = HALF // 2
ROWS = 2 * HALF
DEPTH = 1024
QCOLS = GROUP * HEAD
ALLCOLS = QCOLS + 2 * HEAD
LANES = 4 * HALF
SPAN = 4 * HALF
BLOCKS = 5
WHOLE = 3
AXES = ("seq", "tp")
VMEM_LIMIT = 48 * 1024 * 1024
EXP2_SCALE = float(HEAD) ** (-0.5) * math.log2(math.e)
NT = (((1,), (1,)), ((), ()))
TN = (((0,), (0,)), ((), ()))
rope_base = 1000000.0


def _place(flat):
    seq, tp = divmod(flat, 8)
    x_lo, z = divmod(tp, 4)
    y, rest = divmod(seq, 4)
    x_hi, core = divmod(rest, 2)
    return x_hi * 2 + x_lo, y, z, core


def _index(x, y, z, core):
    x_hi, x_lo = divmod(x % 4, 2)
    return (((y % 4) * 2 + x_hi) * 2 + core) * 8 + x_lo * 4 + z % 4


def _send(value, move):
    pairs = [(i, _index(*move(*_place(i)))) for i in range(128)]
    return lax.ppermute(value, AXES, pairs)


def z_up(x, y, z, c):
    return x, y, z + 1, c


def z_down(x, y, z, c):
    return x, y, z - 1, c


def x_near(x, y, z, c):
    return x ^ 1, y, z, c


def x_far(x, y, z, c):
    return x ^ 2, y, z, c


def y_up(x, y, z, c):
    return x, y + 1, z, c


def y_down(x, y, z, c):
    return x, y - 1, z, c


def y_far(x, y, z, c):
    return x, y + 2, z, c


def other_core(x, y, z, c):
    return x, y, z, 1 - c


def mirror_cross(x, y, z, c):
    return 3 - x, 3 - y, z, 1 - c


def mirror(x, y, z, c):
    return x ^ 2, 3 - y, z, 1 - c


VMEM = pl.BlockSpec(memory_space=pltpu.VMEM)
HBM = pl.BlockSpec(memory_space=pl.ANY)
SMEM = pl.BlockSpec(memory_space=pltpu.SMEM)


def _in_hbm(value):
    return pltpu.with_memory_space_constraint(value, pltpu.HBM)


def _block(index):
    return pl.ds(pl.multiple_of(index * DEPTH, DEPTH), DEPTH)


def _piece_loads(parts, pieces, x, sem):
    loads = []
    for i, piece in enumerate(pieces):
        at = 0
        loads.append([])
        for k, (operand, start, size) in enumerate(piece):
            loads[-1].append(
                pltpu.make_async_copy(
                    parts[operand].at[pl.ds(start, size)],
                    x.at[i, pl.ds(at, size)],
                    sem.at[i, k],
                )
            )
            at += size
    return loads


def _weight_loads(slices, n, far, near, sem):
    return [
        [
            pltpu.make_async_copy(src.at[_block(slices[i]), :], dst.at[i], sem.at[i, j])
            for j, (src, dst) in enumerate(zip(far, near))
        ]
        for i in range(n)
    ]


def _side_by_side(slices, n, far, near, sem):
    loads = []
    for i in range(n):
        at, group = 0, []
        for j, src in enumerate(far):
            width = src.shape[1]
            dst = near.at[i, :, pl.ds(at, width)]
            group.append(pltpu.make_async_copy(src.at[_block(slices[i]), :], dst, sem.at[i, j]))
            at += width
        loads.append(group)
    return loads


def _start(group):
    for copy in group:
        copy.start()


def _wait(group):
    for copy in group:
        copy.wait()


def _proj_body(arrays, pieces, started, slices, *refs):
    n = len(pieces)
    parts, far = refs[:arrays], refs[arrays : arrays + 3]
    refs = refs[arrays + 3 :]
    acc_in, refs = (refs[0], refs[1:]) if started else (None, refs)
    acc, x, near, (x_sem, w_sem, acc_sem) = refs[0], refs[1], refs[2:5], refs[5:8]
    x_loads = _piece_loads(parts, pieces, x, x_sem)
    w_loads = _weight_loads(slices, n, far, near, w_sem)
    for group in [x_loads[0], w_loads[0], *x_loads[1:], w_loads[1]]:
        _start(group)
    if started:
        acc_load = pltpu.make_async_copy(acc_in, acc, acc_sem)
        acc_load.start()
    spans = (slice(0, QCOLS), slice(QCOLS, QCOLS + HEAD), slice(QCOLS + HEAD, ALLCOLS))
    for i in range(n):
        _wait(x_loads[i])
        _wait(w_loads[i])
        if i + 2 < n:
            _start(w_loads[i + 2])
        if started and i == 0:
            acc_load.wait()
        for w, cols in zip(near, spans):
            term = jnp.dot(x[i], w[i], preferred_element_type=jnp.float32)
            if i or started:
                acc[:, cols] += term
            else:
                acc[:, cols] = term


def _project(slices, arrays, pieces, weights, acc=None):
    n = len(pieces)
    started = [] if acc is None else [acc]
    return pl.pallas_call(
        functools.partial(_proj_body, len(arrays), pieces, acc is not None),
        out_shape=jax.ShapeDtypeStruct((ROWS, ALLCOLS), jnp.float32),
        in_specs=[SMEM] + [HBM] * (len(arrays) + 3 + len(started)),
        out_specs=VMEM,
        scratch_shapes=[
            pltpu.VMEM((n, ROWS, DEPTH), jnp.bfloat16),
            pltpu.VMEM((n, DEPTH, QCOLS), jnp.bfloat16),
            pltpu.VMEM((n, DEPTH, HEAD), jnp.bfloat16),
            pltpu.VMEM((n, DEPTH, HEAD), jnp.bfloat16),
            pltpu.SemaphoreType.DMA((n, 3)),
            pltpu.SemaphoreType.DMA((n, 3)),
            pltpu.SemaphoreType.DMA,
        ],
        compiler_params=pltpu.CompilerParams(vmem_limit_bytes=28 * 1024 * 1024),
        cost_estimate=pl.CostEstimate(
            flops=2 * n * ROWS * DEPTH * ALLCOLS,
            bytes_accessed=2 * n * DEPTH * ALLCOLS,
            transcendentals=0,
        ),
        name="project",
    )(slices, *map(_in_hbm, arrays), *weights, *started)


def _rotate(u, cosine, sine):
    return u * cosine[...] + pltpu.roll(u, HEAD // 2, 1) * sine[...]


def _last_kv_body(arrays, pieces, slices, *refs):
    n = len(pieces)
    parts, (w_k, w_v), refs = refs[:arrays], refs[arrays : arrays + 2], refs[arrays + 2 :]
    given, (k_bias, v_bias, cosine, sine, out), refs = refs[0], refs[1:6], refs[6:]
    x, near, acc, x_sem, w_sem, sem = refs
    x_loads = _piece_loads(parts, pieces, x, x_sem)
    w_loads = _side_by_side(slices, n, (w_k, w_v), near, w_sem)
    others = [pltpu.make_async_copy(given.at[:, pl.ds(QCOLS, 2 * HEAD)], acc, sem)]
    for group in x_loads + w_loads + [others]:
        _start(group)
    both = 0
    for i in range(n):
        _wait(x_loads[i])
        _wait(w_loads[i])
        both += jnp.dot(x[i], near[i], preferred_element_type=jnp.float32)
    _wait(others)
    both += acc[...]
    k, v = both[:, :HEAD], both[:, HEAD:]
    k = _rotate(k + k_bias[...], cosine, sine).astype(jnp.bfloat16)
    v = (v + v_bias[...]).astype(jnp.bfloat16)
    for half in range(2):
        rows = slice(half * HALF, (half + 1) * HALF)
        out[half, :, :HEAD] = k[rows]
        out[half, :, HEAD:] = v[rows]


def _last_kv(slices, arrays, pieces, w_k, w_v, acc, k_bias, v_bias, cosine, sine):
    n = len(pieces)
    return pl.pallas_call(
        functools.partial(_last_kv_body, len(arrays), pieces),
        out_shape=jax.ShapeDtypeStruct((2, HALF, 2 * HEAD), jnp.bfloat16),
        in_specs=[SMEM] + [HBM] * (len(arrays) + 3) + [VMEM] * 4,
        out_specs=VMEM,
        scratch_shapes=[
            pltpu.VMEM((n, ROWS, DEPTH), jnp.bfloat16),
            pltpu.VMEM((n, DEPTH, 2 * HEAD), jnp.bfloat16),
            pltpu.VMEM((ROWS, 2 * HEAD), jnp.float32),
            pltpu.SemaphoreType.DMA((n, 4)),
            pltpu.SemaphoreType.DMA((n, 2)),
            pltpu.SemaphoreType.DMA,
        ],
        compiler_params=pltpu.CompilerParams(vmem_limit_bytes=12 * 1024 * 1024),
        cost_estimate=pl.CostEstimate(
            flops=4 * n * ROWS * DEPTH * HEAD,
            bytes_accessed=4 * n * DEPTH * HEAD,
            transcendentals=0,
        ),
        name="last_kv",
    )(slices, *map(_in_hbm, arrays), w_k, w_v, acc, k_bias, v_bias, cosine, sine)


def _last_q_body(arrays, pieces, slices, *refs):
    n = len(pieces)
    parts, w_q, refs = refs[:arrays], refs[arrays], refs[arrays + 1 :]
    given, (q_bias, cosine, sine, out), refs = refs[0], refs[1:5], refs[5:]
    x, near, acc, x_sem, w_sem, sem = refs
    x_loads = _piece_loads(parts, pieces, x, x_sem)
    w_loads = _weight_loads(slices, n, (w_q,), (near,), w_sem)
    others = [pltpu.make_async_copy(given.at[:, pl.ds(0, QCOLS)], acc, sem)]
    _start(x_loads[0])
    _start(w_loads[0])
    _start(others)
    for i in range(1, n):
        _start(x_loads[i])
        _start(w_loads[i])
    for i in range(n):
        _wait(x_loads[i])
        _wait(w_loads[i])
        if i == 0:
            _wait(others)
        if i < n - 1:
            acc[...] += jnp.dot(x[i], near[i], preferred_element_type=jnp.float32)
    for i in range(0, GROUP, 2):
        both = slice(i * HEAD, (i + 2) * HEAD)
        q = acc[:, both] + jnp.dot(x[n - 1], near[n - 1, :, both], preferred_element_type=jnp.float32)
        q += q_bias[:, both]
        for j in range(2):
            cols = slice((i + j) * HEAD, (i + j + 1) * HEAD)
            u = q[:, j * HEAD : (j + 1) * HEAD]
            out[:, cols] = _rotate(u, cosine, sine).astype(jnp.bfloat16)


def _last_q(slices, arrays, pieces, w_q, acc, q_bias, cosine, sine):
    n = len(pieces)
    return pl.pallas_call(
        functools.partial(_last_q_body, len(arrays), pieces),
        out_shape=jax.ShapeDtypeStruct((ROWS, QCOLS), jnp.bfloat16),
        in_specs=[SMEM] + [HBM] * (len(arrays) + 2) + [VMEM] * 3,
        out_specs=VMEM,
        scratch_shapes=[
            pltpu.VMEM((n, ROWS, DEPTH), jnp.bfloat16),
            pltpu.VMEM((n, DEPTH, QCOLS), jnp.bfloat16),
            pltpu.VMEM((ROWS, QCOLS), jnp.float32),
            pltpu.SemaphoreType.DMA((n, 4)),
            pltpu.SemaphoreType.DMA((n, 1)),
            pltpu.SemaphoreType.DMA,
        ],
        compiler_params=pltpu.CompilerParams(vmem_limit_bytes=20 * 1024 * 1024),
        cost_estimate=pl.CostEstimate(
            flops=2 * n * ROWS * DEPTH * QCOLS,
            bytes_accessed=2 * n * DEPTH * QCOLS,
            transcendentals=0,
        ),
        name="last_q",
    )(slices, *map(_in_hbm, arrays), w_q, acc, q_bias, cosine, sine)


def _stitch(shapes, moves, *operands, pinned=True):
    def body(*refs):
        sem = refs[-1]
        copies = []
        for i, (operand, start, size, o, at) in enumerate(moves):
            src, out = refs[operand], refs[len(operands) + o]
            if len(src.shape) < len(out.shape):
                copies.append(pltpu.make_async_copy(src, out.at[at], sem.at[i]))
            else:
                copies.append(
                    pltpu.make_async_copy(
                        src.at[pl.ds(start, size)], out.at[pl.ds(at, size)], sem.at[i]
                    )
                )
        _start(copies)
        _wait(copies)

    return pl.pallas_call(
        body,
        out_shape=[jax.ShapeDtypeStruct(shape, jnp.bfloat16) for shape in shapes],
        in_specs=[HBM] * len(operands),
        out_specs=[VMEM] * len(shapes),
        scratch_shapes=[pltpu.SemaphoreType.DMA((len(moves),))],
        compiler_params=pltpu.CompilerParams(vmem_limit_bytes=4 * 1024 * 1024),
        name="stitch",
    )(*(map(_in_hbm, operands) if pinned else operands))


def _stack_tiles(arrays):
    moves = [(i, 0, 2, 0, 2 * i) for i in range(4)]
    return _stitch([(8, HALF, 2 * HEAD)], moves, *arrays, pinned=False)[0]


def _attend_body(first, final, part, meta, near, far, queries, *refs):
    states_in, refs = ((), refs) if first else (refs[:2], refs[2:])
    outs, refs = refs[:2], refs[2:]
    rows, even, odd, place = refs[:4]
    stat, acc = refs[-2:] if final else outs
    groups = acc.shape[0] // 2
    for group in range(groups):
        for job in range(2):
            for h in range(4):
                col = (part * 4 + group * 4 + h) * HEAD
                rows[2 * group + job, h * HALF : (h + 1) * HALF, :] = queries[
                    job * HALF : (job + 1) * HALF, col : col + HEAD
                ]
    for h in range(4):
        place[0:1, h * HALF : (h + 1) * HALF] = lax.broadcasted_iota(jnp.int32, (1, HALF), 1) + 1
    if first:
        stat[:, 0:1, :] = jnp.full((2 * groups, 1, LANES), -1e30, jnp.float32)
        stat[:, 1:8, :] = jnp.zeros((2 * groups, 7, LANES), jnp.float32)
        acc[...] = jnp.zeros_like(acc)
    else:
        stat[...] = states_in[0][2 * part : 2 * part + 2 * groups]
        acc[...] = states_in[1][2 * part : 2 * part + 2 * groups]
    def entry(block, i):
        return meta[22 + 2 * block[1] + i]

    def tiles(block, cols):
        j = jnp.minimum(entry(block, 1), 3)
        return jnp.concatenate(
            [array[meta[8 * i + 2 * j + t], :, cols] for i, array in enumerate((near, far)) for t in range(2)],
            axis=0,
        )

    def job_of(block):
        return entry(block, 0) + 2 * block[0]

    def score(block, out, mask):
        k = tiles(block, slice(0, HEAD))
        scores = lax.dot_general(k, rows[job_of(block)], NT, preferred_element_type=jnp.float32)
        if mask:
            mine = meta[20 + entry(block, 0)]
            key = lax.broadcasted_iota(jnp.int32, (HALF, LANES), 0)
            parts = []
            for t in range(4):
                tile = 8 * entry(block, 1) + meta[16 + t]
                seen = jnp.where(tile < mine, HALF, 0) + jnp.where(tile == mine, 1, 0) * place[0:1, :]
                parts.append(jnp.where(key < seen, scores[t * HALF : (t + 1) * HALF], -jnp.inf))
            scores = jnp.concatenate(parts, axis=0)
        out[0:SPAN, :] = scores
        out[SPAN : SPAN + 1, :] = jnp.max(scores, axis=0, keepdims=True)

    def finish(block, src):
        job = job_of(block)
        v = tiles(block, slice(HEAD, 2 * HEAD))
        old = stat[job, 0:1, :]
        new = jnp.maximum(old, src[SPAN : SPAN + 1, :])
        weights = jnp.exp2((src[0:SPAN, :] - new) * EXP2_SCALE)
        shrink = jnp.exp2((old - new) * EXP2_SCALE)
        stat[job, 0:1, :] = new
        stat[job, 1:2, :] = stat[job, 1:2, :] * shrink + jnp.sum(weights, axis=0, keepdims=True)
        acc[job] = acc[job] * shrink + lax.dot_general(
            v, weights.astype(jnp.bfloat16), TN, preferred_element_type=jnp.float32
        )

    def whole(b):
        return lax.div(b, WHOLE), lax.rem(b, WHOLE)

    last = [(g, p) for g in range(groups) for p in range(WHOLE, BLOCKS)]
    loops = (WHOLE * groups - 1) // 2
    score((0, 0), even, False)

    @pl.loop(0, loops)
    def _(i):
        score(whole(2 * i + 1), odd, False)
        finish(whole(2 * i), even)
        score(whole(2 * i + 2), even, False)
        finish(whole(2 * i + 1), odd)

    rest = [(b // WHOLE, b % WHOLE) for b in range(2 * loops, WHOLE * groups)]
    steps = [(block, False) for block in rest] + [(block, True) for block in last]
    buffers = (even, odd)
    for i, (block, _) in enumerate(steps):
        if i + 1 < len(steps):
            score(steps[i + 1][0], buffers[(i + 1) % 2], steps[i + 1][1])
        finish(block, buffers[i % 2])
    if final:
        for group in range(groups):
            for job in range(2):
                for h in range(0, 4, 2):
                    cols = slice(h * HALF, (h + 2) * HALF)
                    done = acc[2 * group + job, :, cols] / stat[2 * group + job, 1:2, cols]
                    pair = done.T.astype(jnp.bfloat16)
                    at = (group * 4 + h) * HEAD
                    outs[job][:HALF, at : at + HEAD] = pair[:HALF]
                    outs[job][:HALF, at + HEAD : at + 2 * HEAD] = pair[HALF:]
        if outs[1].shape[0] > HALF:
            spare = outs[1].shape[0] - HALF
            outs[1][HALF:, :] = jnp.zeros((spare, outs[1].shape[1]), jnp.bfloat16)


def _attend(meta, near, far, queries, states=(), groups=2, part=0, spare=0):
    final = bool(states)
    state_shape = [(2 * groups, 8, LANES), (2 * groups, HEAD, LANES)]
    if final:
        out_shape = [
            jax.ShapeDtypeStruct((HALF, groups * 4 * HEAD), jnp.bfloat16),
            jax.ShapeDtypeStruct((HALF + spare, groups * 4 * HEAD), jnp.bfloat16),
        ]
    else:
        out_shape = [jax.ShapeDtypeStruct(shape, jnp.float32) for shape in state_shape]
    operands = [near, far, queries, *states]
    return pl.pallas_call(
        functools.partial(_attend_body, not states, final, part),
        out_shape=out_shape,
        in_specs=[SMEM] + [VMEM] * len(operands),
        out_specs=[VMEM] * len(out_shape),
        scratch_shapes=[
            pltpu.VMEM((2 * groups, LANES, HEAD), jnp.bfloat16),
            pltpu.VMEM((SPAN + 8, LANES), jnp.float32),
            pltpu.VMEM((SPAN + 8, LANES), jnp.float32),
            pltpu.VMEM((8, LANES), jnp.int32),
        ]
        + ([pltpu.VMEM(shape, jnp.float32) for shape in state_shape] if final else []),
        compiler_params=pltpu.CompilerParams(vmem_limit_bytes=28 * 1024 * 1024),
        cost_estimate=pl.CostEstimate(
            flops=4 * groups * BLOCKS * SPAN * HEAD * LANES,
            bytes_accessed=4 * 1024 * 1024,
            transcendentals=groups * BLOCKS * SPAN * LANES,
        ),
        name="attend",
    )(meta, *operands)


def _meta(order, lowest, early_query, late_query, early_count, late_count):
    early_whole, late_whole = early_count // 4, late_count // 4
    four = early_whole + late_whole == 4
    blocks = []
    for b in range(WHOLE):
        late = (b >= early_whole).astype(jnp.int32)
        blocks.append((late, b - late * early_whole))
    blocks.append((four.astype(jnp.int32), jnp.where(four, late_whole - 1, early_whole)))
    blocks.append((1, late_whole))
    entries = [*lowest, early_query, late_query]
    for late, block in blocks:
        entries += [late, block]
    return jnp.concatenate([order, jnp.stack([jnp.asarray(e, jnp.int32) for e in entries])])


def _angles(positions):
    half = HEAD // 2
    freq = rope_base ** (-2.0 * jnp.arange(half, dtype=jnp.float32) / HEAD)
    phase = positions.astype(jnp.float32)[:, None] * freq[None, :]
    cosine, sine = jnp.cos(phase), jnp.sin(phase)
    return jnp.concatenate([cosine, cosine], axis=1), jnp.concatenate([-sine, sine], axis=1)


def _after(value, *earlier):
    return lax.optimization_barrier((value, *earlier))[0]


def local(hidden, w_query, w_key, w_value, q_bias, k_bias, v_bias):
    seq = lax.axis_index("seq")
    tp = lax.axis_index("tp")
    y, x_hi, core = seq // 4, seq // 2 % 2, seq % 2
    x_lo, z = tp // 4, tp % 4
    weights = [w_query, w_key, w_value]
    q_bias, k_bias, v_bias = q_bias[None], k_bias[None], v_bias[None]

    def feature(lo, dz):
        return lo * 4 + (z + dz) % 4

    def tile_seq(dy, dx, dc):
        return ((y + dy) % 4 * 2 + (x_hi ^ dx)) * 2 + (core ^ dc)

    def order(dc):
        where, lowest = [], []
        for dx in (0, 1):
            seqs = [tile_seq(dy, dx, dc) for dy in (0, -1, 1, 2)]
            ranks = jnp.stack([t // 4 for s in seqs for t in (2 * s, 31 - 2 * s)])
            at = jnp.arange(8, dtype=jnp.int32)
            where.append(jnp.sum(jnp.where(ranks[None, :] == at[:, None], at[None, :], 0), axis=1))
            a = 4 * (x_hi ^ dx) + 2 * (core ^ dc)
            lowest += [jnp.minimum(a, 7 - a), jnp.maximum(a, 7 - a)]
        return jnp.concatenate(where).astype(jnp.int32), lowest

    far_lo = 1 - x_lo

    def ints(*values):
        return jnp.stack(values).astype(jnp.int32)

    w_query, w_key, w_value = weights = [
        pltpu.with_memory_space_constraint(w, pltpu.HBM) for w in weights
    ]
    early, late = _stitch(
        [(HALF, DEPTH)] * 2, [(0, 0, HALF, 0, 0), (0, HALF, HALF, 1, 0)], hidden
    )
    side = _send(early, x_near)
    up, down = _send(early, z_up), _send(early, z_down)
    late = _send(late, mirror_cross)
    row = jnp.arange(HALF, dtype=jnp.int32)
    rope = _angles(jnp.concatenate([seq * ROWS + row, (31 - 2 * seq) * HALF + row]))
    mine = seq * 2, 31 - seq * 2
    meta = _meta(*order(0), *mine, seq, 15 - seq)
    other_meta = _meta(*order(1), *mine, seq, 16 - seq)
    up, meta, other_meta, *rope = lax.optimization_barrier((up, meta, other_meta, *rope))

    to_up, to_down = _stitch(
        [(HALF, DEPTH)] * 2,
        [
            (0, 0, PART, 0, 0),
            (2, 0, PART, 0, PART),
            (1, PART, PART, 1, 0),
            (2, 0, PART, 1, PART),
        ],
        up,
        down,
        side,
        pinned=False,
    )
    from_down, from_up = _send(to_up, z_up), _send(to_down, z_down)
    late_side = _send(late, x_near)

    across, both = _stitch(
        [(ROWS, DEPTH)] * 2,
        [
            (2, 0, PART, 0, 0),
            (3, 0, PART, 0, PART),
            (0, PART, PART, 0, HALF),
            (1, PART, PART, 0, HALF + PART),
            (4, 0, HALF, 1, 0),
            (5, 0, HALF, 1, HALF),
        ],
        up,
        down,
        from_down,
        from_up,
        late,
        late_side,
    )
    late_up, late_down = _send(both, z_up), _send(both, z_down)
    got = _send(across, x_near)
    acc = _project(
        ints(feature(x_lo, 0), feature(far_lo, 0)),
        [_after(early, across), late_side, side, late],
        ([(0, 0, HALF), (1, 0, HALF)], [(2, 0, HALF), (3, 0, HALF)]),
        weights,
    )

    to_up, to_down = _stitch(
        [(HALF, DEPTH)] * 2,
        [
            (0, 0, PART, 0, 0),
            (0, HALF, PART, 0, PART),
            (1, PART, PART, 1, 0),
            (1, HALF + PART, PART, 1, PART),
        ],
        _after(late_up, acc),
        late_down,
    )
    late_from_down, late_from_up = _send(to_up, z_up), _send(to_down, z_down)
    acc = _project(
        ints(feature(x_lo, -1), feature(x_lo, 1), feature(far_lo, -1), feature(far_lo, 1)),
        [_after(up, to_up), down, from_down, from_up, got, late_up, late_down],
        (
            [(0, 0, HALF), (5, HALF, HALF)],
            [(1, 0, HALF), (6, HALF, HALF)],
            [(2, PART, PART), (4, HALF, PART), (5, 0, HALF)],
            [(3, PART, PART), (4, HALF + PART, PART), (6, 0, HALF)],
        ),
        weights,
        acc,
    )
    which = ints(feature(far_lo, 2), feature(x_lo, 2))
    arrays = [got, from_down, from_up, late_from_down, late_from_up]
    pieces = (
        [(0, 0, HALF), (3, 0, PART), (4, 0, PART)],
        [(1, 0, PART), (2, 0, PART), (3, PART, PART), (4, PART, PART)],
    )
    kv = _last_kv(which, arrays, pieces, w_key, w_value, acc, k_bias, v_bias, *rope)
    far_kv = _send(kv, x_far)
    near_kv = [kv, _send(kv, y_up), _send(kv, y_down), _send(kv, y_far)]
    queries = _last_q(which, [_after(got, kv), *arrays[1:]], pieces, w_query, acc, q_bias, *rope)
    far_kv = _after(far_kv, queries)
    far_kv = [far_kv, _send(far_kv, y_up), _send(far_kv, y_down), _send(far_kv, y_far)]
    near_tiles = _stack_tiles(near_kv)
    far_tiles = _stack_tiles(far_kv)
    other_kv = [_send(near_tiles, other_core), _send(far_tiles, other_core)]

    states = _attend(_after(meta, far_tiles), near_tiles, far_tiles, queries)
    early_low, late_low = _attend(other_meta, *other_kv, queries, states, groups=1, spare=16)
    back_low = _send(late_low, mirror)
    early_high, late_high = _attend(
        _after(other_meta, late_low), *other_kv, queries, states, groups=1, part=1
    )
    back_high = _send(late_high, mirror)
    return jnp.concatenate(
        [
            jnp.concatenate([early_low, early_high], axis=1),
            jnp.concatenate([back_low[:HALF], back_high], axis=1),
        ],
        axis=0,
    )


def solution(mesh):
    return jax.shard_map(
        local,
        mesh=mesh,
        in_specs=(
            P("seq", "tp"),
            P(None, "tp"),
            P(None, "tp"),
            P(None, "tp"),
            P("tp"),
            P("tp"),
            P("tp"),
        ),
        out_specs=P("seq", "tp"),
        check_vma=False,
    )
```
